32 devices in a mesh: dp: 4 (over z), expert: 8 (over y, x, core).
Axes of the slice: x: 2, y: 2, z: 4, core: 2. Of those that a mesh axis runs over, the one named last changes fastest.
Arguments:
- tokens: bfloat16 [2, 8, 1024, 1536], P(None, 'expert', 'dp'), may hold values from -6 to 6
- cotangent: bfloat16 [2, 8, 1024, 1536], P(None, 'expert', 'dp'), may hold values from -6 to 6
- parents: int32 [2, 8, 8], P(None, 'expert'), may hold values from 0 to 6, as said below
- valid_mask: int32 [2, 8, 1024], P(None, 'expert'), may hold values 0 or 1
- routes: int32 [2, 8, 1024, 8], P(None, 'expert', 'dp'), may hold values from 0 to 15, all different within a row; in each aligned block of 256 rows (0 to 255, 256 to 511, ..., all dimensions but the last counted through in order) at most 192 rows name the same one
- route_gates: float32 [2, 8, 1024, 8], P(None, 'expert', 'dp'), may hold values from 0.06 to 0.19
- norm_gains: bfloat16 [2, 1536], P(None, ('dp', 'expert')), may hold values from 0.5 to 1.5
- w_qkv: bfloat16 [1536, 2560], P(('dp', 'expert')), may hold values from -0.15625 to 0.15625
- w_out: bfloat16 [1536, 1536], P(None, ('dp', 'expert')), may hold values from -1.25 to 1.25
- w_gate_up: bfloat16 [16, 1536, 1024], P('expert', 'dp'), may hold values from -0.15625 to 0.15625
- w_down: bfloat16 [16, 512, 1536], P('expert', 'dp'), may hold values from -1 to 1
Outputs:
- layer_out: bfloat16 [2, 8, 1024, 1536], P(None, 'expert', 'dp')
- grad_tokens: bfloat16 [2, 8, 1024, 1536], P(None, 'expert', 'dp')
- grad_norm_gains: float32 [2, 1536], P(None, ('dp', 'expert'))
- grad_w_qkv: float32 [1536, 2560], P(('dp', 'expert'))
- grad_w_out: float32 [1536, 1536], P(None, ('dp', 'expert'))
- grad_w_gate_up: float32 [16, 1536, 1024], P('expert', 'dp')
- grad_w_down: float32 [16, 512, 1536], P('expert', 'dp')
The draws below stay inside these ranges and needn't reach their ends.
Inputs may be any that keep to these rules, and one draw needn't show every extreme that they name: `parents`: segments 1 to 2 form a chain (each segment's parent is the one before it) and segment 0 is its own parent; every later segment b has a parent from 2 to b - 1, so every segment's path reaches segment 0. `routes`: in each aligned block of 256 rows (the tokens of one tree on one device in one micro-batch) no expert is named by more than 192 rows, a bound that some block reaches.
All inputs are finite; a program needn't handle non-finite values. No bound on the sum of `valid_mask` on one device may be relied on, other than what follows from the above.
Results may differ from the reference program's by a relative error of at most 0.015.
Values may be sent and summed in bfloat16 or wider, within the bound.
No kernel may reach another device: no remote copies, remote signals or barrier semaphores. Data moves between devices by JAX's collectives and lax.ppermute only.
A program may use at most 384 MiB of HBM per device.

```python
import math
import jax
import jax.numpy as jnp
import numpy as np
from jax import lax

D = 1536
H = 24
KV = 8
HD = 64
FFE = 512
TOP = 8
BLOCK = 128
MICRO = 2
TOK_MB = 256
TREE_BLOCKS = 8
TREE_TOK = 1024
TRUNK = 3
TREES = 8
EXPERTS = 16
CAPM = 192
HQ = 1536
QKV = 2560
N_DP = 4


def draw_parents(key, part):
    key = jax.random.fold_in(key, 11)
    labels = jnp.arange(TREE_BLOCKS, dtype=jnp.int32)
    lower = jnp.where(labels < TRUNK, jnp.maximum(labels - 1, 0), TRUNK - 1)
    upper = jnp.where(labels < TRUNK, lower + 1, labels)
    shape_all = (MICRO, TREES, TREE_BLOCKS)
    lower_all = jnp.broadcast_to(lower, shape_all)
    upper_all = jnp.broadcast_to(upper, shape_all)
    return jax.random.randint(key, shape_all, lower_all, upper_all, dtype=jnp.int32)


def with_ends(result, key, least, largest):
    spot = [jax.random.randint(jax.random.fold_in(key, axis), (), 0, length) for axis, length in enumerate(result.shape)]
    longest = result.shape.index(max(result.shape))
    neighbour = spot[:longest] + [(spot[longest] + 1) % result.shape[longest]] + spot[longest + 1:]
    return result.at[tuple(spot)].set(least).at[tuple(neighbour)].set(largest)


def shard_levels(own_key, extent, pieces, smallest, high):
    def one(dim, blocks):
        heights = jax.random.uniform(jax.random.fold_in(jax.random.fold_in(own_key, 6), dim), (blocks,), jnp.float32, smallest / len(pieces), high / len(pieces))
        return jnp.repeat(jnp.exp(heights), extent[dim] // blocks).reshape((-1,) + (1,) * (len(extent) - dim - 1))

    level = one(*pieces[0])
    for cut in pieces[1:]:
        level = level * one(*cut)
    return level


def routed_block(rng, own, number, rows, number_of, top, limit, slope):
    sequence = jax.random.permutation(rng, number_of)
    packed, ordinary = portions_of(number_of, rows * top, limit, slope, True), portions_of(number_of, rows * top, limit, slope, False)
    places = jnp.arange(number_of)

    def named(lengths, offset_by):
        used = int((lengths > 0).sum())
        fixed = max(1, used // 4)
        moved = fixed + (places - fixed + offset_by * (used - fixed)) % max(1, number_of - fixed)
        return jnp.zeros((number_of,), jnp.int32).at[sequence[jnp.where(places < fixed, places, moved)]].set(jnp.asarray(lengths, jnp.int32))

    lengths = jnp.where(number % 4 == 0, named(packed, number // 4), named(ordinary, number - number // 4 - 1))
    mixed = jax.random.permutation(jax.random.fold_in(own, 3), number_of)
    source_of, taker = mixed[0:number_of // 2 * 2:2], mixed[1:number_of // 2 * 2:2]
    margin = jnp.minimum(lengths[source_of] - 1, limit - lengths[taker]) // 2
    margin = jnp.where((source_of == sequence[0]) | (taker == sequence[0]) | (lengths[taker] == 0), 0, jnp.maximum(margin, 0))
    moved = jax.random.randint(jax.random.fold_in(own, 4), (number_of // 2,), 0, 1 << 20) % (margin + 1)
    lengths = lengths.at[source_of].add(-moved).at[taker].add(moved)
    items = jnp.searchsorted(jnp.cumsum(lengths), jnp.arange(rows * top), side="right").astype(jnp.int32)
    listing = items.reshape(top, rows).T
    listing = listing[jax.random.permutation(jax.random.fold_in(own, 1), rows)]
    offset_by = jax.random.randint(jax.random.fold_in(own, 2), (rows, 1), 0, top)
    return jnp.take_along_axis(listing, (jnp.arange(top)[None, :] + offset_by) % top, axis=1)


def portions_of(count, total, limit, lean, full):
    portions = [(1 << 20) // math.isqrt(grade ** lean) + 1 for grade in range(1, count + 1)]
    largest = limit if full else min(limit, max(-(-total // count), total * portions[0] // sum(portions)))
    least = 1 if total - largest >= count - 1 else 0
    given, rest = [largest] + [least] * (count - 1), total - largest - least * (count - 1)
    while rest > 0:
        free = [i for i in range(1, count) if given[i] < largest] or [i for i in range(1, count) if given[i] < limit]
        pool, remaining = sum([portions[i] for i in free]), rest
        for i in free:
            more = min(limit - given[i], max(1, remaining * portions[i] // pool), rest)
            given[i] = given[i] + more
            rest = rest - more
    return np.array(given)


def centred(rng, extent, width, most, shards=(), kind=jnp.bfloat16):
    loudness = shard_levels(rng, extent, shards, -0.22, 0.18) if shards else 1.0
    result = jax.random.normal(rng, extent, jnp.float32) * width * loudness
    return jnp.minimum(jnp.maximum(result, -most), most).astype(kind)


def setup_inputs(seed: int = 0) -> dict:
    seeds = jax.random.split(jax.random.key(seed), 12)
    tokens = centred(seeds[0], (MICRO, TREES, TREE_TOK, D), 1.0, 6.0, ((1, 8), (2, 4)))
    cotangent = centred(seeds[1], (MICRO, TREES, TREE_TOK, D), 1.0, 6.0, ((1, 8), (2, 4)))
    parents = draw_parents(jax.random.fold_in(seeds[11], 71), 0)
    valid_mask = with_ends((jax.random.randint(seeds[3], (MICRO, TREES, TREE_TOK), 0, 4) < 3).astype(jnp.int32), jax.random.fold_in(seeds[3], 1), 0, 1)
    routes_keys = jax.random.split(jax.random.fold_in(seeds[4], 1), MICRO * TREES * TREE_TOK // TOK_MB)
    routes_turns = jax.random.permutation(jax.random.fold_in(seeds[4], 3), MICRO * TREES * TREE_TOK // TOK_MB)
    routes = jax.vmap(lambda own, number: routed_block(jax.random.fold_in(seeds[4], 2), own, number, TOK_MB, EXPERTS, TOP, CAPM, 1))(routes_keys, routes_turns).reshape((MICRO, TREES, TREE_TOK, TOP))
    route_gates = jnp.clip(jnp.exp(math.log(0.19) - 1.15267952 * jax.random.uniform(seeds[5], (MICRO, TREES, TREE_TOK, TOP), jnp.float32) ** shard_levels(seeds[5], (MICRO, TREES, TREE_TOK, TOP), ((1, 8), (2, 4)), -0.2, 0.2)), 0.06, 0.19)
    norm_gains = jnp.clip(1.0 + 0.1 * jax.random.normal(seeds[6], (2, D), jnp.float32), 0.5, 1.5).astype(jnp.bfloat16)
    w_qkv = centred(seeds[7], (D, QKV), D ** -0.5, 0.15625, ((0, 32),))
    w_out = centred(seeds[8], (HQ, D), (HQ // 64) ** -0.5, 1.25, ((1, 32),))
    w_gate_up = centred(seeds[9], (EXPERTS, D, 2 * FFE), D ** -0.5, 0.15625, ((0, 8), (1, 4)))
    w_down = centred(seeds[10], (EXPERTS, FFE, D), (FFE // 16) ** -0.5, 1.0, ((0, 8), (1, 4)))
    return dict(tokens=tokens, cotangent=cotangent, parents=parents, valid_mask=valid_mask, routes=routes, route_gates=route_gates, norm_gains=norm_gains, w_qkv=w_qkv, w_out=w_out, w_gate_up=w_gate_up, w_down=w_down)


EPSILON = 1e-06
NEGATIVE = -1e+30
HIGHEST_PREC = lax.Precision.HIGHEST

@jax.custom_vjp
def low(v):
    return lax.optimization_barrier(v.astype(jnp.bfloat16)).astype(jnp.float32)

@jax.custom_vjp
def low_back(v):
    return v

def low_keep(v):
    return (low(v), None)

def low_pass(kept, grad):
    return (grad,)

def back_keep(v):
    return (v, None)

def back_low(kept, grad):
    return (low(grad),)
low.defvjp(low_keep, low_pass)
low_back.defvjp(back_keep, back_low)

def rms_norm(values_in, gain):
    return values_in * lax.rsqrt(lax.optimization_barrier(jnp.mean(values_in * values_in, axis=-1, keepdims=True)) + EPSILON) * gain

def ancestry(parents_in):
    count = parents_in.shape[-1]
    labels = jnp.arange(count, dtype=jnp.int32)
    start = jnp.broadcast_to(labels, parents_in.shape).astype(jnp.int32)
    reach_first = (start[..., :, None] == labels).astype(jnp.int32)

    def extend(step_num, carry):
        current, reach = carry
        current = jnp.take_along_axis(parents_in, current, axis=-1).astype(jnp.int32)
        reach = jnp.maximum(reach, (current[..., :, None] == labels).astype(jnp.int32))
        return (current, reach)
    return lax.fori_loop(0, count, extend, (start, reach_first))[1]

def allowed_pairs(block_rows, valid_in, first_row):
    token_table = jnp.repeat(jnp.repeat(block_rows, BLOCK, axis=1), BLOCK, axis=2)
    query_pos = first_row + jnp.arange(token_table.shape[1], dtype=jnp.int32)
    key_pos = jnp.arange(token_table.shape[2], dtype=jnp.int32)
    causal = key_pos[None, :] <= query_pos[:, None]
    itself = key_pos[None, :] == query_pos[:, None]
    return (token_table > 0) & causal[None] & ((valid_in[:, None, :] > 0) | itself[None])

def slot_positions(routes_flat, expert_count):
    labels = jnp.arange(expert_count, dtype=jnp.int32)
    hits = (routes_flat[..., None] == labels).astype(jnp.int32)
    before = jnp.cumsum(hits, axis=-2) - hits
    return lax.optimization_barrier(jnp.sum(before * hits, axis=-1))

def slot_targets(route_tree):
    micro_count = route_tree.shape[0]
    blocks = route_tree.reshape(micro_count, N_DP, -1)
    position = slot_positions(blocks, EXPERTS)
    offset = (jnp.arange(N_DP, dtype=jnp.int32)[None, :, None] * micro_count + jnp.arange(micro_count, dtype=jnp.int32)[:, None, None]) * CAPM
    return (blocks * (N_DP * micro_count * CAPM) + offset + position).reshape(-1)

def layer(x_float, gain_pair, qkv_weight, out_weight, gate_up_weight, down_weight, allowed, target, gate_tree):
    micro_count, length, model_width = x_float.shape
    group_size = H // KV
    query_width = H * HD
    kv_width = KV * HD
    h_in = low(rms_norm(x_float, gain_pair[0]))
    qkv = low_back(low(jnp.einsum('mtd,de->mte', h_in, qkv_weight, precision=HIGHEST_PREC)))
    queries = qkv[..., :query_width].reshape(micro_count, length, KV, group_size, HD)
    keys_tree = qkv[..., query_width:query_width + kv_width].reshape(micro_count, length, KV, HD)
    values_tree = qkv[..., query_width + kv_width:].reshape(micro_count, length, KV, HD)

    def attend(tree_items):
        query_part, key_part, value_part, keep_mask = tree_items
        scores = jnp.einsum('qkgd,tkd->kgqt', query_part, key_part, precision=HIGHEST_PREC) * HD ** (-0.5)
        scores = jnp.where(keep_mask[None, None], low_back(scores), NEGATIVE)
        attn_probs = low(jax.nn.softmax(scores, axis=-1))
        return jnp.einsum('kgqt,tkd->qkgd', attn_probs, value_part, precision=HIGHEST_PREC)
    attn_mixed = lax.map(jax.checkpoint(attend), (queries, keys_tree, values_tree, allowed))
    attn_mixed = low_back(low(attn_mixed.reshape(micro_count, length, query_width)))
    branch = low_back(jnp.einsum('mte,ed->mtd', attn_mixed, out_weight, precision=HIGHEST_PREC))
    x_mid = x_float + branch
    h_mid = low(rms_norm(x_mid, gain_pair[1]))
    top_count = gate_tree.shape[-1]
    spread = jnp.repeat(h_mid, top_count, axis=1).reshape(-1, model_width)
    expert_count = gate_up_weight.shape[0]
    slot_rows = jnp.zeros((expert_count * N_DP * micro_count * CAPM, model_width), jnp.float32).at[target].set(spread)
    slot_rows = low_back(slot_rows).reshape(expert_count, -1, model_width)
    gate_up = low_back(jnp.einsum('erd,edf->erf', slot_rows, gate_up_weight, precision=HIGHEST_PREC))
    activation = low(jax.nn.silu(gate_up[..., :FFE]) * gate_up[..., FFE:])
    expert_out = low_back(low(jnp.einsum('erf,efd->erd', activation, down_weight, precision=HIGHEST_PREC)))
    picked = expert_out.reshape(-1, model_width)[target].reshape(micro_count, length, top_count, model_width)
    return x_mid + lax.optimization_barrier(jnp.sum(gate_tree[..., None] * picked, axis=2))

def reference(tokens, cotangent, parents, valid_mask, routes, route_gates, norm_gains, w_qkv, w_out, w_gate_up, w_down):
    weights = tuple((w.astype(jnp.float32) for w in (norm_gains, w_qkv, w_out, w_gate_up, w_down)))

    def one_tree(totals, tree_items):
        x_tree, cot_tree, parent_tree, valid_tree, route_tree, gate_tree = tree_items
        allowed = allowed_pairs(ancestry(parent_tree), valid_tree, 0)
        target = slot_targets(route_tree)

        def forward(x_float, gain_pair, qkv_weight, out_weight, gate_up_weight, down_weight):
            return layer(x_float, gain_pair, qkv_weight, out_weight, gate_up_weight, down_weight, allowed, target, gate_tree)
        layer_out, pull_back = jax.vjp(forward, x_tree.astype(jnp.float32), *weights)
        tree_grads = pull_back(cot_tree.astype(jnp.float32))
        totals = tuple((t + g for t, g in zip(totals, tree_grads[1:])))
        return (totals, (layer_out.astype(jnp.bfloat16), tree_grads[0].astype(jnp.bfloat16)))
    zero_grads = tuple((jnp.zeros(w.shape, jnp.float32) for w in weights))
    tree_items = tuple((jnp.moveaxis(a, 1, 0) for a in (tokens, cotangent, parents, valid_mask, routes, route_gates)))
    totals, (outputs, grads_in) = lax.scan(one_tree, zero_grads, tree_items)
    return (jnp.moveaxis(outputs, 0, 1), jnp.moveaxis(grads_in, 0, 1), totals[0], totals[1], totals[2], totals[3], totals[4])
```

```python
import functools

import jax
import jax.numpy as jnp
from jax import lax
from jax.experimental import pallas as pl
from jax.experimental.pallas import tpu as pltpu
from jax.sharding import PartitionSpec as P

H = 24
KV = 8
HD = 64
FFE = 512
BLOCK = 128
PAIRS = KV // 2
GROUP = H // KV
PAIR_Q = 2 * GROUP * HD
PAIR_K = 2 * HD

EPSILON = 1e-06
NEGATIVE = -1e30
F32 = jnp.float32
BF16 = jnp.bfloat16


def mm(a, b):
    return jnp.dot(a, b, preferred_element_type=F32)


def mm_nt(a, b):
    return lax.dot_general(a, b, (((1,), (1,)), ((), ())), preferred_element_type=F32)


def mm_tn(a, b):
    return lax.dot_general(a, b, (((0,), (0,)), ((), ())), preferred_element_type=F32)


def rms_norm(values_in, gain):
    return (
        values_in
        * lax.rsqrt(jnp.mean(values_in * values_in, axis=-1, keepdims=True) + EPSILON)
        * gain
    )


def rms_back(values, gain, grad):
    inv = lax.rsqrt(jnp.mean(values * values, axis=-1, keepdims=True) + EPSILON)
    unit = values * inv
    scaled = grad * gain
    grad_values = inv * (scaled - unit * jnp.mean(scaled * unit, axis=-1, keepdims=True))
    return grad_values, jnp.sum(grad * unit, axis=0)


def padded_rows(rows, half):
    blank = jnp.zeros_like(rows)
    return jnp.concatenate([rows, blank] if half == 0 else [blank, rows], axis=0)


def attend_kernel(chunks, q_ref, *refs):
    k_refs, v_refs = refs[:chunks], refs[chunks : 2 * chunks]
    bias_ref, o_ref, lse_ref, s_scr, p_scr = refs[2 * chunks :]
    rows = q_ref.shape[0]
    keys = k_refs[0].shape[0]
    q_t = q_ref[...].T * jnp.asarray(HD**-0.5, BF16)
    v_t = [v[...].T for v in v_refs]
    outs, totals = [], []
    for head in range(2 * GROUP):
        half = head // GROUP
        slot = head % 2
        q_pad = padded_rows(q_t[head * HD : (head + 1) * HD], half)
        peak = None
        for c in range(chunks):
            part = slice(c * keys, (c + 1) * keys)
            scores = mm(k_refs[c][...], q_pad) + bias_ref[part, :]
            s_scr[slot, part, :] = scores
            top = jnp.max(scores, axis=0, keepdims=True)
            peak = top if peak is None else jnp.maximum(peak, top)
        total = jnp.zeros((1, rows), F32)
        mixed = jnp.zeros((HD, rows), F32)
        for c in range(chunks):
            part = slice(c * keys, (c + 1) * keys)
            prob = jnp.exp(s_scr[slot, part, :] - peak)
            total = total + jnp.sum(prob, axis=0, keepdims=True)
            p_scr[slot, part, :] = prob.astype(BF16)
        for c in range(chunks):
            part = slice(c * keys, (c + 1) * keys)
            mixed = mixed + mm(v_t[c][half * HD : (half + 1) * HD], p_scr[slot, part, :])
        outs.append(mixed / total)
        totals.append(peak + jnp.log(total))
    o_ref[...] = jnp.concatenate(outs, axis=0).T.astype(BF16)
    blank = jnp.zeros((8 - 2 * GROUP, rows), F32)
    lse_ref[0] = jnp.concatenate(totals + [blank], axis=0)


def kv_specs(chunks, keys):
    k_spec = pl.BlockSpec((keys, PAIR_K), lambda j: (0, j))
    v_spec = pl.BlockSpec((keys, PAIR_K), lambda j: (0, PAIRS + j))
    return [k_spec] * chunks + [v_spec] * chunks


def attend(queries, kv_chunks, bias):
    rows, width = queries.shape
    chunks, keys = len(kv_chunks), kv_chunks[0].shape[0]
    work = 4 * H * rows * chunks * keys * HD
    q_spec = pl.BlockSpec((rows, PAIR_Q), lambda j: (0, j))
    return pl.pallas_call(
        functools.partial(attend_kernel, chunks),
        grid=(PAIRS,),
        in_specs=[q_spec]
        + kv_specs(chunks, keys)
        + [pl.BlockSpec((chunks * keys, rows), lambda j: (0, 0))],
        out_specs=[q_spec, pl.BlockSpec((1, 8, rows), lambda j: (j, 0, 0))],
        out_shape=[
            jax.ShapeDtypeStruct(queries.shape, BF16),
            jax.ShapeDtypeStruct((PAIRS, 8, rows), F32),
        ],
        scratch_shapes=[
            pltpu.VMEM((2, chunks * keys, rows), F32),
            pltpu.VMEM((2, chunks * keys, rows), BF16),
        ],
        compiler_params=pltpu.CompilerParams(vmem_limit_bytes=32 * 1024 * 1024),
        cost_estimate=pl.CostEstimate(
            flops=8 * work, bytes_accessed=4 * 1024 * 1024, transcendentals=work // (4 * HD)
        ),
        name="path_attention",
    )(queries, *kv_chunks, *kv_chunks, bias)


def attend_back_kernel(chunks, q_ref, g_ref, *refs):
    k_refs, v_refs = refs[:chunks], refs[chunks : 2 * chunks]
    bias_ref, lse_ref, dq_ref = refs[2 * chunks : 2 * chunks + 3]
    out_refs = refs[2 * chunks + 3 : 3 * chunks + 3]
    p_scr, gp_scr, ps_scr, ds_scr = refs[3 * chunks + 3 :]
    rows = q_ref.shape[0]
    keys = k_refs[0].shape[0]
    q_t = q_ref[...].T * jnp.asarray(HD**-0.5, BF16)
    g_t = g_ref[...].T
    k_t = [k[...].T for k in k_refs]
    dqs, q_pads, g_pads = [], [], []
    for head in range(2 * GROUP):
        half = head // GROUP
        slot = head % 2
        here = slice(head * rows, (head + 1) * rows)
        q_pad = padded_rows(q_t[head * HD : (head + 1) * HD], half)
        g_pad = padded_rows(g_t[head * HD : (head + 1) * HD], half)
        q_pads.append(q_pad)
        g_pads.append(g_pad)
        lse = lse_ref[0, head : head + 1, :]
        delta = jnp.zeros((1, rows), F32)
        for c in range(chunks):
            part = slice(c * keys, (c + 1) * keys)
            prob = jnp.exp(mm(k_refs[c][...], q_pad) + bias_ref[part, :] - lse)
            grad_prob = mm(v_refs[c][...], g_pad)
            delta = delta + jnp.sum(prob * grad_prob, axis=0, keepdims=True)
            p_scr[slot, part, :] = prob
            gp_scr[slot, part, :] = grad_prob
            ps_scr[part, here] = prob.astype(BF16)
        dq = jnp.zeros((HD, rows), F32)
        for c in range(chunks):
            part = slice(c * keys, (c + 1) * keys)
            ds = (p_scr[slot, part, :] * (gp_scr[slot, part, :] - delta)).astype(BF16)
            ds_scr[part, here] = ds
            dq = dq + mm(k_t[c][half * HD : (half + 1) * HD], ds)
        dqs.append(dq * HD**-0.5)
    dq_ref[...] = jnp.concatenate(dqs, axis=0).T.astype(BF16)
    q_all = jnp.concatenate(q_pads, axis=1)
    g_all = jnp.concatenate(g_pads, axis=1)
    for c in range(chunks):
        part = slice(c * keys, (c + 1) * keys)
        out_refs[c][0] = mm_nt(ds_scr[part, :], q_all).astype(BF16)
        out_refs[c][1] = mm_nt(ps_scr[part, :], g_all).astype(BF16)


def attend_back(queries, grad_mixed, kv_chunks, bias, lse):
    rows, width = queries.shape
    chunks, keys = len(kv_chunks), kv_chunks[0].shape[0]
    work = 10 * H * rows * chunks * keys * HD
    q_spec = pl.BlockSpec((rows, PAIR_Q), lambda j: (0, j))
    return pl.pallas_call(
        functools.partial(attend_back_kernel, chunks),
        grid=(PAIRS,),
        in_specs=[q_spec, q_spec]
        + kv_specs(chunks, keys)
        + [
            pl.BlockSpec((chunks * keys, rows), lambda j: (0, 0)),
            pl.BlockSpec((1, 8, rows), lambda j: (j, 0, 0)),
        ],
        out_specs=[q_spec] + [pl.BlockSpec((2, keys, PAIR_K), lambda j: (0, 0, j))] * chunks,
        out_shape=[jax.ShapeDtypeStruct(queries.shape, BF16)]
        + [jax.ShapeDtypeStruct((2, keys, KV * HD), BF16)] * chunks,
        scratch_shapes=[
            pltpu.VMEM((2, chunks * keys, rows), F32),
            pltpu.VMEM((2, chunks * keys, rows), F32),
            pltpu.VMEM((chunks * keys, 2 * GROUP * rows), BF16),
            pltpu.VMEM((chunks * keys, 2 * GROUP * rows), BF16),
        ],
        compiler_params=pltpu.CompilerParams(vmem_limit_bytes=40 * 1024 * 1024),
        cost_estimate=pl.CostEstimate(
            flops=6 * work, bytes_accessed=8 * 1024 * 1024, transcendentals=work // (10 * HD)
        ),
        name="path_attention_back",
    )(queries, grad_mixed, *kv_chunks, *kv_chunks, bias, lse)


def ancestry(parents_in):
    count = parents_in.shape[-1]
    labels = jnp.arange(count, dtype=jnp.int32)
    reach = (parents_in[..., :, None] == labels) | (labels[:, None] == labels)
    steps = 1
    while steps < count:
        reach = jnp.any(reach[..., :, :, None] & reach[..., None, :, :], axis=-2)
        steps *= 2
    return reach


def mask_bias(parents, valid, dp_index, n_dp, rows):
    micro = parents.shape[0]
    per = rows // BLOCK
    reach = lax.dynamic_slice_in_dim(ancestry(parents), dp_index * per, per, 1)
    early = (n_dp - 1) * per
    reach = jnp.pad(reach, ((0, 0), (0, 0), (early, 0)))
    reach = lax.dynamic_slice_in_dim(reach, dp_index * per, n_dp * per, 2)
    ok = jnp.pad(valid > 0, ((0, 0), (early * BLOCK, 0)))
    ok = lax.dynamic_slice_in_dim(ok, dp_index * rows, n_dp * rows, 1)
    by_key = jnp.repeat(jnp.swapaxes(reach, 1, 2), BLOCK, axis=1)
    shape = (micro, n_dp * rows, rows)
    key = lax.broadcasted_iota(jnp.int32, shape, 1) - (n_dp - 1) * rows
    query = lax.broadcasted_iota(jnp.int32, shape, 2)
    onpath = jnp.zeros(shape, bool)
    for i in range(per):
        onpath = onpath | ((query // BLOCK == i) & by_key[:, :, i : i + 1])
    allowed = onpath & (key <= query) & (ok[:, :, None] | (key == query))
    return jnp.where(allowed, 0.0, NEGATIVE).astype(F32)


def expert_kernel(block, has_prev, has_acc, last, *refs):
    refs = list(refs)

    def take(n):
        out = refs[:n]
        del refs[:n]
        return out

    h_refs, c_refs = take(4), take(4)
    gate_ref, wgu_ref, wd_ref = take(3)
    prev = take(4) if has_prev else None
    acc_in = take(2) if has_acc else None
    y_sib, y_own, gh_sib, gh_own, dwgu_ref, dwd_ref = take(6)
    hb, cb, yb, gb, acc_gu, acc_d, sem_in, sem_out, sem_acc = take(9)
    if has_prev:
        yp, gp, sem_prev = take(3)
    lead = h_refs[0].shape[0]
    half = (lead + h_refs[1].shape[0]) // block
    steps = 2 * half

    def fetch_tokens(refs, buffer, sem, at, slot):
        head, tail = refs

        @pl.when(at == 0)
        def _():
            rest = block - lead
            pltpu.make_async_copy(head, buffer.at[slot, pl.ds(0, lead)], sem).start()
            pltpu.make_async_copy(
                tail.at[pl.ds(0, rest)], buffer.at[slot, pl.ds(lead, rest)], sem
            ).start()

        @pl.when(at > 0)
        def _():
            rows = pl.ds(pl.multiple_of(at * block - lead, lead), block)
            pltpu.make_async_copy(tail.at[rows], buffer.at[slot], sem).start()

    def fetch_side(side, at, slot):
        fetch_tokens(h_refs[2 * side : 2 * side + 2], hb, sem_in.at[0, slot], at, slot)
        fetch_tokens(c_refs[2 * side : 2 * side + 2], cb, sem_in.at[1, slot], at, slot)
        if has_prev:
            rows = pl.ds(pl.multiple_of(at * block, block), block)
            for n, buffer in enumerate((yp, gp)):
                pltpu.make_async_copy(
                    prev[2 * n + side].at[rows], buffer.at[slot], sem_prev.at[n, slot]
                ).start()

    def fetch(i, slot):
        @pl.when(i < half)
        def _():
            fetch_side(0, i, slot)

        @pl.when(i >= half)
        def _():
            fetch_side(1, i - half, slot)

    def fetched(slot):
        for n, buffer in enumerate((hb, cb)):
            pltpu.make_async_copy(buffer.at[slot], buffer.at[slot], sem_in.at[n, slot]).wait()
        if has_prev:
            for n, buffer in enumerate((yp, gp)):
                pltpu.make_async_copy(
                    buffer.at[slot], buffer.at[slot], sem_prev.at[n, slot]
                ).wait()

    def copies_out(y_ref, g_ref, at, slot):
        rows = pl.ds(pl.multiple_of(at * block, block), block)
        return (
            pltpu.make_async_copy(yb.at[slot], y_ref.at[rows], sem_out.at[0, slot]),
            pltpu.make_async_copy(gb.at[slot], g_ref.at[rows], sem_out.at[1, slot]),
        )

    def stored(slot):
        for copy in copies_out(y_own, gh_own, 0, slot):
            copy.wait()

    fetch(0, 0)
    if has_acc:
        acc_copies = [
            pltpu.make_async_copy(acc_in[0], acc_gu, sem_acc.at[0]),
            pltpu.make_async_copy(acc_in[1], acc_d, sem_acc.at[1]),
        ]
        for copy in acc_copies:
            copy.start()
    else:
        acc_gu[...] = jnp.zeros_like(acc_gu)
        acc_d[...] = jnp.zeros_like(acc_d)

    def step(i, carry):
        slot = lax.rem(i, 2)

        @pl.when(i + 1 < steps)
        def _():
            fetch(i + 1, 1 - slot)

        fetched(slot)

        @pl.when(i >= 2)
        def _():
            stored(slot)

        tokens = hb[slot]
        grads = cb[slot]
        scale = gate_ref[pl.ds(pl.multiple_of(i * block, block), block), :]
        gate_up = mm(tokens, wgu_ref[...])
        grad_act = mm_nt(grads, wd_ref[...]) * scale
        gate, up = gate_up[:, :FFE], gate_up[:, FFE:]
        sig = jax.nn.sigmoid(gate)
        silu = gate * sig
        act = (silu * up * scale).astype(BF16)
        grad_gate = grad_act * up * (sig + silu * (1.0 - sig))
        grad_gu = jnp.concatenate([grad_gate, grad_act * silu], axis=1).astype(BF16)
        y = mm(act, wd_ref[...])
        gh = mm_nt(grad_gu, wgu_ref[...])
        if has_prev:
            y = y + yp[slot].astype(F32)
            gh = gh + gp[slot].astype(F32)
        yb[slot] = y.astype(BF16)
        gb[slot] = gh.astype(BF16)

        @pl.when(i < half)
        def _():
            for copy in copies_out(y_sib, gh_sib, i, slot):
                copy.start()

        @pl.when(i >= half)
        def _():
            for copy in copies_out(y_own, gh_own, i - half, slot):
                copy.start()

        if has_acc:

            @pl.when(i == 0)
            def _():
                for copy in acc_copies:
                    copy.wait()

        acc_d[...] += mm_tn(act, grads)
        acc_gu[...] += mm_tn(tokens, grad_gu)
        return carry

    lax.fori_loop(0, steps, step, 0)
    stored(steps % 2)
    stored((steps - 1) % 2)
    if last:
        dwgu_ref[...] = acc_gu[...].astype(BF16)
        dwd_ref[...] = acc_d[...].astype(BF16)
    else:
        out = [
            pltpu.make_async_copy(acc_gu, dwgu_ref, sem_acc.at[0]),
            pltpu.make_async_copy(acc_d, dwd_ref, sem_acc.at[1]),
        ]
        for copy in out:
            copy.start()
        for copy in out:
            copy.wait()


def expert_pass(h_all, c_all, gates, wgu, wd, previous, totals, last, block=512):
    rows = h_all[0].shape[0] + h_all[1].shape[0]
    width = h_all[0].shape[1]
    hidden = wd.shape[0]
    far = pl.BlockSpec(memory_space=pl.ANY)
    near = pl.BlockSpec(memory_space=pltpu.VMEM)
    token_out = jax.ShapeDtypeStruct((rows, width), BF16)
    token_buffer = pltpu.VMEM((2, block, width), BF16)
    grad_type = BF16 if last else F32
    scratch = [token_buffer] * 4 + [
        pltpu.VMEM((width, 2 * hidden), F32),
        pltpu.VMEM((hidden, width), F32),
        pltpu.SemaphoreType.DMA((2, 2)),
        pltpu.SemaphoreType.DMA((2, 2)),
        pltpu.SemaphoreType.DMA((2,)),
    ]
    extra, aliases = [], {}
    if previous is not None:
        scratch += [token_buffer] * 2 + [pltpu.SemaphoreType.DMA((2, 2))]
        aliases = {11 + n: n for n in range(4)}
        extra += list(previous)
    if totals is not None:
        extra += list(totals)
    return pl.pallas_call(
        functools.partial(
            expert_kernel, block, previous is not None, totals is not None, last
        ),
        in_specs=[far] * 8 + [near] * 3 + [far] * len(extra),
        out_specs=[far] * 4 + [near if last else far] * 2,
        out_shape=[token_out] * 4
        + [
            jax.ShapeDtypeStruct((width, 2 * hidden), grad_type),
            jax.ShapeDtypeStruct((hidden, width), grad_type),
        ],
        scratch_shapes=scratch,
        input_output_aliases=aliases,
        compiler_params=pltpu.CompilerParams(vmem_limit_bytes=60 * 1024 * 1024),
        cost_estimate=pl.CostEstimate(
            flops=18 * 2 * rows * width * hidden,
            bytes_accessed=2 * 12 * rows * width,
            transcendentals=2 * rows * hidden,
        ),
        name="expert_pass",
    )(*h_all, *c_all, gates, wgu, wd, *extra)


def join(*items):
    return lax.optimization_barrier(items)


class Plane:
    def __init__(self, count):
        self.count = count
        self.chips = count // 2

    def swap(self, x):
        return lax.ppermute(x, "expert", [(i, i ^ 1) for i in range(self.count)])

    def cross(self, x, k):
        return lax.ppermute(x, "expert", [(i, i ^ (2 * k)) for i in range(self.count)])

    def crosses(self, x, ks=None):
        return [self.cross(x, k) for k in (ks or range(1, self.chips))]

    def sums(self, own, arrived):
        rows = own.shape[0] // self.chips
        parts = []
        for k in range(self.chips):
            here = slice(k * rows, (k + 1) * rows)
            parts.append(own[here].astype(F32) + arrived[here].astype(F32))
        return [parts[0]] + [p.astype(BF16) for p in parts[1:]]

    def send(self, parts, ks=None):
        return [self.cross(parts[k], k) for k in (ks or range(1, self.chips))]


def added(first, others):
    for x in others:
        first = first + x.astype(F32)
    return first


def dp_cross(x, k, n_dp):
    return lax.ppermute(x, "dp", [(i, i ^ k) for i in range(n_dp)])


def dp_along(x, by, n_dp):
    pairs = [(i, i + by) for i in range(n_dp) if 0 <= i + by < n_dp]
    return lax.ppermute(x, "dp", pairs)


def over_dp(x, n_dp, dp_index):
    below, above = [x], [x]
    for _ in range(n_dp - 1):
        below.append(dp_along(below[-1], 1, n_dp))
        above.append(dp_along(above[-1], -1, n_dp))
    rows = x.shape[0]
    whole = jnp.zeros((n_dp * rows,) + x.shape[1:], x.dtype)
    for d in range(n_dp):
        piece = x if d == 0 else jnp.where(dp_index >= d, below[d], above[n_dp - d])
        at = lax.rem(dp_index - d + n_dp, n_dp) * rows
        whole = lax.dynamic_update_slice_in_dim(whole, piece, at, 0)
    return whole


def all_rows(plane, x, n_dp):
    me = lax.axis_index("expert")
    core, chip, dp_index = me % 2, me // 2, lax.axis_index("dp")
    line = jnp.zeros((n_dp,) + x.shape, x.dtype)
    for k in range(n_dp):
        piece = x if k == 0 else dp_cross(x, k, n_dp)
        line = lax.dynamic_update_index_in_dim(line, piece, dp_index ^ k, 0)
    blocks = [line] + plane.crosses(line)
    whole = jnp.zeros((n_dp, plane.chips, 2) + x.shape, x.dtype)
    for c, held in enumerate((blocks, plane.swap(jnp.stack(blocks)))):
        for k in range(plane.chips):
            at = (0, chip ^ k, core ^ c, 0, 0)
            whole = lax.dynamic_update_slice(whole, held[k][:, None, None], at)
    return whole.reshape((-1,) + x.shape[1:])


def sum_of_all(plane, grads, n_dp):
    rows, width = grads.shape
    chunk = rows // (n_dp * plane.count)
    split = grads.reshape(n_dp, plane.chips, 2, chunk, width)
    me = lax.axis_index("expert")
    core, chip, dp_index = me % 2, me // 2, lax.axis_index("dp")
    own = lax.dynamic_index_in_dim(split, core, 2, keepdims=False)
    other = lax.dynamic_index_in_dim(split, 1 - core, 2, keepdims=False)
    both = (own.astype(F32) + plane.swap(other).astype(F32)).astype(BF16)

    def of_chip(k):
        return lax.dynamic_index_in_dim(both, chip ^ k, 1, keepdims=False)

    parts = [of_chip(k) for k in range(plane.chips)]
    total = added(parts[0].astype(F32), plane.send(parts))
    small = total.astype(BF16)
    out = lax.dynamic_index_in_dim(total, dp_index, 0, keepdims=False)
    for k in range(1, n_dp):
        piece = lax.dynamic_index_in_dim(small, dp_index ^ k, 0, keepdims=False)
        out = out + dp_cross(piece, k, n_dp).astype(F32)
    return out


def body(
    n_dp,
    n_expert,
    tokens,
    cotangent,
    parents,
    valid_mask,
    routes,
    route_gates,
    norm_gains,
    w_qkv,
    w_out,
    w_gate_up,
    w_down,
):
    both = ("dp", "expert")
    micro, _, rows, width = tokens.shape
    micros = range(micro)
    count = micro * rows
    top = routes.shape[-1]
    query_width = H * HD
    kv_width = KV * HD
    local_experts = w_gate_up.shape[0]
    experts = local_experts * n_expert
    plane = Plane(n_expert)
    dp_index = lax.axis_index("dp")

    gains_t = jnp.pad(norm_gains.T, ((0, 0), (0, 126)))
    first = lax.all_gather(
        jnp.concatenate([w_qkv, gains_t], axis=1), both, axis=0, tiled=True
    )
    gate_up_w = [over_dp(w_gate_up[0], n_dp, dp_index)]
    down_w = [over_dp(w_down[0], n_dp, dp_index)]
    for e in range(1, local_experts):
        gate_up_w.append(lax.all_gather(w_gate_up[e], "dp", axis=0, tiled=True))
        down_w.append(lax.all_gather(w_down[e], "dp", axis=0, tiled=True))
    w_out_t = all_rows(plane, w_out.T, n_dp)

    chosen = routes.reshape(count, top)[:, :, None] == jnp.arange(experts, dtype=jnp.int32)
    table = jnp.sum(jnp.where(chosen, route_gates.reshape(count, top)[:, :, None], 0.0), axis=1)
    table = table.T.reshape(n_expert, local_experts, micro, rows)
    table = lax.all_to_all(table, "expert", split_axis=0, concat_axis=0, tiled=True)
    order = [2 * k + 1 for k in range(plane.chips)] + [2 * k for k in range(plane.chips)]
    table = jnp.take(table, lax.axis_index("expert") ^ jnp.array(order, jnp.int32), axis=0)
    gates = [[table[:, e, m].reshape(-1, 1) for m in micros] for e in range(local_experts)]
    bias = mask_bias(
        parents.reshape(micro, -1), valid_mask.reshape(micro, -1), dp_index, n_dp, rows
    )
    x_in = [tokens[m, 0].astype(F32) for m in micros]
    grad_out = [cotangent[m, 0] for m in micros]
    first, gate_up_w[0], down_w[0], w_out_t, gates, bias = join(
        first, gate_up_w[0], down_w[0], w_out_t, gates, bias
    )

    qkv_width = w_qkv.shape[1]
    w_q, w_kv = first[:, :query_width], first[:, query_width:qkv_width]
    gain_in = first[:, qkv_width].astype(F32)
    gain_mid = first[:, qkv_width + 1].astype(F32)
    h_in = [rms_norm(x, gain_in).astype(BF16) for x in x_in]
    kv = [mm(h, w_kv).astype(BF16) for h in h_in]
    queries = [mm(h, w_q).astype(BF16) for h in h_in]
    lags = range(1, n_dp)
    middle = n_dp // 2

    def lagged(x, ds):
        return {d: dp_along(x, d, n_dp) for d in ds}

    def in_order(x, held):
        return [held[d] for d in reversed(lags)] + [x]

    def attention(m):
        mixed, total = attend(queries[m], kv_chunks[m], bias[m])
        middle_x = x_in[m] + mm_nt(mixed, w_out_t)
        return mixed, total, middle_x, rms_norm(middle_x, gain_mid).astype(BF16)

    near, far = list(range(1, plane.chips - 1)), [plane.chips - 1]
    held_0, kv[1], queries, c_cross_0 = join(
        lagged(kv[0], lags), kv[1], queries, plane.crosses(grad_out[0])
    )
    kv_chunks = [in_order(kv[0], held_0)]
    held_1 = lagged(kv[1], [middle])
    c_others = [jnp.concatenate(c_cross_0, axis=0)]
    c_swapped = [[plane.swap(grad_out[0]), plane.swap(c_others[0])]]
    state_0, held_1, c_swapped = join(attention(0), held_1, c_swapped)
    h_mid = [state_0[3]]
    held_1.update(lagged(kv[1], [d for d in lags if d != middle]))
    held_1, h_far, h_swap = join(
        held_1, plane.crosses(h_mid[0], far), plane.swap(h_mid[0])
    )
    kv_chunks.append(in_order(kv[1], held_1))
    state_1, h_near = join(attention(1), plane.crosses(h_mid[0], near))
    h_mid.append(state_1[3])
    attn, lse, x_mid, _ = zip(state_0, state_1)

    def run(e, m, gate):
        *out, d_gu, d_d = expert_pass(
            h_all[m],
            c_all[m],
            gate,
            gate_up_w[e],
            down_w[e],
            carried[m],
            totals[e],
            m + 1 == micro,
        )
        return out, (d_gu, d_d)

    totals, carried = [None] * local_experts, [None] * micro
    h_others = jnp.concatenate(h_near + h_far, axis=0)
    h_all = [[h_swap, plane.swap(h_others), h_mid[0], h_others], None]
    c_all = [c_swapped[0] + [grad_out[0], c_others[0]], None]
    (carried[0], totals[0]), h_cross, h_swap, c_swap = join(
        run(0, 0, gates[0][0]),
        plane.crosses(h_mid[1]),
        plane.swap(h_mid[1]),
        plane.swap(grad_out[1]),
    )
    h_others = jnp.concatenate(h_cross, axis=0)
    gate, h_others, c_sent = join(gates[1][0], h_others, grad_out[1])
    (carried[0], totals[1]), h_others_swap, c_cross = join(
        run(1, 0, gate), plane.swap(h_others), plane.crosses(c_sent)
    )
    h_all[1] = [h_swap, h_others_swap, h_mid[1], h_others]
    c_others = jnp.concatenate(c_cross, axis=0)
    y_sib_0, y_own_0, gh_sib_0, gh_own_0 = carried[0]
    arrived, c_others_swap, c_others = join(plane.swap(gh_sib_0), plane.swap(c_others), c_others)
    c_all[1] = [c_swap, c_others_swap, grad_out[1], c_others]
    gh_parts_0 = plane.sums(gh_own_0, arrived)
    gate, gh_parts_0 = join(gates[0][1], gh_parts_0)
    (carried[1], totals[0]), gh_sent_0, arrived = join(
        run(0, 1, gate), plane.send(gh_parts_0), plane.swap(y_sib_0)
    )
    y_parts_0 = plane.sums(y_own_0, arrived)
    gate, y_parts_0 = join(gates[1][1], y_parts_0)
    (carried[1], totals[1]), y_sent_0 = join(run(1, 1, gate), plane.send(y_parts_0))
    y_sib_1, y_own_1, gh_sib_1, gh_own_1 = carried[1]

    def middle_back(m, grad_h_mid):
        part, gain_part = rms_back(x_mid[m], gain_mid, grad_h_mid)
        grad_x_mid = grad_out[m].astype(F32) + part
        branch = grad_x_mid.astype(BF16)
        return grad_x_mid, gain_part, branch, mm(branch, w_out_t).astype(BF16)

    def attention_back(m, grad_mixed):
        dq, *dkv = attend_back(queries[m], grad_mixed, kv_chunks[m], bias[m], lse[m])
        return dq, dkv

    def returned(dkv, ds):
        return {d: dp_along(dkv[n_dp - 1 - d], -d, n_dp) for d in ds}

    def kv_total(dkv, held):
        return added(dkv[-1].astype(F32), [held[d] for d in lags]).astype(BF16)

    back_0, arrived, y_sib_1 = join(
        middle_back(0, added(gh_parts_0[0], gh_sent_0)), plane.swap(gh_sib_1), y_sib_1
    )
    gh_parts_1 = plane.sums(gh_own_1, arrived)
    grad_mixed, gh_parts_1 = join(back_0[3], gh_parts_1)
    (grad_q_0, dkv_0), gh_far, arrived = join(
        attention_back(0, grad_mixed), plane.send(gh_parts_1, far), plane.swap(y_sib_1)
    )
    held_0 = returned(dkv_0, [middle])
    y_parts_1 = plane.sums(y_own_1, arrived)
    held_0, gh_near, y_parts_1 = join(held_0, plane.send(gh_parts_1, near), y_parts_1)
    held_0.update(returned(dkv_0, [d for d in lags if d != middle]))

    def last_back():
        back = middle_back(1, added(gh_parts_1[0], gh_near + gh_far))
        return back, attention_back(1, back[3])

    (back_1, (grad_q_1, dkv_1)), held_0, y_sent_1 = join(
        last_back(), held_0, plane.send(y_parts_1)
    )
    grad_kv = [kv_total(dkv_0, held_0)]
    x_out = [
        x_mid[0] + added(y_parts_0[0], y_sent_0),
        x_mid[1] + added(y_parts_1[0], y_sent_1),
    ]
    grad_x_mid, grad_gain_mid, grad_branch, _ = zip(back_0, back_1)
    grad_q = [grad_q_0, grad_q_1]

    def weight_grad(left, right):
        total = sum(mm_tn(a, b) for a, b in zip(left, right))
        return total.astype(BF16)

    held_1, grad_wout_s, grad_wq_s = join(
        returned(dkv_1, lags),
        sum_of_all(plane, weight_grad(grad_branch, attn), n_dp),
        sum_of_all(plane, weight_grad(h_in, grad_q), n_dp),
    )
    grad_kv.append(kv_total(dkv_1, held_1))
    grad_wkv = jnp.concatenate(
        [weight_grad(h_in, [g[n] for g in grad_kv]) for n in range(2)], axis=1
    )
    grad_wkv_s = sum_of_all(plane, grad_wkv, n_dp)
    grad_x, grad_gain_in = [], 0.0
    for m in micros:
        grad_h_in = (
            mm_nt(grad_q[m], w_q)
            + mm_nt(grad_kv[m][0], w_kv[:, :kv_width])
            + mm_nt(grad_kv[m][1], w_kv[:, kv_width:])
        )
        part, gain_part = rms_back(x_in[m], gain_in, grad_h_in)
        grad_x.append((grad_x_mid[m] + part).astype(BF16))
        grad_gain_in = grad_gain_in + gain_part
    world = n_dp * n_expert
    gain_grads = jnp.stack([grad_gain_in, sum(grad_gain_mid)]).reshape(2, world, width // world)
    gain_grads = jnp.swapaxes(gain_grads, 0, 1)
    gain_grads = lax.all_to_all(gain_grads, both, split_axis=0, concat_axis=0, tiled=True)
    reduced = [
        [lax.psum_scatter(t, "dp", scatter_dimension=0, tiled=True) for t in pair]
        for pair in totals
    ]
    reduced, gain_grads = join(reduced, gain_grads)
    grad_gu_s, grad_down_s = (
        jnp.stack([pair[n].astype(F32) for pair in reduced]) for n in range(2)
    )
    return (
        jnp.stack([x.astype(BF16) for x in x_out])[:, None],
        jnp.stack(grad_x)[:, None],
        jnp.sum(gain_grads, axis=0),
        jnp.concatenate([grad_wq_s, grad_wkv_s], axis=1),
        grad_wout_s.T,
        grad_gu_s,
        grad_down_s,
    )


def solution(mesh):
    tokens_spec = P(None, "expert", "dp", None)
    experts_spec = P("expert", "dp", None)
    rows_spec = P(("dp", "expert"), None)
    columns_spec = P(None, ("dp", "expert"))
    return jax.shard_map(
        functools.partial(body, mesh.shape["dp"], mesh.shape["expert"]),
        mesh=mesh,
        in_specs=(
            tokens_spec,
            tokens_spec,
            P(None, "expert", None),
            P(None, "expert", None),
            tokens_spec,
            tokens_spec,
            columns_spec,
            rows_spec,
            columns_spec,
            experts_spec,
            experts_spec,
        ),
        out_specs=(
            tokens_spec,
            tokens_spec,
            columns_spec,
            rows_spec,
            columns_spec,
            experts_spec,
            experts_spec,
        ),
        check_vma=False,
    )
```

```python
import functools

import jax
import jax.numpy as jnp
from jax import lax
from jax.experimental import pallas as pl
from jax.experimental.pallas import tpu as pltpu
from jax.sharding import PartitionSpec as P

H = 24
KV = 8
HD = 64
FFE = 512
BLOCK = 128
PAIRS = KV // 2
GROUP = H // KV
PAIR_Q = 2 * GROUP * HD
PAIR_K = 2 * HD

EPSILON = 1e-06
NEGATIVE = -1e30
F32 = jnp.float32
BF16 = jnp.bfloat16


def mm(a, b):
    return jnp.dot(a, b, preferred_element_type=F32)


def mm_nt(a, b):
    return lax.dot_general(a, b, (((1,), (1,)), ((), ())), preferred_element_type=F32)


def mm_tn(a, b):
    return lax.dot_general(a, b, (((0,), (0,)), ((), ())), preferred_element_type=F32)


def rms_norm(values_in, gain):
    return (
        values_in
        * lax.rsqrt(jnp.mean(values_in * values_in, axis=-1, keepdims=True) + EPSILON)
        * gain
    )


def rms_back(values, gain, grad):
    inv = lax.rsqrt(jnp.mean(values * values, axis=-1, keepdims=True) + EPSILON)
    unit = values * inv
    scaled = grad * gain
    grad_values = inv * (scaled - unit * jnp.mean(scaled * unit, axis=-1, keepdims=True))
    return grad_values, jnp.sum(grad * unit, axis=0)


def padded_rows(rows, half):
    blank = jnp.zeros_like(rows)
    return jnp.concatenate([rows, blank] if half == 0 else [blank, rows], axis=0)


def attend_kernel(chunks, q_ref, *refs):
    k_refs, v_refs = refs[:chunks], refs[chunks : 2 * chunks]
    bias_ref, o_ref, lse_ref, s_scr, p_scr = refs[2 * chunks :]
    rows = q_ref.shape[0]
    keys = k_refs[0].shape[0]
    q_t = q_ref[...].T * jnp.asarray(HD**-0.5, BF16)
    v_t = [v[...].T for v in v_refs]
    outs, totals = [], []
    for head in range(2 * GROUP):
        half = head // GROUP
        slot = head % 2
        q_pad = padded_rows(q_t[head * HD : (head + 1) * HD], half)
        peak = None
        for c in range(chunks):
            part = slice(c * keys, (c + 1) * keys)
            scores = mm(k_refs[c][...], q_pad) + bias_ref[part, :]
            s_scr[slot, part, :] = scores
            top = jnp.max(scores, axis=0, keepdims=True)
            peak = top if peak is None else jnp.maximum(peak, top)
        total = jnp.zeros((1, rows), F32)
        mixed = jnp.zeros((HD, rows), F32)
        for c in range(chunks):
            part = slice(c * keys, (c + 1) * keys)
            prob = jnp.exp(s_scr[slot, part, :] - peak)
            total = total + jnp.sum(prob, axis=0, keepdims=True)
            p_scr[slot, part, :] = prob.astype(BF16)
        for c in range(chunks):
            part = slice(c * keys, (c + 1) * keys)
            mixed = mixed + mm(v_t[c][half * HD : (half + 1) * HD], p_scr[slot, part, :])
        outs.append(mixed / total)
        totals.append(peak + jnp.log(total))
    o_ref[...] = jnp.concatenate(outs, axis=0).T.astype(BF16)
    blank = jnp.zeros((8 - 2 * GROUP, rows), F32)
    lse_ref[0] = jnp.concatenate(totals + [blank], axis=0)


def kv_specs(chunks, keys):
    k_spec = pl.BlockSpec((keys, PAIR_K), lambda j: (0, j))
    v_spec = pl.BlockSpec((keys, PAIR_K), lambda j: (0, PAIRS + j))
    return [k_spec] * chunks + [v_spec] * chunks


def attend(queries, kv_chunks, bias):
    rows, width = queries.shape
    chunks, keys = len(kv_chunks), kv_chunks[0].shape[0]
    work = 4 * H * rows * chunks * keys * HD
    q_spec = pl.BlockSpec((rows, PAIR_Q), lambda j: (0, j))
    return pl.pallas_call(
        functools.partial(attend_kernel, chunks),
        grid=(PAIRS,),
        in_specs=[q_spec]
        + kv_specs(chunks, keys)
        + [pl.BlockSpec((chunks * keys, rows), lambda j: (0, 0))],
        out_specs=[q_spec, pl.BlockSpec((1, 8, rows), lambda j: (j, 0, 0))],
        out_shape=[
            jax.ShapeDtypeStruct(queries.shape, BF16),
            jax.ShapeDtypeStruct((PAIRS, 8, rows), F32),
        ],
        scratch_shapes=[
            pltpu.VMEM((2, chunks * keys, rows), F32),
            pltpu.VMEM((2, chunks * keys, rows), BF16),
        ],
        compiler_params=pltpu.CompilerParams(vmem_limit_bytes=60 * 1024 * 1024),
        cost_estimate=pl.CostEstimate(
            flops=work // 64, bytes_accessed=1024 * 1024, transcendentals=0
        ),
        name="path_attention",
    )(queries, *kv_chunks, *kv_chunks, bias)


def attend_back_kernel(chunks, q_ref, g_ref, *refs):
    k_refs, v_refs = refs[:chunks], refs[chunks : 2 * chunks]
    bias_ref, lse_ref, dq_ref = refs[2 * chunks : 2 * chunks + 3]
    out_refs = refs[2 * chunks + 3 : 3 * chunks + 3]
    p_scr, gp_scr, ps_scr, ds_scr = refs[3 * chunks + 3 :]
    rows = q_ref.shape[0]
    keys = k_refs[0].shape[0]
    q_t = q_ref[...].T * jnp.asarray(HD**-0.5, BF16)
    g_t = g_ref[...].T
    k_t = [k[...].T for k in k_refs]
    dqs, q_pads, g_pads = [], [], []
    for head in range(2 * GROUP):
        half = head // GROUP
        slot = head % 2
        here = slice(head * rows, (head + 1) * rows)
        q_pad = padded_rows(q_t[head * HD : (head + 1) * HD], half)
        g_pad = padded_rows(g_t[head * HD : (head + 1) * HD], half)
        q_pads.append(q_pad)
        g_pads.append(g_pad)
        lse = lse_ref[0, head : head + 1, :]
        delta = jnp.zeros((1, rows), F32)
        for c in range(chunks):
            part = slice(c * keys, (c + 1) * keys)
            prob = jnp.exp(mm(k_refs[c][...], q_pad) + bias_ref[part, :] - lse)
            grad_prob = mm(v_refs[c][...], g_pad)
            delta = delta + jnp.sum(prob * grad_prob, axis=0, keepdims=True)
            p_scr[slot, part, :] = prob
            gp_scr[slot, part, :] = grad_prob
            ps_scr[part, here] = prob.astype(BF16)
        dq = jnp.zeros((HD, rows), F32)
        for c in range(chunks):
            part = slice(c * keys, (c + 1) * keys)
            ds = (p_scr[slot, part, :] * (gp_scr[slot, part, :] - delta)).astype(BF16)
            ds_scr[part, here] = ds
            dq = dq + mm(k_t[c][half * HD : (half + 1) * HD], ds)
        dqs.append(dq * HD**-0.5)
    dq_ref[...] = jnp.concatenate(dqs, axis=0).T.astype(BF16)
    q_all = jnp.concatenate(q_pads, axis=1)
    g_all = jnp.concatenate(g_pads, axis=1)
    for c in range(chunks):
        part = slice(c * keys, (c + 1) * keys)
        out_refs[c][0] = mm_nt(ds_scr[part, :], q_all).astype(BF16)
        out_refs[c][1] = mm_nt(ps_scr[part, :], g_all).astype(BF16)


def attend_back(queries, grad_mixed, kv_chunks, bias, lse):
    rows, width = queries.shape
    chunks, keys = len(kv_chunks), kv_chunks[0].shape[0]
    work = 10 * H * rows * chunks * keys * HD
    q_spec = pl.BlockSpec((rows, PAIR_Q), lambda j: (0, j))
    return pl.pallas_call(
        functools.partial(attend_back_kernel, chunks),
        grid=(PAIRS,),
        in_specs=[q_spec, q_spec]
        + kv_specs(chunks, keys)
        + [
            pl.BlockSpec((chunks * keys, rows), lambda j: (0, 0)),
            pl.BlockSpec((1, 8, rows), lambda j: (j, 0, 0)),
        ],
        out_specs=[q_spec] + [pl.BlockSpec((2, keys, PAIR_K), lambda j: (0, 0, j))] * chunks,
        out_shape=[jax.ShapeDtypeStruct(queries.shape, BF16)]
        + [jax.ShapeDtypeStruct((2, keys, KV * HD), BF16)] * chunks,
        scratch_shapes=[
            pltpu.VMEM((2, chunks * keys, rows), F32),
            pltpu.VMEM((2, chunks * keys, rows), F32),
            pltpu.VMEM((chunks * keys, 2 * GROUP * rows), BF16),
            pltpu.VMEM((chunks * keys, 2 * GROUP * rows), BF16),
        ],
        compiler_params=pltpu.CompilerParams(vmem_limit_bytes=60 * 1024 * 1024),
        cost_estimate=pl.CostEstimate(
            flops=work // 64, bytes_accessed=1024 * 1024, transcendentals=0
        ),
        name="path_attention_back",
    )(queries, grad_mixed, *kv_chunks, *kv_chunks, bias, lse)


def ancestry(parents_in):
    count = parents_in.shape[-1]
    labels = jnp.arange(count, dtype=jnp.int32)
    reach = (parents_in[..., :, None] == labels) | (labels[:, None] == labels)
    steps = 1
    while steps < count:
        reach = jnp.any(reach[..., :, :, None] & reach[..., None, :, :], axis=-2)
        steps *= 2
    return reach


def mask_bias(parents, valid, dp_index, n_dp, rows):
    micro = parents.shape[0]
    per = rows // BLOCK
    reach = lax.dynamic_slice_in_dim(ancestry(parents), dp_index * per, per, 1)
    early = (n_dp - 1) * per
    reach = jnp.pad(reach, ((0, 0), (0, 0), (early, 0)))
    reach = lax.dynamic_slice_in_dim(reach, dp_index * per, n_dp * per, 2)
    ok = jnp.pad(valid > 0, ((0, 0), (early * BLOCK, 0)))
    ok = lax.dynamic_slice_in_dim(ok, dp_index * rows, n_dp * rows, 1)
    by_key = jnp.repeat(jnp.swapaxes(reach, 1, 2), BLOCK, axis=1)
    shape = (micro, n_dp * rows, rows)
    key = lax.broadcasted_iota(jnp.int32, shape, 1) - (n_dp - 1) * rows
    query = lax.broadcasted_iota(jnp.int32, shape, 2)
    onpath = jnp.zeros(shape, bool)
    for i in range(per):
        onpath = onpath | ((query // BLOCK == i) & by_key[:, :, i : i + 1])
    allowed = onpath & (key <= query) & (ok[:, :, None] | (key == query))
    return jnp.where(allowed, 0.0, NEGATIVE).astype(F32)


def expert_kernel(block, chips, shards, has_prev, has_acc, last, *refs):
    refs = list(refs)

    def take(n):
        out = refs[:n]
        del refs[:n]
        return out

    h_refs, c_refs = take(2 * chips), take(2)
    order_ref, gate_ref, w_ref = take(3)
    prev = take(4) if has_prev else None
    acc_in = take(2) if has_acc else None
    y_sib, y_own, gh_sib, gh_own = take(4)
    grad_refs = take(2)
    hb, cb, yb, gb, acc_gu, acc_d, wg_ref, wu_ref, wd_ref, sem_in, sem_out, sem_acc, sem_w = take(13)
    if has_prev:
        yp, gp, sem_prev = take(3)
    lead = h_refs[0].shape[0]
    per = block // lead
    half = chips // per
    steps = 2 * half

    def fetch(i, slot):
        for j in range(steps):

            @pl.when(i == j)
            def _():
                for r in range(per):
                    at = j * per + r
                    rows = pl.ds(r * lead, lead)
                    pltpu.make_async_copy(
                        h_refs[at], hb.at[slot, rows], sem_in.at[0, slot]
                    ).start()
                    pltpu.make_async_copy(
                        c_refs[at // chips].at[order_ref[at % chips]],
                        cb.at[slot, rows],
                        sem_in.at[1, slot],
                    ).start()
                if has_prev:
                    rows = pl.ds((j % half) * block, block)
                    for n, buffer in enumerate((yp, gp)):
                        pltpu.make_async_copy(
                            prev[2 * n + j // half].at[rows], buffer.at[slot], sem_prev.at[n, slot]
                        ).start()

    def fetched(slot):
        for n, buffer in enumerate((hb, cb)):
            pltpu.make_async_copy(buffer.at[slot], buffer.at[slot], sem_in.at[n, slot]).wait()
        if has_prev:
            for n, buffer in enumerate((yp, gp)):
                pltpu.make_async_copy(
                    buffer.at[slot], buffer.at[slot], sem_prev.at[n, slot]
                ).wait()

    def copies_out(y_ref, g_ref, at, slot):
        rows = pl.ds(pl.multiple_of(at * block, block), block)
        return (
            pltpu.make_async_copy(yb.at[slot], y_ref.at[rows], sem_out.at[0, slot]),
            pltpu.make_async_copy(gb.at[slot], g_ref.at[rows], sem_out.at[1, slot]),
        )

    def stored(slot):
        for copy in copies_out(y_own, gh_own, 0, slot):
            copy.wait()

    hidden, width = acc_d.shape
    tiles = width // hidden
    band = hidden // shards
    weight_copies = [
        pltpu.make_async_copy(w_ref.at[:, pl.ds(0, hidden)], wg_ref, sem_w.at[0]),
        pltpu.make_async_copy(w_ref.at[:, pl.ds(hidden, hidden)], wu_ref, sem_w.at[1]),
    ]
    for z in range(shards):
        for j in range(tiles):
            copy = pltpu.make_async_copy(
                w_ref.at[pl.ds((z * tiles + j) * band, band), pl.ds(2 * hidden, hidden)],
                wd_ref.at[pl.ds(z * band, band), pl.ds(j * hidden, hidden)],
                sem_w.at[2 + z * tiles + j],
            )
            weight_copies.append(copy)
    for copy in weight_copies:
        copy.start()
    fetch(0, 0)
    if has_acc:
        acc_copies = [
            pltpu.make_async_copy(acc_in[0], acc_gu, sem_acc.at[0]),
            pltpu.make_async_copy(acc_in[1], acc_d, sem_acc.at[1]),
        ]
        for copy in acc_copies:
            copy.start()
    else:
        acc_gu[...] = jnp.zeros_like(acc_gu)
        acc_d[...] = jnp.zeros_like(acc_d)

    for copy in weight_copies:
        copy.wait()

    def step(i, carry):
        slot = lax.rem(i, 2)

        @pl.when(i + 1 < steps)
        def _():
            fetch(i + 1, 1 - slot)

        fetched(slot)

        @pl.when(i >= 2)
        def _():
            stored(slot)

        tokens = hb[slot]
        grads = cb[slot]
        scale = jnp.broadcast_to(gate_ref[i], (8, block)).T[:, :1]
        gate = mm(tokens, wg_ref[...])
        up = mm(tokens, wu_ref[...])
        grad_act = mm_nt(grads, wd_ref[...]) * scale
        sig = jax.nn.sigmoid(gate)
        silu = gate * sig
        act = (silu * up * scale).astype(BF16)
        grad_gate = (grad_act * up * (sig + silu * (1.0 - sig))).astype(BF16)
        grad_up = (grad_act * silu).astype(BF16)
        y = mm(act, wd_ref[...])
        gh = mm_nt(grad_gate, wg_ref[...]) + mm_nt(grad_up, wu_ref[...])
        if has_prev:
            y = y + yp[slot].astype(F32)
            gh = gh + gp[slot].astype(F32)
        yb[slot] = y.astype(BF16)
        gb[slot] = gh.astype(BF16)

        @pl.when(i < half)
        def _():
            for copy in copies_out(y_sib, gh_sib, i, slot):
                copy.start()

        @pl.when(i >= half)
        def _():
            for copy in copies_out(y_own, gh_own, i - half, slot):
                copy.start()

        if has_acc:

            @pl.when(i == 0)
            def _():
                for copy in acc_copies:
                    copy.wait()

        acc_d[...] += mm_tn(act, grads)
        acc_gu[:, :FFE] += mm_tn(tokens, grad_gate)
        acc_gu[:, FFE:] += mm_tn(tokens, grad_up)
        return carry

    lax.fori_loop(0, steps, step, 0)
    stored(steps % 2)
    stored((steps - 1) % 2)
    if last:
        cut = grad_refs[0].shape[1] - 2 * hidden
        grad_refs[0][:, : 2 * hidden] = acc_gu[...].astype(BF16)
        for z in range(shards):
            for j in range(tiles):
                rows = slice((z * tiles + j) * band, (z * tiles + j + 1) * band)
                piece = acc_d[z * band : (z + 1) * band, j * hidden : (j + 1) * hidden].astype(BF16)
                grad_refs[0][rows, 2 * hidden :] = piece[:, :cut]
                grad_refs[1][rows, :] = piece[:, cut:]
    else:
        out = [
            pltpu.make_async_copy(acc_gu, grad_refs[0], sem_acc.at[0]),
            pltpu.make_async_copy(acc_d, grad_refs[1], sem_acc.at[1]),
        ]
        for copy in out:
            copy.start()
        for copy in out:
            copy.wait()


def expert_pass(h_all, c_all, order, gates, weight, shards, previous, totals, last, block=512):
    chips = len(h_all) // 2
    lead, width = h_all[0].shape
    rows = chips * lead
    hidden = weight.shape[1] // 3
    far = pl.BlockSpec(memory_space=pl.ANY)
    near = pl.BlockSpec(memory_space=pltpu.VMEM)
    scalars = pl.BlockSpec(memory_space=pltpu.SMEM)
    token_out = jax.ShapeDtypeStruct((rows, width), BF16)
    token_buffer = pltpu.VMEM((2, block, width), BF16)
    if last:
        first = 2 * hidden + hidden // 4
        grads = [((width, first), BF16), ((width, 3 * hidden - first), BF16)]
    else:
        grads = [((width, 2 * hidden), F32), ((hidden, width), F32)]
    scratch = [token_buffer] * 4 + [
        pltpu.VMEM((width, 2 * hidden), F32),
        pltpu.VMEM((hidden, width), F32),
        pltpu.VMEM((width, hidden), BF16),
        pltpu.VMEM((width, hidden), BF16),
        pltpu.VMEM((hidden, width), BF16),
        pltpu.SemaphoreType.DMA((2, 2)),
        pltpu.SemaphoreType.DMA((2, 2)),
        pltpu.SemaphoreType.DMA((2,)),
        pltpu.SemaphoreType.DMA((2 + shards * (width // hidden),)),
    ]
    extra, aliases = [], {}
    if previous is not None:
        scratch += [token_buffer] * 2 + [pltpu.SemaphoreType.DMA((2, 2))]
        aliases = {2 * chips + 5 + n: n for n in range(4)}
        extra += list(previous)
    if totals is not None:
        extra += list(totals)
    return pl.pallas_call(
        functools.partial(
            expert_kernel, block, chips, shards, previous is not None, totals is not None, last
        ),
        in_specs=[far] * (2 * chips + 2) + [scalars, near, far] + [far] * len(extra),
        out_specs=[far] * 4 + [near if last else far] * len(grads),
        out_shape=[token_out] * 4 + [jax.ShapeDtypeStruct(*g) for g in grads],
        scratch_shapes=scratch,
        input_output_aliases=aliases,
        compiler_params=pltpu.CompilerParams(vmem_limit_bytes=60 * 1024 * 1024),
        cost_estimate=pl.CostEstimate(
            flops=rows * width, bytes_accessed=rows * width, transcendentals=0
        ),
        name="expert_pass",
    )(*h_all, *c_all, order, gates, weight, *extra)


SMALL = pl.CostEstimate(flops=1024, bytes_accessed=1024, transcendentals=0)
FAR = pl.BlockSpec(memory_space=pl.ANY)
NEAR = pl.BlockSpec(memory_space=pltpu.VMEM)
SCALARS = pl.BlockSpec(memory_space=pltpu.SMEM)


def small_call(kernel, name, inputs, outs, in_specs=None, scratch=()):
    return pl.pallas_call(
        kernel,
        in_specs=in_specs or [NEAR] * len(inputs),
        out_specs=[NEAR] * len(outs),
        out_shape=[jax.ShapeDtypeStruct(shape, dtype) for shape, dtype in outs],
        scratch_shapes=list(scratch),
        compiler_params=pltpu.CompilerParams(vmem_limit_bytes=48 * 1024 * 1024),
        cost_estimate=SMALL,
        name=name,
    )(*inputs)


def assemble_kernel(counts, chunk, place_ref, *refs):
    out_ref, sem = refs[len(counts) :]
    copies, n = [], 0
    for ref, count in zip(refs, counts):
        for at in range(count):
            rows = pl.ds(pl.multiple_of(place_ref[n] * chunk, chunk), chunk)
            copies.append(pltpu.make_async_copy(ref.at[at], out_ref.at[rows], sem))
            n += 1
    for copy in copies:
        copy.start()
    for copy in copies:
        copy.wait()


def assemble(blocks, places):
    chunk, width = blocks[0].shape[1:]
    counts = [x.shape[0] for x in blocks]
    rows = sum(counts) * chunk
    if chunk % 16:
        bands = jnp.concatenate(blocks, axis=0)
        whole = jnp.zeros_like(bands).at[places].set(bands)
        return whole.reshape(rows, width)
    return pl.pallas_call(
        functools.partial(assemble_kernel, counts, chunk),
        in_specs=[SCALARS] + [FAR] * len(blocks),
        out_specs=NEAR,
        out_shape=jax.ShapeDtypeStruct((rows, width), BF16),
        scratch_shapes=[pltpu.SemaphoreType.DMA],
        compiler_params=pltpu.CompilerParams(vmem_limit_bytes=32 * 1024 * 1024),
        cost_estimate=SMALL,
        name="assemble",
    )(places, *blocks)


def project_kernel(width, *refs):
    micro = (len(refs) - 2) // 3
    x_refs, w_ref = refs[:micro], refs[micro]
    h_refs, kv_refs, gains_ref = refs[micro + 1 : -1 - micro], refs[-1 - micro : -1], refs[-1]
    kv_from = w_ref.shape[1] - 128 - kv_refs[0].shape[1]
    gains = w_ref[:, -128:].astype(F32).T
    gains_ref[...] = gains[:8]
    for x_ref, h_ref, kv_ref in zip(x_refs, h_refs, kv_refs):
        h = rms_norm(x_ref[...].astype(F32), gains[:1]).astype(BF16)
        h_ref[...] = h
        kv_ref[...] = mm(h, w_ref[:, kv_from:-128]).astype(BF16)


def project(xs, weight, kv_width):
    rows, width = xs[0].shape
    outs = (
        [((rows, width), BF16)] * len(xs)
        + [((rows, kv_width), BF16)] * len(xs)
        + [((8, width), F32)]
    )
    got = small_call(functools.partial(project_kernel, width), "project", [*xs, weight], outs)
    return list(got[: len(xs)]), list(got[len(xs) : -1]), got[-1]


def middle_kernel(attn_ref, x_ref, gains_ref, w_ref, mid_ref, h_ref):
    mid = x_ref[...].astype(F32) + mm_nt(attn_ref[...], w_ref[...])
    mid_ref[...] = mid
    h_ref[...] = rms_norm(mid, gains_ref[1:2]).astype(BF16)


def middle(attn, x, gains, w_out_t):
    return small_call(
        middle_kernel,
        "middle",
        [attn, x, gains, w_out_t],
        [(x.shape, F32), (x.shape, BF16)],
    )


def middle_back_kernel(got_ref, mid_ref, c_ref, gains_ref, w_ref, gx_ref, branch_ref, gain_ref, mixed_ref):
    grad = got_ref[0].astype(F32)
    for k in range(1, got_ref.shape[0]):
        grad = grad + got_ref[k].astype(F32)
    part, gain_part = rms_back(mid_ref[...], gains_ref[1:2], grad)
    grad_x = c_ref[...].astype(F32) + part
    branch = grad_x.astype(BF16)
    gx_ref[...] = grad_x
    branch_ref[...] = branch
    gain_ref[...] = jnp.broadcast_to(gain_part[None], gain_ref.shape)
    mixed_ref[...] = mm(branch, w_ref[...]).astype(BF16)


def middle_back(got, mid, c, gains, w_out_t):
    return small_call(
        middle_back_kernel,
        "middle_back",
        [got, mid, c, gains, w_out_t],
        [(c.shape, F32), (c.shape, BF16), ((8, c.shape[1]), F32), (c.shape, BF16)],
    )


def input_back_kernel(q_ref, kv_ref, x_ref, mid_ref, gains_ref, w_ref, grad_ref):
    query_width = q_ref.shape[1]
    cut = query_width + kv_ref.shape[1]
    grad_h = mm_nt(q_ref[...], w_ref[:, :query_width])
    grad_h = grad_h + mm_nt(kv_ref[...], w_ref[:, query_width:cut])
    part, _ = rms_back(x_ref[...].astype(F32), gains_ref[:1], grad_h)
    grad_ref[...] = (mid_ref[...] + part).astype(BF16)


def input_back(grad_q, grad_kv, x, grad_x_mid, gains, weight):
    return small_call(
        input_back_kernel,
        "input_back",
        [grad_q, grad_kv, x, grad_x_mid, gains, weight],
        [(x.shape, BF16)],
    )[0]


def unpack_kernel(*refs):
    up_ref, down_ref = refs[-2:]
    for e in range(up_ref.shape[0]):
        first, second = refs[2 * e][...], refs[2 * e + 1][...]
        cut = up_ref.shape[2]
        up_ref[e] = first[:, :cut].astype(F32)
        pieces = jnp.concatenate([first[:, cut:], second], axis=1).astype(F32)
        rows, wide = down_ref.shape[1], pieces.shape[1]
        for j in range(down_ref.shape[2] // wide):
            down_ref[e, :, j * wide : (j + 1) * wide] = pieces[j * rows : (j + 1) * rows]


def unpack(totals, up_shape, down_shape):
    flat = [t for pair in totals for t in pair]
    return small_call(unpack_kernel, "unpack", flat, [(up_shape, F32), (down_shape, F32)])


def band_totals_kernel(counts, dp_ref, *refs):
    refs = list(refs)
    groups = []
    for count in counts:
        groups.append(refs[:count])
        del refs[:count]
    own_ref, piece_refs = refs[0], refs[1:]

    def total(ref):
        held = ref[0].astype(F32)
        for k in range(1, ref.shape[0]):
            held = held + ref[k].astype(F32)
        return held

    columns = []
    for group in groups:
        if len(group) == 1 and len(group[0].shape) == 4:
            columns.append(total(group[0]))
        else:
            columns.append(functools.reduce(jnp.add, [ref[...].astype(F32) for ref in group]))
    whole = jnp.concatenate(columns, axis=-1)
    dp_index = dp_ref[0]
    for z in range(whole.shape[0]):

        @pl.when(dp_index == z)
        def _():
            own_ref[...] = whole[z]

        for k, ref in enumerate(piece_refs):

            @pl.when((dp_index ^ (k + 1)) == z)
            def _():
                ref[...] = whole[z].astype(BF16)


def band_totals(groups, dp_index):
    n_dp, chunk = groups[0][0].shape[-3:-1]
    width = sum(group[0].shape[-1] for group in groups)
    inputs = [dp_index.reshape(1)] + [x for group in groups for x in group]
    own, *pieces = small_call(
        functools.partial(band_totals_kernel, [len(group) for group in groups]),
        "band_totals",
        inputs,
        [((chunk, width), F32)] + [((chunk, width), BF16)] * (n_dp - 1),
        in_specs=[SCALARS] + [NEAR] * (len(inputs) - 1),
    )
    return own, pieces


def sums_kernel(order_ref, own_ref, other_ref, out_ref):
    out_ref[...] = (own_ref[...].astype(F32) + other_ref[...].astype(F32)).astype(BF16)


def sums(own, other, order):
    blank = (0,) * (own.ndim - 1)
    block = (1,) + own.shape[1:]
    spec = pl.BlockSpec(block, lambda i, order: (i,) + blank)
    return pl.pallas_call(
        sums_kernel,
        grid_spec=pltpu.PrefetchScalarGridSpec(
            num_scalar_prefetch=1,
            grid=(own.shape[0],),
            in_specs=[spec, spec],
            out_specs=pl.BlockSpec(block, lambda i, order: (order[i],) + blank),
        ),
        out_shape=jax.ShapeDtypeStruct(own.shape, BF16),
        compiler_params=pltpu.CompilerParams(vmem_limit_bytes=32 * 1024 * 1024),
        cost_estimate=SMALL,
        name="sums",
    )(order, own, other)


def weight_grad_kernel(parts, chunk, n_dp, core_ref, *refs):
    left, right = refs[:parts], refs[parts : 2 * parts]
    own_ref, other_ref = refs[2 * parts :]
    total = mm_tn(left[0][...], right[0][...])
    for a, b in zip(left[1:], right[1:]):
        total = total + mm_tn(a[...], b[...])
    total = total.astype(BF16)
    chips = total.shape[0] // (2 * chunk * n_dp)
    pairs = total.reshape(n_dp, chips, 2, chunk, total.shape[1])
    first = core_ref[0] == 0
    for z in range(n_dp):
        for j in range(chips):
            own_ref[j, z] = jnp.where(first, pairs[z, j, 0], pairs[z, j, 1])
            other_ref[j, z] = jnp.where(first, pairs[z, j, 1], pairs[z, j, 0])


def weight_grad(left, right, n_dp, chips, core):
    width, columns = left[0].shape[1], right[0].shape[1]
    chunk = width // (2 * n_dp * chips)
    if chunk % 16:
        total = sum(mm_tn(a, b) for a, b in zip(left, right)).astype(BF16)
        pairs = total.reshape(n_dp, chips, 2, chunk, columns)
        return [
            jnp.swapaxes(lax.dynamic_index_in_dim(pairs, c, 2, keepdims=False), 0, 1)
            for c in (core, 1 - core)
        ]
    parts, tokens = len(left), left[0].shape[0]
    block = 512
    shape = (chips, n_dp, chunk)
    band = jax.ShapeDtypeStruct(shape + (columns,), BF16)
    band_spec = pl.BlockSpec(shape + (block,), lambda j: (0, 0, 0, j))
    return pl.pallas_call(
        functools.partial(weight_grad_kernel, parts, chunk, n_dp),
        grid=(columns // block,),
        in_specs=[SCALARS]
        + [pl.BlockSpec((tokens, width), lambda j: (0, 0))] * parts
        + [pl.BlockSpec((tokens, block), lambda j: (0, j))] * parts,
        out_specs=[band_spec, band_spec],
        out_shape=[band, band],
        compiler_params=pltpu.CompilerParams(vmem_limit_bytes=32 * 1024 * 1024),
        cost_estimate=SMALL,
        name="weight_grad",
    )(core.reshape(1).astype(jnp.int32), *left, *right)


def join(*items):
    return lax.optimization_barrier(items)


class Plane:
    def __init__(self, count):
        self.count = count
        self.chips = count // 2

    def swap(self, x):
        return lax.ppermute(x, "expert", [(i, i ^ 1) for i in range(self.count)])

    def cross(self, x, k):
        return lax.ppermute(x, "expert", [(i, i ^ (2 * k)) for i in range(self.count)])

    def exchange(self, x):
        groups = [[chip * 2 + c for chip in range(self.chips)] for c in range(2)]
        return lax.all_to_all(
            x, "expert", split_axis=0, concat_axis=0, axis_index_groups=groups, tiled=True
        )

    def spread(self, x):
        return self.exchange(jnp.broadcast_to(x[None], (self.chips,) + x.shape))

    def doubled(self, held, n):
        bits = [1 << i for i in range(self.chips.bit_length() - 1)]
        return [
            {**blocks, **{k ^ bit: self.cross(x, bit) for k, x in blocks.items()}}
            for blocks, bit in zip(held, (bits[n], bits[-1 - n]))
        ]

    def crosses(self, x, ks):
        return [self.cross(x, k) for k in ks]


def added(first, others):
    for x in others:
        first = first + x.astype(F32)
    return first


def dp_cross(x, k, n_dp):
    return lax.ppermute(x, "dp", [(i, i ^ k) for i in range(n_dp)])


def dp_along(x, by, n_dp):
    pairs = [(i, i + by) for i in range(n_dp) if 0 <= i + by < n_dp]
    return lax.ppermute(x, "dp", pairs)


def dp_others(x, n_dp):
    return [dp_cross(x, k, n_dp) for k in range(1, n_dp)]


def body(
    n_dp,
    n_expert,
    tokens,
    cotangent,
    parents,
    valid_mask,
    routes,
    route_gates,
    norm_gains,
    w_qkv,
    w_out,
    w_gate_up,
    w_down,
):
    both = ("dp", "expert")
    micro, _, rows, width = tokens.shape
    micros = range(micro)
    count = micro * rows
    top = routes.shape[-1]
    query_width = H * HD
    kv_width = KV * HD
    local_experts = w_gate_up.shape[0]
    experts = local_experts * n_expert
    plane = Plane(n_expert)
    dp_index = lax.axis_index("dp")

    x_in = [tokens[m, 0] for m in micros]
    grad_out = [cotangent[m, 0] for m in micros]
    expert_index = lax.axis_index("expert")
    core, chip = expert_index % 2, expert_index // 2
    every, lags = range(1, plane.chips), range(1, n_dp)
    near, far = every[:-1], every[-1:]

    def over_dp(x):
        return lax.all_gather(x, "dp", axis=0, tiled=True)

    chosen = routes.reshape(count, top)[:, :, None] == jnp.arange(experts, dtype=jnp.int32)
    table = jnp.sum(jnp.where(chosen, route_gates.reshape(count, top)[:, :, None], 0.0), axis=1)
    table = table.T.reshape(n_expert, local_experts, micro, rows)
    table = lax.all_to_all(table, "expert", split_axis=0, concat_axis=0, tiled=True)
    sides = [2 * k + 1 for k in range(plane.chips)] + [2 * k for k in range(plane.chips)]
    table = jnp.take(table, expert_index ^ jnp.array(sides, jnp.int32), axis=0)
    gates = [[table[:, e, m].reshape(-1, 1, 512) for m in micros] for e in range(local_experts)]
    bias = mask_bias(
        parents.reshape(micro, -1), valid_mask.reshape(micro, -1), dp_index, n_dp, rows
    )
    bias = [bias[m] for m in micros]
    same = jnp.arange(plane.chips, dtype=jnp.int32)
    order = chip ^ same

    half = n_dp // 2

    def bands(line, chip_at, core_at):
        return [((dp_index ^ z) * plane.chips + chip_at) * 2 + core_at for z in line]

    def wide(x):
        return jnp.broadcast_to(x[None], (plane.chips,) + x.shape)

    packed = [
        jnp.concatenate(
            [w_gate_up[e], w_down[e].reshape(-1, width // FFE, FFE).swapaxes(0, 1).reshape(-1, FFE)],
            axis=1,
        )
        for e in range(local_experts)
    ]
    gains_t = jnp.pad(norm_gains.T, ((0, 0), (0, 126)))
    own_rows = jnp.concatenate([w_qkv, gains_t], axis=1)
    qkv_line, out_rows, gates, bias, order, w_first = join(
        [own_rows] + dp_others(own_rows, n_dp),
        jnp.broadcast_to(w_out.T[None], (n_dp,) + w_out.shape[::-1]),
        gates,
        bias,
        order,
        packed[0],
    )
    expert_w = [over_dp(w_first)]
    line = jnp.stack(qkv_line)
    held = plane.doubled([{0: line[:half]}, {0: line[half:]}], 0)
    out_line = lax.all_to_all(out_rows, "dp", split_axis=0, concat_axis=0, tiled=True)
    held, line_swap = join(held, plane.swap(line))
    for n in range(1, plane.chips.bit_length() - 1):
        held = plane.doubled(held, n)
    held, out_line, c_wide, w_last = join(
        held, out_line, [wide(c) for c in grad_out], packed[1]
    )
    moved = [(h, k, held[h][k]) for k in every for h in range(2)]
    out_spread = plane.exchange(wide(out_line))
    swapped = list(join(*[plane.swap(x) for _, _, x in moved]))
    lines = [range(half), range(half, n_dp)]
    places = bands(range(n_dp), chip, core) + bands(range(n_dp), chip, 1 - core)
    for c in (core, 1 - core):
        for h, k, _ in moved:
            places += bands(lines[h], chip ^ k, c)
    weight = assemble(
        [line, line_swap] + [x for _, _, x in moved] + swapped, jnp.stack(places)
    )

    (h_in, kv, gains), out_spread = join(project(x_in, weight, 2 * kv_width), out_spread)
    w_q = weight[:, :query_width]
    queries = [mm(h, w_q).astype(BF16) for h in h_in]

    c_0 = plane.exchange(c_wide[0])
    out_swap = plane.swap(out_spread)
    places = []
    for c in (core, 1 - core):
        for j in range(plane.chips):
            places += [(z * plane.chips + j) * 2 + c for z in range(n_dp)]
    w_out_t = assemble(
        [x.reshape((-1,) + x.shape[2:]) for x in (out_spread, out_swap)], jnp.stack(places)
    )
    chunks_0, kv[1], queries, w_out_t, c_0, expert_w[0] = join(
        [dp_along(kv[0], d, n_dp) for d in reversed(lags)],
        kv[1],
        queries,
        w_out_t,
        c_0,
        expert_w[0],
    )
    kv_chunks = [list(chunks_0) + [kv[0]]]
    ends = [lags[0], lags[-1]]
    between = [d for d in lags if d not in ends]
    (mixed, total), held, c_swap = join(
        attend(queries[0], kv_chunks[0], bias[0]),
        [dp_along(kv[1], d, n_dp) for d in between],
        plane.swap(c_0),
    )
    held_1 = dict(zip(between, held))
    c_1 = plane.exchange(c_wide[1])
    c_all = [[c_swap, c_0]]
    attn, lse = [mixed], [total]
    x, h = middle(attn[0], x_in[0], gains, w_out_t)
    x_mid, h_mid = [x], [h]
    held, h_others, w_last, c_1 = join(
        [dp_along(kv[1], d, n_dp) for d in ends], plane.crosses(h, every), w_last, c_1
    )
    held_1.update(zip(ends, held))
    kv_chunks.append([held_1[d] for d in reversed(lags)] + [kv[1]])
    (mixed, total), h_swap = join(
        attend(queries[1], kv_chunks[1], bias[1]),
        [plane.swap(x) for x in [h] + list(h_others)],
    )
    attn.append(mixed)
    lse.append(total)
    h_all = [[*h_swap, h, *h_others], None]
    (x, h), c_swap = join(middle(attn[1], x_in[1], gains, w_out_t), plane.swap(c_1))
    c_all.append([c_swap, c_1])
    x_mid.append(x)
    h_mid.append(h)

    def run(e, m, gate):
        out = expert_pass(
            h_all[m],
            c_all[m],
            order,
            gate,
            expert_w[e],
            n_dp,
            carried[m],
            totals[e],
            m + 1 == micro,
        )
        return out[:4], out[4:]

    def split(x):
        return x.reshape((plane.chips, -1) + x.shape[1:])

    totals, carried = [None] * local_experts, [None] * micro
    (carried[0], totals[0]), h_cross, h_swap = join(
        run(0, 0, gates[0][0]), plane.crosses(h_mid[1], every), plane.swap(h_mid[1])
    )
    h_all[1] = [h_swap] + [plane.swap(x) for x in h_cross] + [h_mid[1]] + h_cross
    (carried[1], totals[0]), w_whole, gate = join(
        run(0, 1, gates[0][1]), over_dp(w_last), gates[1][0]
    )
    expert_w.append(w_whole)

    def summed(x):
        return lax.psum_scatter(x, "dp", scatter_dimension=0, tiled=True)

    totals_s = [[summed(t) for t in totals[0]]]
    carried[0], totals[1] = run(1, 0, gate)
    y_sib_0, y_own_0, gh_sib_0, gh_own_0 = carried[0]
    gh_chips = sums(split(gh_own_0), split(plane.swap(gh_sib_0)), order)
    gate, gh_chips, y_sib_0 = join(gates[1][1], gh_chips, y_sib_0)
    (carried[1], totals[1]), gh_got, y_swap_0, totals_s[0] = join(
        run(1, 1, gate), plane.exchange(gh_chips), plane.swap(y_sib_0), totals_s[0]
    )
    y_sib_1, y_own_1, gh_sib_1, gh_own_1 = carried[1]

    def back_of(m, got):
        return middle_back(got, x_mid[m], grad_out[m], gains, w_out_t)

    def attention_back(m, grad_mixed):
        dq, *dkv = attend_back(queries[m], grad_mixed, kv_chunks[m], bias[m], lse[m])
        return dq, dkv

    def returned(dkv, ds):
        return [dp_along(dkv[n_dp - 1 - d], -d, n_dp) for d in ds]

    def weights_of(left, right):
        return weight_grad(left, right, n_dp, plane.chips, core)

    back_0, gh_swap, y_sib_1 = join(back_of(0, gh_got), plane.swap(gh_sib_1), y_sib_1)
    gh_chips = sums(split(gh_own_1), split(gh_swap), order)
    grad_mixed, gh_chips, y_swap_0 = join(back_0[3], gh_chips, y_swap_0)
    gh_got = plane.exchange(gh_chips)
    totals_s.append([summed(totals[1][0])])
    grad_q_0, dkv_0 = attention_back(0, grad_mixed)
    y_swap_0, grad_q_0 = join(y_swap_0, grad_q_0)
    grad_q_0, dkv_0, gh_got, y_chips_0, y_swap_1 = join(
        grad_q_0,
        dkv_0,
        gh_got,
        sums(split(y_own_0), split(y_swap_0), order),
        plane.swap(y_sib_1),
    )
    back_1 = back_of(1, gh_got)
    grad_x_mid, grad_branch, gain_parts, _ = zip(back_0, back_1)
    gain_mid = sum(g[:1] for g in gain_parts)
    soon, late = [lags[0], *between], [lags[-1]]
    out_bands = weights_of(grad_branch, attn)
    (grad_q_1, dkv_1), held, totals_s[1][0], y_got_0, y_swap_1, gain_swap, out_swap = join(
        attention_back(1, back_1[3]),
        returned(dkv_0, soon),
        totals_s[1][0],
        plane.exchange(y_chips_0),
        y_swap_1,
        plane.swap(gain_mid),
        plane.swap(out_bands[1]),
    )
    gain_mid = gain_mid + gain_swap
    out_got = plane.exchange(sums(out_bands[0], out_swap, same))
    held_0 = dict(zip(soon, held))
    grad_q = [grad_q_0, grad_q_1]

    held, q_bands, last_half, y_chips_1, gain_near = join(
        returned(dkv_1, ends),
        weights_of(h_in, grad_q),
        totals[1][1],
        sums(split(y_own_1), split(y_swap_1), order),
        plane.crosses(gain_mid, near),
    )
    held_1 = dict(zip(ends, held))
    held, held_late, q_swap, gain_far = join(
        returned(dkv_1, between),
        returned(dkv_0, late),
        plane.swap(q_bands[1]),
        plane.crosses(gain_mid, far),
    )
    gain_mid = added(gain_mid, gain_near + gain_far)
    held_1.update(zip(between, held))
    held_0.update(zip(late, held_late))
    totals_s[1].append(summed(last_half))
    total_0 = added(dkv_0[-1].astype(F32), [held_0[d] for d in lags])
    total_1 = added(dkv_1[-1].astype(F32), [held_1[d] for d in lags])
    grad_kv = [jnp.concatenate([t[0], t[1]], axis=1).astype(BF16) for t in (total_0, total_1)]
    kv_bands = weights_of(h_in, grad_kv)
    gain_rows = lax.dynamic_index_in_dim(
        gain_mid.reshape(n_dp, n_expert, -1), expert_index, 1, keepdims=False
    )
    gain_rows = jnp.pad(gain_rows[:, :, None], ((0, 0), (0, 0), (0, 127)))
    kv_swap, q_chips, gain_rows, out_got = join(
        plane.swap(kv_bands[1]), sums(q_bands[0], q_swap, same), gain_rows, out_got
    )
    kv_chips = sums(kv_bands[0], kv_swap, order)
    kv_own, grad_kv, q_chips = join([kv_chips[k] for k in range(plane.chips)], grad_kv, q_chips)
    grad_x = [
        input_back(grad_q[m], grad_kv[m], x_in[m], grad_x_mid[m], gains, weight) for m in micros
    ]
    out_total, out_pieces = band_totals([[out_got]], dp_index)

    def over_dp_links(pieces):
        return [dp_cross(x, z, n_dp) for z, x in zip(lags, pieces)]

    kv_sent, q_got, grad_x, totals_s, y_chips_1, out_sent = join(
        [plane.cross(kv_own[k], k) for k in every],
        plane.exchange(q_chips),
        grad_x,
        totals_s,
        y_chips_1,
        over_dp_links(out_pieces),
    )
    y_got_1 = plane.exchange(y_chips_1)
    grad_gu_s, grad_down_s = unpack(totals_s, w_gate_up.shape, w_down.shape)
    total, pieces = band_totals([[q_got], [kv_own[0], *kv_sent], [gain_rows]], dp_index)
    sent, y_got_1, grad_gu_s, grad_down_s = join(
        over_dp_links(pieces), y_got_1, grad_gu_s, grad_down_s
    )
    out_total, total = added(out_total, out_sent), added(total, sent)

    qkv_width = w_qkv.shape[1]
    grad_wqkv = total[:, :qkv_width]
    gain_in = jnp.sum(w_qkv.astype(F32) * grad_wqkv, axis=1) / norm_gains[0].astype(F32)
    x_out = [
        x_mid[m] + jnp.sum(y.astype(F32), axis=0) for m, y in enumerate((y_got_0, y_got_1))
    ]
    return (
        jnp.stack([x.astype(BF16) for x in x_out])[:, None],
        jnp.stack(grad_x)[:, None],
        jnp.stack([gain_in, total[:, qkv_width]]),
        grad_wqkv,
        out_total.T,
        grad_gu_s,
        grad_down_s,
    )


def solution(mesh):
    tokens_spec = P(None, "expert", "dp", None)
    experts_spec = P("expert", "dp", None)
    rows_spec = P(("dp", "expert"), None)
    columns_spec = P(None, ("dp", "expert"))
    return jax.shard_map(
        functools.partial(body, mesh.shape["dp"], mesh.shape["expert"]),
        mesh=mesh,
        in_specs=(
            tokens_spec,
            tokens_spec,
            P(None, "expert", None),
            P(None, "expert", None),
            tokens_spec,
            tokens_spec,
            columns_spec,
            rows_spec,
            columns_spec,
            experts_spec,
            experts_spec,
        ),
        out_specs=(
            tokens_spec,
            tokens_spec,
            columns_spec,
            rows_spec,
            columns_spec,
            experts_spec,
            experts_spec,
        ),
        check_vma=False,
    )
```

```python
import functools

import jax
import jax.numpy as jnp
from jax import lax
from jax.experimental import pallas as pl
from jax.experimental.pallas import tpu as pltpu
from jax.sharding import PartitionSpec as P

H = 24
KV = 8
HD = 64
FFE = 512
BLOCK = 128
PAIRS = KV // 2
GROUP = H // KV
PAIR_Q = 2 * GROUP * HD
PAIR_K = 2 * HD

EPSILON = 1e-06
NEGATIVE = -1e30
F32 = jnp.float32
BF16 = jnp.bfloat16


def mm(a, b):
    return jnp.dot(a, b, preferred_element_type=F32)


def mm_nt(a, b):
    return lax.dot_general(a, b, (((1,), (1,)), ((), ())), preferred_element_type=F32)


def mm_tn(a, b):
    return lax.dot_general(a, b, (((0,), (0,)), ((), ())), preferred_element_type=F32)


def rms_norm(values_in, gain):
    return (
        values_in
        * lax.rsqrt(jnp.mean(values_in * values_in, axis=-1, keepdims=True) + EPSILON)
        * gain
    )


def rms_back(values, gain, grad):
    inv = lax.rsqrt(jnp.mean(values * values, axis=-1, keepdims=True) + EPSILON)
    unit = values * inv
    scaled = grad * gain
    grad_values = inv * (scaled - unit * jnp.mean(scaled * unit, axis=-1, keepdims=True))
    return grad_values, jnp.sum(grad * unit, axis=0)


def padded_rows(rows, half):
    blank = jnp.zeros_like(rows)
    return jnp.concatenate([rows, blank] if half == 0 else [blank, rows], axis=0)


def attend_kernel(chunks, q_ref, *refs):
    k_refs, v_refs = refs[:chunks], refs[chunks : 2 * chunks]
    bias_ref, o_ref, lse_ref, s_scr, p_scr = refs[2 * chunks :]
    rows = q_ref.shape[0]
    keys = k_refs[0].shape[0]
    q_t = q_ref[...].T * jnp.asarray(HD**-0.5, BF16)
    v_t = [v[...].T for v in v_refs]
    outs, totals = [], []
    for head in range(2 * GROUP):
        half = head // GROUP
        slot = head % 2
        q_pad = padded_rows(q_t[head * HD : (head + 1) * HD], half)
        peak = None
        for c in range(chunks):
            part = slice(c * keys, (c + 1) * keys)
            scores = mm(k_refs[c][...], q_pad) + bias_ref[part, :]
            s_scr[slot, part, :] = scores
            top = jnp.max(scores, axis=0, keepdims=True)
            peak = top if peak is None else jnp.maximum(peak, top)
        total = jnp.zeros((1, rows), F32)
        mixed = jnp.zeros((HD, rows), F32)
        for c in range(chunks):
            part = slice(c * keys, (c + 1) * keys)
            prob = jnp.exp(s_scr[slot, part, :] - peak)
            total = total + jnp.sum(prob, axis=0, keepdims=True)
            p_scr[slot, part, :] = prob.astype(BF16)
        for c in range(chunks):
            part = slice(c * keys, (c + 1) * keys)
            mixed = mixed + mm(v_t[c][half * HD : (half + 1) * HD], p_scr[slot, part, :])
        outs.append(mixed / total)
        totals.append(peak + jnp.log(total))
    o_ref[...] = jnp.concatenate(outs, axis=0).T.astype(BF16)
    blank = jnp.zeros((8 - 2 * GROUP, rows), F32)
    lse_ref[0] = jnp.concatenate(totals + [blank], axis=0)


def kv_specs(chunks, keys):
    k_spec = pl.BlockSpec((keys, PAIR_K), lambda j: (0, j))
    v_spec = pl.BlockSpec((keys, PAIR_K), lambda j: (0, PAIRS + j))
    return [k_spec] * chunks + [v_spec] * chunks


def attend(queries, kv_chunks, bias):
    rows, width = queries.shape
    chunks, keys = len(kv_chunks), kv_chunks[0].shape[0]
    work = 4 * H * rows * chunks * keys * HD
    q_spec = pl.BlockSpec((rows, PAIR_Q), lambda j: (0, j))
    return pl.pallas_call(
        functools.partial(attend_kernel, chunks),
        grid=(PAIRS,),
        in_specs=[q_spec]
        + kv_specs(chunks, keys)
        + [pl.BlockSpec((chunks * keys, rows), lambda j: (0, 0))],
        out_specs=[q_spec, pl.BlockSpec((1, 8, rows), lambda j: (j, 0, 0))],
        out_shape=[
            jax.ShapeDtypeStruct(queries.shape, BF16),
            jax.ShapeDtypeStruct((PAIRS, 8, rows), F32),
        ],
        scratch_shapes=[
            pltpu.VMEM((2, chunks * keys, rows), F32),
            pltpu.VMEM((2, chunks * keys, rows), BF16),
        ],
        compiler_params=pltpu.CompilerParams(vmem_limit_bytes=60 * 1024 * 1024),
        cost_estimate=pl.CostEstimate(
            flops=work // 64, bytes_accessed=1024 * 1024, transcendentals=0
        ),
        name="path_attention",
    )(queries, *kv_chunks, *kv_chunks, bias)


def attend_back_kernel(chunks, q_ref, g_ref, *refs):
    k_refs, v_refs = refs[:chunks], refs[chunks : 2 * chunks]
    bias_ref, lse_ref, dq_ref = refs[2 * chunks : 2 * chunks + 3]
    out_refs = refs[2 * chunks + 3 : 3 * chunks + 3]
    p_scr, gp_scr, ps_scr, ds_scr = refs[3 * chunks + 3 :]
    rows = q_ref.shape[0]
    keys = k_refs[0].shape[0]
    q_t = q_ref[...].T * jnp.asarray(HD**-0.5, BF16)
    g_t = g_ref[...].T
    k_t = [k[...].T for k in k_refs]
    dqs, q_pads, g_pads = [], [], []
    for head in range(2 * GROUP):
        half = head // GROUP
        slot = head % 2
        here = slice(head * rows, (head + 1) * rows)
        q_pad = padded_rows(q_t[head * HD : (head + 1) * HD], half)
        g_pad = padded_rows(g_t[head * HD : (head + 1) * HD], half)
        q_pads.append(q_pad)
        g_pads.append(g_pad)
        lse = lse_ref[0, head : head + 1, :]
        delta = jnp.zeros((1, rows), F32)
        for c in range(chunks):
            part = slice(c * keys, (c + 1) * keys)
            prob = jnp.exp(mm(k_refs[c][...], q_pad) + bias_ref[part, :] - lse)
            grad_prob = mm(v_refs[c][...], g_pad)
            delta = delta + jnp.sum(prob * grad_prob, axis=0, keepdims=True)
            p_scr[slot, part, :] = prob
            gp_scr[slot, part, :] = grad_prob
            ps_scr[part, here] = prob.astype(BF16)
        dq = jnp.zeros((HD, rows), F32)
        for c in range(chunks):
            part = slice(c * keys, (c + 1) * keys)
            ds = (p_scr[slot, part, :] * (gp_scr[slot, part, :] - delta)).astype(BF16)
            ds_scr[part, here] = ds
            dq = dq + mm(k_t[c][half * HD : (half + 1) * HD], ds)
        dqs.append(dq * HD**-0.5)
    dq_ref[...] = jnp.concatenate(dqs, axis=0).T.astype(BF16)
    q_all = jnp.concatenate(q_pads, axis=1)
    g_all = jnp.concatenate(g_pads, axis=1)
    for c in range(chunks):
        part = slice(c * keys, (c + 1) * keys)
        out_refs[c][0] = mm_nt(ds_scr[part, :], q_all).astype(BF16)
        out_refs[c][1] = mm_nt(ps_scr[part, :], g_all).astype(BF16)


def attend_back(queries, grad_mixed, kv_chunks, bias, lse):
    rows, width = queries.shape
    chunks, keys = len(kv_chunks), kv_chunks[0].shape[0]
    work = 10 * H * rows * chunks * keys * HD
    q_spec = pl.BlockSpec((rows, PAIR_Q), lambda j: (0, j))
    return pl.pallas_call(
        functools.partial(attend_back_kernel, chunks),
        grid=(PAIRS,),
        in_specs=[q_spec, q_spec]
        + kv_specs(chunks, keys)
        + [
            pl.BlockSpec((chunks * keys, rows), lambda j: (0, 0)),
            pl.BlockSpec((1, 8, rows), lambda j: (j, 0, 0)),
        ],
        out_specs=[q_spec] + [pl.BlockSpec((2, keys, PAIR_K), lambda j: (0, 0, j))] * chunks,
        out_shape=[jax.ShapeDtypeStruct(queries.shape, BF16)]
        + [jax.ShapeDtypeStruct((2, keys, KV * HD), BF16)] * chunks,
        scratch_shapes=[
            pltpu.VMEM((2, chunks * keys, rows), F32),
            pltpu.VMEM((2, chunks * keys, rows), F32),
            pltpu.VMEM((chunks * keys, 2 * GROUP * rows), BF16),
            pltpu.VMEM((chunks * keys, 2 * GROUP * rows), BF16),
        ],
        compiler_params=pltpu.CompilerParams(vmem_limit_bytes=60 * 1024 * 1024),
        cost_estimate=pl.CostEstimate(
            flops=work // 64, bytes_accessed=1024 * 1024, transcendentals=0
        ),
        name="path_attention_back",
    )(queries, grad_mixed, *kv_chunks, *kv_chunks, bias, lse)


def ancestry(parents_in):
    count = parents_in.shape[-1]
    labels = jnp.arange(count, dtype=jnp.int32)
    reach = (parents_in[..., :, None] == labels) | (labels[:, None] == labels)
    steps = 1
    while steps < count:
        reach = jnp.any(reach[..., :, :, None] & reach[..., None, :, :], axis=-2)
        steps *= 2
    return reach


def mask_bias(parents, valid, dp_index, n_dp, rows):
    micro = parents.shape[0]
    per = rows // BLOCK
    reach = lax.dynamic_slice_in_dim(ancestry(parents), dp_index * per, per, 1)
    early = (n_dp - 1) * per
    reach = jnp.pad(reach, ((0, 0), (0, 0), (early, 0)))
    reach = lax.dynamic_slice_in_dim(reach, dp_index * per, n_dp * per, 2)
    ok = jnp.pad(valid > 0, ((0, 0), (early * BLOCK, 0)))
    ok = lax.dynamic_slice_in_dim(ok, dp_index * rows, n_dp * rows, 1)
    by_key = jnp.repeat(jnp.swapaxes(reach, 1, 2), BLOCK, axis=1)
    shape = (micro, n_dp * rows, rows)
    key = lax.broadcasted_iota(jnp.int32, shape, 1) - (n_dp - 1) * rows
    query = lax.broadcasted_iota(jnp.int32, shape, 2)
    onpath = jnp.zeros(shape, bool)
    for i in range(per):
        onpath = onpath | ((query // BLOCK == i) & by_key[:, :, i : i + 1])
    allowed = onpath & (key <= query) & (ok[:, :, None] | (key == query))
    return jnp.where(allowed, 0.0, NEGATIVE).astype(F32)


def expert_kernel(block, chips, shards, has_prev, has_acc, last, *refs):
    refs = list(refs)

    def take(n):
        out = refs[:n]
        del refs[:n]
        return out

    h_refs, c_refs = take(2 * chips), take(2)
    order_ref, gate_ref, w_ref = take(3)
    prev = take(4) if has_prev else None
    acc_in = take(2) if has_acc else None
    y_sib, y_own, gh_sib, gh_own = take(4)
    grad_refs = take(2)
    hb, cb, yb, gb, acc_gu, acc_d, wg_ref, wu_ref, wd_ref, sem_in, sem_out, sem_acc, sem_w = take(13)
    if has_prev:
        yp, gp, sem_prev = take(3)
    lead = h_refs[0].shape[0]
    per = block // lead
    half = chips // per
    steps = 2 * half

    def fetch(i, slot):
        for j in range(steps):

            @pl.when(i == j)
            def _():
                for r in range(per):
                    at = j * per + r
                    rows = pl.ds(r * lead, lead)
                    pltpu.make_async_copy(
                        h_refs[at], hb.at[slot, rows], sem_in.at[0, slot]
                    ).start()
                    pltpu.make_async_copy(
                        c_refs[at // chips].at[order_ref[at % chips]],
                        cb.at[slot, rows],
                        sem_in.at[1, slot],
                    ).start()
                if has_prev:
                    rows = pl.ds((j % half) * block, block)
                    for n, buffer in enumerate((yp, gp)):
                        pltpu.make_async_copy(
                            prev[2 * n + j // half].at[rows], buffer.at[slot], sem_prev.at[n, slot]
                        ).start()

    def fetched(slot):
        for n, buffer in enumerate((hb, cb)):
            pltpu.make_async_copy(buffer.at[slot], buffer.at[slot], sem_in.at[n, slot]).wait()
        if has_prev:
            for n, buffer in enumerate((yp, gp)):
                pltpu.make_async_copy(
                    buffer.at[slot], buffer.at[slot], sem_prev.at[n, slot]
                ).wait()

    def copies_out(y_ref, g_ref, at, slot):
        rows = pl.ds(pl.multiple_of(at * block, block), block)
        return (
            pltpu.make_async_copy(yb.at[slot], y_ref.at[rows], sem_out.at[0, slot]),
            pltpu.make_async_copy(gb.at[slot], g_ref.at[rows], sem_out.at[1, slot]),
        )

    def stored(slot):
        for copy in copies_out(y_own, gh_own, 0, slot):
            copy.wait()

    hidden, width = acc_d.shape
    tiles = width // hidden
    band = hidden // shards
    weight_copies = [
        pltpu.make_async_copy(w_ref.at[:, pl.ds(0, hidden)], wg_ref, sem_w.at[0]),
        pltpu.make_async_copy(w_ref.at[:, pl.ds(hidden, hidden)], wu_ref, sem_w.at[1]),
    ]
    for z in range(shards):
        for j in range(tiles):
            copy = pltpu.make_async_copy(
                w_ref.at[pl.ds((z * tiles + j) * band, band), pl.ds(2 * hidden, hidden)],
                wd_ref.at[pl.ds(z * band, band), pl.ds(j * hidden, hidden)],
                sem_w.at[2 + z * tiles + j],
            )
            weight_copies.append(copy)
    for copy in weight_copies:
        copy.start()
    fetch(0, 0)
    if has_acc:
        acc_copies = [
            pltpu.make_async_copy(acc_in[0], acc_gu, sem_acc.at[0]),
            pltpu.make_async_copy(acc_in[1], acc_d, sem_acc.at[1]),
        ]
        for copy in acc_copies:
            copy.start()
    else:
        acc_gu[...] = jnp.zeros_like(acc_gu)
        acc_d[...] = jnp.zeros_like(acc_d)

    for copy in weight_copies:
        copy.wait()

    def step(i, carry):
        slot = lax.rem(i, 2)

        @pl.when(i + 1 < steps)
        def _():
            fetch(i + 1, 1 - slot)

        fetched(slot)

        @pl.when(i >= 2)
        def _():
            stored(slot)

        tokens = hb[slot]
        grads = cb[slot]
        scale = jnp.broadcast_to(gate_ref[i], (8, block)).T[:, :1]
        gate = mm(tokens, wg_ref[...])
        up = mm(tokens, wu_ref[...])
        grad_act = mm_nt(grads, wd_ref[...]) * scale
        sig = jax.nn.sigmoid(gate)
        silu = gate * sig
        act = (silu * up * scale).astype(BF16)
        grad_gate = (grad_act * up * (sig + silu * (1.0 - sig))).astype(BF16)
        grad_up = (grad_act * silu).astype(BF16)
        y = mm(act, wd_ref[...])
        gh = mm_nt(grad_gate, wg_ref[...]) + mm_nt(grad_up, wu_ref[...])
        if has_prev:
            y = y + yp[slot].astype(F32)
            gh = gh + gp[slot].astype(F32)
        yb[slot] = y.astype(BF16)
        gb[slot] = gh.astype(BF16)

        @pl.when(i < half)
        def _():
            for copy in copies_out(y_sib, gh_sib, i, slot):
                copy.start()

        @pl.when(i >= half)
        def _():
            for copy in copies_out(y_own, gh_own, i - half, slot):
                copy.start()

        if has_acc:

            @pl.when(i == 0)
            def _():
                for copy in acc_copies:
                    copy.wait()

        acc_d[...] += mm_tn(act, grads)
        acc_gu[:, :FFE] += mm_tn(tokens, grad_gate)
        acc_gu[:, FFE:] += mm_tn(tokens, grad_up)
        return carry

    lax.fori_loop(0, steps, step, 0)
    stored(steps % 2)
    stored((steps - 1) % 2)
    if last:
        cut = grad_refs[0].shape[1]
        grad_refs[0][...] = acc_gu[:, :cut].astype(BF16)
        grad_refs[1][:, : 2 * hidden - cut] = acc_gu[:, cut:].astype(BF16)
        for z in range(shards):
            for j in range(tiles):
                rows = slice((z * tiles + j) * band, (z * tiles + j + 1) * band)
                piece = acc_d[z * band : (z + 1) * band, j * hidden : (j + 1) * hidden]
                grad_refs[1][rows, 2 * hidden - cut :] = piece.astype(BF16)
    else:
        out = [
            pltpu.make_async_copy(acc_gu, grad_refs[0], sem_acc.at[0]),
            pltpu.make_async_copy(acc_d, grad_refs[1], sem_acc.at[1]),
        ]
        for copy in out:
            copy.start()
        for copy in out:
            copy.wait()


def expert_pass(h_all, c_all, order, gates, weight, shards, previous, totals, last, block=512):
    chips = len(h_all) // 2
    lead, width = h_all[0].shape
    rows = chips * lead
    hidden = weight.shape[1] // 3
    far = pl.BlockSpec(memory_space=pl.ANY)
    near = pl.BlockSpec(memory_space=pltpu.VMEM)
    scalars = pl.BlockSpec(memory_space=pltpu.SMEM)
    token_out = jax.ShapeDtypeStruct((rows, width), BF16)
    token_buffer = pltpu.VMEM((2, block, width), BF16)
    if last:
        first = 3 * hidden // 2
        grads = [((width, first), BF16), ((width, 3 * hidden - first), BF16)]
    else:
        grads = [((width, 2 * hidden), F32), ((hidden, width), F32)]
    scratch = [token_buffer] * 4 + [
        pltpu.VMEM((width, 2 * hidden), F32),
        pltpu.VMEM((hidden, width), F32),
        pltpu.VMEM((width, hidden), BF16),
        pltpu.VMEM((width, hidden), BF16),
        pltpu.VMEM((hidden, width), BF16),
        pltpu.SemaphoreType.DMA((2, 2)),
        pltpu.SemaphoreType.DMA((2, 2)),
        pltpu.SemaphoreType.DMA((2,)),
        pltpu.SemaphoreType.DMA((2 + shards * (width // hidden),)),
    ]
    extra, aliases = [], {}
    if previous is not None:
        scratch += [token_buffer] * 2 + [pltpu.SemaphoreType.DMA((2, 2))]
        aliases = {2 * chips + 5 + n: n for n in range(4)}
        extra += list(previous)
    if totals is not None:
        extra += list(totals)
    return pl.pallas_call(
        functools.partial(
            expert_kernel, block, chips, shards, previous is not None, totals is not None, last
        ),
        in_specs=[far] * (2 * chips + 2) + [scalars, near, far] + [far] * len(extra),
        out_specs=[far] * 4 + [near if last else far] * len(grads),
        out_shape=[token_out] * 4 + [jax.ShapeDtypeStruct(*g) for g in grads],
        scratch_shapes=scratch,
        input_output_aliases=aliases,
        compiler_params=pltpu.CompilerParams(vmem_limit_bytes=60 * 1024 * 1024),
        cost_estimate=pl.CostEstimate(
            flops=rows * width, bytes_accessed=rows * width, transcendentals=0
        ),
        name="expert_pass",
    )(*h_all, *c_all, order, gates, weight, *extra)


SMALL = pl.CostEstimate(flops=1024, bytes_accessed=1024, transcendentals=0)
FAR = pl.BlockSpec(memory_space=pl.ANY)
NEAR = pl.BlockSpec(memory_space=pltpu.VMEM)
SCALARS = pl.BlockSpec(memory_space=pltpu.SMEM)


def small_call(kernel, name, inputs, outs, in_specs=None, scratch=()):
    return pl.pallas_call(
        kernel,
        in_specs=in_specs or [NEAR] * len(inputs),
        out_specs=[NEAR] * len(outs),
        out_shape=[jax.ShapeDtypeStruct(shape, dtype) for shape, dtype in outs],
        scratch_shapes=list(scratch),
        compiler_params=pltpu.CompilerParams(vmem_limit_bytes=48 * 1024 * 1024),
        cost_estimate=SMALL,
        name=name,
    )(*inputs)


def assemble_kernel(counts, chunk, place_ref, *refs):
    out_ref, sem = refs[len(counts) :]
    copies, n = [], 0
    for ref, count in zip(refs, counts):
        for at in range(count):
            rows = pl.ds(pl.multiple_of(place_ref[n] * chunk, chunk), chunk)
            copies.append(pltpu.make_async_copy(ref.at[at], out_ref.at[rows], sem))
            n += 1
    for copy in copies:
        copy.start()
    for copy in copies:
        copy.wait()


def assemble(blocks, places):
    chunk, width = blocks[0].shape[1:]
    counts = [x.shape[0] for x in blocks]
    rows = sum(counts) * chunk
    if chunk % 16:
        bands = jnp.concatenate(blocks, axis=0)
        whole = jnp.zeros_like(bands).at[places].set(bands)
        return whole.reshape(rows, width)
    return pl.pallas_call(
        functools.partial(assemble_kernel, counts, chunk),
        in_specs=[SCALARS] + [FAR] * len(blocks),
        out_specs=NEAR,
        out_shape=jax.ShapeDtypeStruct((rows, width), BF16),
        scratch_shapes=[pltpu.SemaphoreType.DMA],
        compiler_params=pltpu.CompilerParams(vmem_limit_bytes=32 * 1024 * 1024),
        cost_estimate=SMALL,
        name="assemble",
    )(places, *blocks)


def project_kernel(width, *refs):
    micro = (len(refs) - 2) // 3
    x_refs, w_ref = refs[:micro], refs[micro]
    h_refs, kv_refs, gains_ref = refs[micro + 1 : -1 - micro], refs[-1 - micro : -1], refs[-1]
    kv_from = w_ref.shape[1] - 128 - kv_refs[0].shape[1]
    gains = w_ref[:, -128:].astype(F32).T
    gains_ref[...] = gains[:8]
    for x_ref, h_ref, kv_ref in zip(x_refs, h_refs, kv_refs):
        h = rms_norm(x_ref[...].astype(F32), gains[:1]).astype(BF16)
        h_ref[...] = h
        kv_ref[...] = mm(h, w_ref[:, kv_from:-128]).astype(BF16)


def project(xs, weight, kv_width):
    rows, width = xs[0].shape
    outs = (
        [((rows, width), BF16)] * len(xs)
        + [((rows, kv_width), BF16)] * len(xs)
        + [((8, width), F32)]
    )
    got = small_call(functools.partial(project_kernel, width), "project", [*xs, weight], outs)
    return list(got[: len(xs)]), list(got[len(xs) : -1]), got[-1]


def middle_kernel(attn_ref, x_ref, gains_ref, w_ref, mid_ref, h_ref):
    mid = x_ref[...].astype(F32) + mm_nt(attn_ref[...], w_ref[...])
    mid_ref[...] = mid
    h_ref[...] = rms_norm(mid, gains_ref[1:2]).astype(BF16)


def middle(attn, x, gains, w_out_t):
    return small_call(
        middle_kernel,
        "middle",
        [attn, x, gains, w_out_t],
        [(x.shape, F32), (x.shape, BF16)],
    )


def middle_back_kernel(got_ref, mid_ref, c_ref, gains_ref, w_ref, gx_ref, branch_ref, gain_ref, mixed_ref):
    grad = got_ref[0].astype(F32)
    for k in range(1, got_ref.shape[0]):
        grad = grad + got_ref[k].astype(F32)
    part, gain_part = rms_back(mid_ref[...], gains_ref[1:2], grad)
    grad_x = c_ref[...].astype(F32) + part
    branch = grad_x.astype(BF16)
    gx_ref[...] = grad_x
    branch_ref[...] = branch
    gain_ref[...] = jnp.broadcast_to(gain_part[None], gain_ref.shape)
    mixed_ref[...] = mm(branch, w_ref[...]).astype(BF16)


def middle_back(got, mid, c, gains, w_out_t):
    return small_call(
        middle_back_kernel,
        "middle_back",
        [got, mid, c, gains, w_out_t],
        [(c.shape, F32), (c.shape, BF16), ((8, c.shape[1]), F32), (c.shape, BF16)],
    )


def input_back_kernel(q_ref, kv_ref, x_ref, mid_ref, gains_ref, w_ref, grad_ref):
    query_width = q_ref.shape[1]
    cut = w_ref.shape[1] - 128
    grad_h = mm_nt(q_ref[...], w_ref[:, :query_width])
    grad_h = grad_h + mm_nt(kv_ref[:, : cut - query_width], w_ref[:, query_width:cut])
    part, _ = rms_back(x_ref[...].astype(F32), gains_ref[:1], grad_h)
    grad_ref[...] = (mid_ref[...] + part).astype(BF16)


def input_back(grad_q, grad_kv, x, grad_x_mid, gains, weight):
    return small_call(
        input_back_kernel,
        "input_back",
        [grad_q, grad_kv, x, grad_x_mid, gains, weight],
        [(x.shape, BF16)],
    )[0]


def unpack_kernel(*refs):
    up_ref, down_ref = refs[-2:]
    for e in range(up_ref.shape[0]):
        first, second = refs[2 * e][...], refs[2 * e + 1][...]
        cut = up_ref.shape[2] - first.shape[1]
        up_ref[e] = jnp.concatenate([first, second[:, :cut]], axis=1).astype(F32)
        pieces = second[:, cut:].astype(F32)
        rows, wide = down_ref.shape[1], pieces.shape[1]
        for j in range(down_ref.shape[2] // wide):
            down_ref[e, :, j * wide : (j + 1) * wide] = pieces[j * rows : (j + 1) * rows]


def unpack(totals, up_shape, down_shape):
    flat = [t for pair in totals for t in pair]
    return small_call(unpack_kernel, "unpack", flat, [(up_shape, F32), (down_shape, F32)])


def band_totals_kernel(counts, dp_ref, *refs):
    refs = list(refs)
    groups = []
    for count in counts:
        groups.append(refs[:count])
        del refs[:count]
    own_ref, piece_refs = refs[0], refs[1:]

    def total(ref):
        held = ref[0].astype(F32)
        for k in range(1, ref.shape[0]):
            held = held + ref[k].astype(F32)
        return held

    columns = []
    for group in groups:
        if len(group) == 1 and len(group[0].shape) == 4:
            columns.append(total(group[0]))
        else:
            columns.append(functools.reduce(jnp.add, [ref[...].astype(F32) for ref in group]))
    whole = jnp.concatenate(columns, axis=-1)
    dp_index = dp_ref[0]
    for z in range(whole.shape[0]):

        @pl.when(dp_index == z)
        def _():
            own_ref[...] = whole[z]

        for k, ref in enumerate(piece_refs):

            @pl.when((dp_index ^ (k + 1)) == z)
            def _():
                ref[...] = whole[z].astype(BF16)


def band_totals(groups, dp_index):
    n_dp, chunk = groups[0][0].shape[-3:-1]
    width = sum(group[0].shape[-1] for group in groups)
    inputs = [dp_index.reshape(1)] + [x for group in groups for x in group]
    own, *pieces = small_call(
        functools.partial(band_totals_kernel, [len(group) for group in groups]),
        "band_totals",
        inputs,
        [((chunk, width), F32)] + [((chunk, width), BF16)] * (n_dp - 1),
        in_specs=[SCALARS] + [NEAR] * (len(inputs) - 1),
    )
    return own, pieces


def sums_kernel(order_ref, own_ref, other_ref, out_ref):
    out_ref[...] = (own_ref[...].astype(F32) + other_ref[...].astype(F32)).astype(BF16)


def sums(own, other, order):
    blank = (0,) * (own.ndim - 1)
    block = (1,) + own.shape[1:]
    spec = pl.BlockSpec(block, lambda i, order: (i,) + blank)
    return pl.pallas_call(
        sums_kernel,
        grid_spec=pltpu.PrefetchScalarGridSpec(
            num_scalar_prefetch=1,
            grid=(own.shape[0],),
            in_specs=[spec, spec],
            out_specs=pl.BlockSpec(block, lambda i, order: (order[i],) + blank),
        ),
        out_shape=jax.ShapeDtypeStruct(own.shape, BF16),
        compiler_params=pltpu.CompilerParams(vmem_limit_bytes=32 * 1024 * 1024),
        cost_estimate=SMALL,
        name="sums",
    )(order, own, other)


def weight_grad_kernel(parts, chunk, n_dp, has_extra, core_ref, *refs):
    left, right = refs[:parts], refs[parts : 2 * parts]
    own_ref, other_ref = refs[-2:]
    total = mm_tn(left[0][...], right[0][...])
    for a, b in zip(left[1:], right[1:]):
        total = total + mm_tn(a[...], b[...])
    if has_extra:
        total = total + refs[2 * parts][...].astype(F32)
    total = total.astype(BF16)
    chips = total.shape[0] // (2 * chunk * n_dp)
    pairs = total.reshape(n_dp, chips, 2, chunk, total.shape[1])
    first = core_ref[0] == 0
    for z in range(n_dp):
        for j in range(chips):
            own_ref[j, z] = jnp.where(first, pairs[z, j, 0], pairs[z, j, 1])
            other_ref[j, z] = jnp.where(first, pairs[z, j, 1], pairs[z, j, 0])


def weight_grad(left, right, n_dp, chips, core, extra=None):
    width, columns = left[0].shape[1], right[0].shape[1]
    chunk = width // (2 * n_dp * chips)
    if chunk % 16:
        total = sum(mm_tn(a, b) for a, b in zip(left, right))
        if extra is not None:
            total = total + extra.astype(F32)
        total = total.astype(BF16)
        pairs = total.reshape(n_dp, chips, 2, chunk, columns)
        return [
            jnp.swapaxes(lax.dynamic_index_in_dim(pairs, c, 2, keepdims=False), 0, 1)
            for c in (core, 1 - core)
        ]
    parts, tokens = len(left), left[0].shape[0]
    block = 512 if columns % 512 == 0 else 384
    shape = (chips, n_dp, chunk)
    extras = [] if extra is None else [extra]
    band = jax.ShapeDtypeStruct(shape + (columns,), BF16)
    band_spec = pl.BlockSpec(shape + (block,), lambda j: (0, 0, 0, j))
    return pl.pallas_call(
        functools.partial(weight_grad_kernel, parts, chunk, n_dp, bool(extras)),
        grid=(columns // block,),
        in_specs=[SCALARS]
        + [pl.BlockSpec((tokens, width), lambda j: (0, 0))] * parts
        + [pl.BlockSpec((tokens, block), lambda j: (0, j))] * parts
        + [pl.BlockSpec((width, block), lambda j: (0, j))] * len(extras),
        out_specs=[band_spec, band_spec],
        out_shape=[band, band],
        compiler_params=pltpu.CompilerParams(vmem_limit_bytes=32 * 1024 * 1024),
        cost_estimate=SMALL,
        name="weight_grad",
    )(core.reshape(1).astype(jnp.int32), *left, *right, *extras)


def join(*items):
    return lax.optimization_barrier(items)


class Plane:
    def __init__(self, count):
        self.count = count
        self.chips = count // 2

    def swap(self, x):
        return lax.ppermute(x, "expert", [(i, i ^ 1) for i in range(self.count)])

    def cross(self, x, k):
        return lax.ppermute(x, "expert", [(i, i ^ (2 * k)) for i in range(self.count)])

    def exchange(self, x):
        groups = [[chip * 2 + c for chip in range(self.chips)] for c in range(2)]
        return lax.all_to_all(
            x, "expert", split_axis=0, concat_axis=0, axis_index_groups=groups, tiled=True
        )

    def spread(self, x):
        return self.exchange(jnp.broadcast_to(x[None], (self.chips,) + x.shape))

    def doubled(self, held, n):
        bits = [1 << i for i in range(self.chips.bit_length() - 1)]
        return [
            {**blocks, **{k ^ bit: self.cross(x, bit) for k, x in blocks.items()}}
            for blocks, bit in zip(held, (bits[n], bits[-1 - n]))
        ]

    def crosses(self, x, ks):
        return [self.cross(x, k) for k in ks]


def added(first, others):
    for x in others:
        first = first + x.astype(F32)
    return first


def dp_cross(x, k, n_dp):
    return lax.ppermute(x, "dp", [(i, i ^ k) for i in range(n_dp)])


def dp_along(x, by, n_dp):
    pairs = [(i, i + by) for i in range(n_dp) if 0 <= i + by < n_dp]
    return lax.ppermute(x, "dp", pairs)


def dp_others(x, n_dp):
    return [dp_cross(x, k, n_dp) for k in range(1, n_dp)]


def body(
    n_dp,
    n_expert,
    tokens,
    cotangent,
    parents,
    valid_mask,
    routes,
    route_gates,
    norm_gains,
    w_qkv,
    w_out,
    w_gate_up,
    w_down,
):
    both = ("dp", "expert")
    micro, _, rows, width = tokens.shape
    micros = range(micro)
    count = micro * rows
    top = routes.shape[-1]
    query_width = H * HD
    kv_width = KV * HD
    local_experts = w_gate_up.shape[0]
    experts = local_experts * n_expert
    plane = Plane(n_expert)
    dp_index = lax.axis_index("dp")

    x_in = [tokens[m, 0] for m in micros]
    grad_out = [cotangent[m, 0] for m in micros]
    expert_index = lax.axis_index("expert")
    core, chip = expert_index % 2, expert_index // 2
    every, lags = range(1, plane.chips), range(1, n_dp)
    near, far = every[:-1], every[-1:]

    def over_dp(x):
        return lax.all_gather(x, "dp", axis=0, tiled=True)

    chosen = routes.reshape(count, top)[:, :, None] == jnp.arange(experts, dtype=jnp.int32)
    table = jnp.sum(jnp.where(chosen, route_gates.reshape(count, top)[:, :, None], 0.0), axis=1)
    table = table.T.reshape(n_expert, local_experts, micro, rows)
    table = lax.all_to_all(table, "expert", split_axis=0, concat_axis=0, tiled=True)
    sides = [2 * k + 1 for k in range(plane.chips)] + [2 * k for k in range(plane.chips)]
    table = jnp.take(table, expert_index ^ jnp.array(sides, jnp.int32), axis=0)
    gates = [[table[:, e, m].reshape(-1, 1, 512) for m in micros] for e in range(local_experts)]
    bias = mask_bias(
        parents.reshape(micro, -1), valid_mask.reshape(micro, -1), dp_index, n_dp, rows
    )
    bias = [bias[m] for m in micros]
    same = jnp.arange(plane.chips, dtype=jnp.int32)
    order = chip ^ same

    half = n_dp // 2

    def bands(line, chip_at, core_at):
        return [((dp_index ^ z) * plane.chips + chip_at) * 2 + core_at for z in line]

    def wide(x):
        return jnp.broadcast_to(x[None], (plane.chips,) + x.shape)

    packed = [
        jnp.concatenate(
            [w_gate_up[e], w_down[e].reshape(-1, width // FFE, FFE).swapaxes(0, 1).reshape(-1, FFE)],
            axis=1,
        )
        for e in range(local_experts)
    ]
    gains_t = jnp.pad(norm_gains.T, ((0, 0), (0, 126)))
    own_rows = jnp.concatenate([w_qkv, gains_t], axis=1)
    qkv_line, out_rows, gates, bias, order, w_first = join(
        [own_rows] + dp_others(own_rows, n_dp),
        jnp.broadcast_to(w_out.T[None], (n_dp,) + w_out.shape[::-1]),
        gates,
        bias,
        order,
        packed[0],
    )
    expert_w = [over_dp(w_first)]
    line = jnp.stack(qkv_line)
    held = plane.doubled([{0: line[:half]}, {0: line[half:]}], 0)
    out_line = lax.all_to_all(out_rows, "dp", split_axis=0, concat_axis=0, tiled=True)
    held, line_swap = join(held, plane.swap(line))
    for n in range(1, plane.chips.bit_length() - 1):
        held = plane.doubled(held, n)
    held, out_line, c_wide, w_last = join(
        held, out_line, [wide(c) for c in grad_out], packed[1]
    )
    moved = [(h, k, held[h][k]) for k in every for h in range(2)]
    out_spread = plane.exchange(wide(out_line))
    swapped = list(join(*[plane.swap(x) for _, _, x in moved]))
    lines = [range(half), range(half, n_dp)]
    places = bands(range(n_dp), chip, core) + bands(range(n_dp), chip, 1 - core)
    for c in (core, 1 - core):
        for h, k, _ in moved:
            places += bands(lines[h], chip ^ k, c)
    weight = assemble(
        [line, line_swap] + [x for _, _, x in moved] + swapped, jnp.stack(places)
    )

    (h_in, kv, gains), out_spread = join(project(x_in, weight, 2 * kv_width), out_spread)
    w_q = weight[:, :query_width]
    queries = [mm(h, w_q).astype(BF16) for h in h_in]

    c_0 = plane.exchange(c_wide[0])
    out_swap = plane.swap(out_spread)
    places = []
    for c in (core, 1 - core):
        for j in range(plane.chips):
            places += [(z * plane.chips + j) * 2 + c for z in range(n_dp)]
    w_out_t = assemble(
        [x.reshape((-1,) + x.shape[2:]) for x in (out_spread, out_swap)], jnp.stack(places)
    )
    chunks_0, kv[1], queries, w_out_t, c_0, expert_w[0] = join(
        [dp_along(kv[0], d, n_dp) for d in reversed(lags)],
        kv[1],
        queries,
        w_out_t,
        c_0,
        expert_w[0],
    )
    kv_chunks = [list(chunks_0) + [kv[0]]]
    ends = [lags[0], lags[-1]]
    between = [d for d in lags if d not in ends]
    (mixed, total), held, c_swap = join(
        attend(queries[0], kv_chunks[0], bias[0]),
        [dp_along(kv[1], d, n_dp) for d in between],
        plane.swap(c_0),
    )
    held_1 = dict(zip(between, held))
    c_1 = plane.exchange(c_wide[1])
    c_all = [[c_swap, c_0]]
    attn, lse = [mixed], [total]
    x, h = middle(attn[0], x_in[0], gains, w_out_t)
    x_mid, h_mid = [x], [h]
    held, h_others, w_last, c_1 = join(
        [dp_along(kv[1], d, n_dp) for d in ends], plane.crosses(h, every), w_last, c_1
    )
    held_1.update(zip(ends, held))
    kv_chunks.append([held_1[d] for d in reversed(lags)] + [kv[1]])
    (mixed, total), h_swap = join(
        attend(queries[1], kv_chunks[1], bias[1]),
        [plane.swap(x) for x in [h] + list(h_others)],
    )
    attn.append(mixed)
    lse.append(total)
    h_all = [[*h_swap, h, *h_others], None]
    (x, h), c_swap = join(middle(attn[1], x_in[1], gains, w_out_t), plane.swap(c_1))
    c_all.append([c_swap, c_1])
    x_mid.append(x)
    h_mid.append(h)

    def run(e, m, gate):
        out = expert_pass(
            h_all[m],
            c_all[m],
            order,
            gate,
            expert_w[e],
            n_dp,
            carried[m],
            totals[e],
            m + 1 == micro,
        )
        return out[:4], out[4:]

    def split(x):
        return x.reshape((plane.chips, -1) + x.shape[1:])

    totals, carried = [None] * local_experts, [None] * micro
    (carried[0], totals[0]), h_cross, h_swap = join(
        run(0, 0, gates[0][0]), plane.crosses(h_mid[1], every), plane.swap(h_mid[1])
    )
    h_all[1] = [h_swap] + [plane.swap(x) for x in h_cross] + [h_mid[1]] + h_cross
    (carried[1], totals[0]), w_whole, gate = join(
        run(0, 1, gates[0][1]), over_dp(w_last), gates[1][0]
    )
    expert_w.append(w_whole)

    def summed(x):
        return lax.psum_scatter(x, "dp", scatter_dimension=0, tiled=True)

    totals_s = [[summed(t) for t in totals[0]]]
    carried[0], totals[1] = run(1, 0, gate)
    y_sib_0, y_own_0, gh_sib_0, gh_own_0 = carried[0]
    gh_chips = sums(split(gh_own_0), split(plane.swap(gh_sib_0)), order)
    gate, gh_chips, y_sib_0 = join(gates[1][1], gh_chips, y_sib_0)
    (carried[1], totals[1]), gh_got, y_swap_0 = join(
        run(1, 1, gate), plane.exchange(gh_chips), plane.swap(y_sib_0)
    )
    y_sib_1, y_own_1, gh_sib_1, gh_own_1 = carried[1]

    def back_of(m, got):
        return middle_back(got, x_mid[m], grad_out[m], gains, w_out_t)

    def attention_back(m, grad_mixed):
        dq, *dkv = attend_back(queries[m], grad_mixed, kv_chunks[m], bias[m], lse[m])
        return dq, dkv

    def returned(dkv, ds):
        return [dp_along(dkv[n_dp - 1 - d], -d, n_dp) for d in ds]

    def weights_of(left, right, extra=None):
        return weight_grad(left, right, n_dp, plane.chips, core, extra)

    back_0, gh_swap, y_sib_1 = join(back_of(0, gh_got), plane.swap(gh_sib_1), y_sib_1)
    gh_chips = sums(split(gh_own_1), split(gh_swap), order)
    grad_mixed, gh_chips, y_swap_0 = join(back_0[3], gh_chips, y_swap_0)
    gh_got = plane.exchange(gh_chips)
    totals_s.append([summed(totals[1][0])])
    grad_q_0, dkv_0 = attention_back(0, grad_mixed)
    y_swap_0, grad_q_0 = join(y_swap_0, grad_q_0)
    grad_q_0, dkv_0, gh_got, y_chips_0, y_swap_1, totals_s[0], totals_s[1][0] = join(
        grad_q_0,
        dkv_0,
        gh_got,
        sums(split(y_own_0), split(y_swap_0), order),
        plane.swap(y_sib_1),
        totals_s[0],
        totals_s[1][0],
    )
    back_1 = back_of(1, gh_got)
    grad_x_mid, grad_branch, gain_parts, _ = zip(back_0, back_1)
    gain_mid = sum(g[0] for g in gain_parts)
    gain_high = gain_mid.astype(BF16)
    gain_mid = jnp.stack([gain_high, (gain_mid - gain_high.astype(F32)).astype(BF16)], axis=1)
    gain_mid = jnp.pad(gain_mid, ((0, 0), (2 * kv_width, 126)))
    soon, late = lags[:1], lags[-1:]
    grad_mixed, out_bands, held = join(
        back_1[3], weights_of(grad_branch, attn), returned(dkv_0, soon)
    )
    held_0 = dict(zip(soon, held))
    (grad_q_1, dkv_1), held, y_got_0, y_swap_1, gain_mid, out_swap = join(
        attention_back(1, grad_mixed),
        returned(dkv_0, between),
        plane.exchange(y_chips_0),
        y_swap_1,
        gain_mid,
        plane.swap(out_bands[1]),
    )
    held_0.update(zip(between, held))
    grad_q = [grad_q_0, grad_q_1]

    held, q_bands, y_chips_1, gain_mid, out_chips = join(
        returned(dkv_1, ends),
        weights_of(h_in, grad_q),
        sums(split(y_own_1), split(y_swap_1), order),
        gain_mid,
        sums(out_bands[0], out_swap, same),
    )
    held_1 = dict(zip(ends, held))
    out_got = plane.exchange(out_chips)
    held, held_late, q_chips, out_got, last_half = join(
        returned(dkv_1, between),
        returned(dkv_0, late),
        sums(q_bands[0], plane.swap(q_bands[1]), same),
        out_got,
        totals[1][1],
    )
    held_1.update(zip(between, held))
    held_0.update(zip(late, held_late))
    totals_s[1].append(summed(last_half))
    total_0 = added(dkv_0[-1].astype(F32), [held_0[d] for d in lags])
    total_1 = added(dkv_1[-1].astype(F32), [held_1[d] for d in lags])
    blank = jnp.zeros((rows, 128), F32)
    grad_kv = [
        jnp.concatenate([t[0], t[1], blank], axis=1).astype(BF16) for t in (total_0, total_1)
    ]
    kv_bands = weights_of(h_in, grad_kv, gain_mid)
    q_got = plane.exchange(q_chips)
    kv_swap, out_got = join(plane.swap(kv_bands[1]), out_got)
    kv_chips = sums(kv_bands[0], kv_swap, order)
    kv_own = [kv_chips[k] for k in range(plane.chips)]
    out_total, out_pieces = band_totals([[out_got]], dp_index)

    def over_dp_links(pieces):
        return [dp_cross(x, z, n_dp) for z, x in zip(lags, pieces)]

    kv_sent, q_got, grad_kv, totals_s, y_chips_1, out_sent = join(
        [plane.cross(kv_own[k], k) for k in every],
        q_got,
        grad_kv,
        totals_s,
        y_chips_1,
        over_dp_links(out_pieces),
    )
    grad_x = [
        input_back(grad_q[m], grad_kv[m], x_in[m], grad_x_mid[m], gains, weight) for m in micros
    ]
    y_got_1 = plane.exchange(y_chips_1)
    grad_gu_s, grad_down_s = unpack(totals_s, w_gate_up.shape, w_down.shape)
    total, pieces = band_totals([[q_got], [kv_own[0], *kv_sent]], dp_index)
    sent, y_got_1, grad_gu_s, grad_down_s, grad_x = join(
        over_dp_links(pieces), y_got_1, grad_gu_s, grad_down_s, grad_x
    )
    out_total, total = added(out_total, out_sent), added(total, sent)

    qkv_width = w_qkv.shape[1]
    grad_wqkv = total[:, :qkv_width]
    gain_in = jnp.sum(w_qkv.astype(F32) * grad_wqkv, axis=1) / norm_gains[0].astype(F32)
    x_out = [
        x_mid[m] + jnp.sum(y.astype(F32), axis=0) for m, y in enumerate((y_got_0, y_got_1))
    ]
    return (
        jnp.stack([x.astype(BF16) for x in x_out])[:, None],
        jnp.stack(grad_x)[:, None],
        jnp.stack([gain_in, total[:, qkv_width] + total[:, qkv_width + 1]]),
        grad_wqkv,
        out_total.T,
        grad_gu_s,
        grad_down_s,
    )


def solution(mesh):
    tokens_spec = P(None, "expert", "dp", None)
    experts_spec = P("expert", "dp", None)
    rows_spec = P(("dp", "expert"), None)
    columns_spec = P(None, ("dp", "expert"))
    return jax.shard_map(
        functools.partial(body, mesh.shape["dp"], mesh.shape["expert"]),
        mesh=mesh,
        in_specs=(
            tokens_spec,
            tokens_spec,
            P(None, "expert", None),
            P(None, "expert", None),
            tokens_spec,
            tokens_spec,
            columns_spec,
            rows_spec,
            columns_spec,
            experts_spec,
            experts_spec,
        ),
        out_specs=(
            tokens_spec,
            tokens_spec,
            columns_spec,
            rows_spec,
            columns_spec,
            experts_spec,
            experts_spec,
        ),
        check_vma=False,
    )
```

```python
import functools

import jax
import jax.numpy as jnp
from jax import lax
from jax.experimental import pallas as pl
from jax.experimental.pallas import tpu as pltpu
from jax.sharding import PartitionSpec as P

H = 24
KV = 8
HD = 64
FFE = 512
BLOCK = 128
PAIRS = KV // 2
GROUP = H // KV
PAIR_Q = 2 * GROUP * HD
PAIR_K = 2 * HD

EPSILON = 1e-06
NEGATIVE = -1e30
F32 = jnp.float32
BF16 = jnp.bfloat16


def mm(a, b):
    return jnp.dot(a, b, preferred_element_type=F32)


def mm_nt(a, b):
    return lax.dot_general(a, b, (((1,), (1,)), ((), ())), preferred_element_type=F32)


def mm_tn(a, b):
    return lax.dot_general(a, b, (((0,), (0,)), ((), ())), preferred_element_type=F32)


def rms_norm(values_in, gain):
    return (
        values_in
        * lax.rsqrt(jnp.mean(values_in * values_in, axis=-1, keepdims=True) + EPSILON)
        * gain
    )


def rms_back(values, gain, grad):
    inv = lax.rsqrt(jnp.mean(values * values, axis=-1, keepdims=True) + EPSILON)
    unit = values * inv
    scaled = grad * gain
    grad_values = inv * (scaled - unit * jnp.mean(scaled * unit, axis=-1, keepdims=True))
    return grad_values, jnp.sum(grad * unit, axis=0)


def padded_rows(rows, half):
    blank = jnp.zeros_like(rows)
    return jnp.concatenate([rows, blank] if half == 0 else [blank, rows], axis=0)


def attend_kernel(chunks, q_ref, *refs):
    k_refs, v_refs = refs[:chunks], refs[chunks : 2 * chunks]
    bias_ref, o_ref, lse_ref, s_scr, p_scr = refs[2 * chunks :]
    rows = q_ref.shape[0]
    keys = k_refs[0].shape[0]
    q_t = q_ref[...].T * jnp.asarray(HD**-0.5, BF16)
    v_t = [v[...].T for v in v_refs]
    outs, totals = [], []
    for head in range(2 * GROUP):
        half = head // GROUP
        slot = head % 2
        q_pad = padded_rows(q_t[head * HD : (head + 1) * HD], half)
        peak = None
        for c in range(chunks):
            part = slice(c * keys, (c + 1) * keys)
            scores = mm(k_refs[c][...], q_pad) + bias_ref[part, :]
            s_scr[slot, part, :] = scores
            top = jnp.max(scores, axis=0, keepdims=True)
            peak = top if peak is None else jnp.maximum(peak, top)
        total = jnp.zeros((1, rows), F32)
        mixed = jnp.zeros((HD, rows), F32)
        for c in range(chunks):
            part = slice(c * keys, (c + 1) * keys)
            prob = jnp.exp(s_scr[slot, part, :] - peak)
            total = total + jnp.sum(prob, axis=0, keepdims=True)
            p_scr[slot, part, :] = prob.astype(BF16)
        for c in range(chunks):
            part = slice(c * keys, (c + 1) * keys)
            mixed = mixed + mm(v_t[c][half * HD : (half + 1) * HD], p_scr[slot, part, :])
        outs.append(mixed / total)
        totals.append(peak + jnp.log(total))
    o_ref[...] = jnp.concatenate(outs, axis=0).T.astype(BF16)
    blank = jnp.zeros((8 - 2 * GROUP, rows), F32)
    lse_ref[0] = jnp.concatenate(totals + [blank], axis=0)


def kv_specs(chunks, keys):
    k_spec = pl.BlockSpec((keys, PAIR_K), lambda j: (0, j))
    v_spec = pl.BlockSpec((keys, PAIR_K), lambda j: (0, PAIRS + j))
    return [k_spec] * chunks + [v_spec] * chunks


def attend(queries, kv_chunks, bias):
    rows, width = queries.shape
    chunks, keys = len(kv_chunks), kv_chunks[0].shape[0]
    work = 4 * H * rows * chunks * keys * HD
    q_spec = pl.BlockSpec((rows, PAIR_Q), lambda j: (0, j))
    return pl.pallas_call(
        functools.partial(attend_kernel, chunks),
        grid=(PAIRS,),
        in_specs=[q_spec]
        + kv_specs(chunks, keys)
        + [pl.BlockSpec((chunks * keys, rows), lambda j: (0, 0))],
        out_specs=[q_spec, pl.BlockSpec((1, 8, rows), lambda j: (j, 0, 0))],
        out_shape=[
            jax.ShapeDtypeStruct(queries.shape, BF16),
            jax.ShapeDtypeStruct((PAIRS, 8, rows), F32),
        ],
        scratch_shapes=[
            pltpu.VMEM((2, chunks * keys, rows), F32),
            pltpu.VMEM((2, chunks * keys, rows), BF16),
        ],
        compiler_params=pltpu.CompilerParams(vmem_limit_bytes=60 * 1024 * 1024),
        cost_estimate=pl.CostEstimate(
            flops=work // 64, bytes_accessed=1024 * 1024, transcendentals=0
        ),
        name="path_attention",
    )(queries, *kv_chunks, *kv_chunks, bias)


def attend_back_kernel(chunks, q_ref, g_ref, *refs):
    k_refs, v_refs = refs[:chunks], refs[chunks : 2 * chunks]
    bias_ref, lse_ref, dq_ref = refs[2 * chunks : 2 * chunks + 3]
    out_refs = refs[2 * chunks + 3 : 3 * chunks + 3]
    p_scr, gp_scr, ps_scr, ds_scr = refs[3 * chunks + 3 :]
    rows = q_ref.shape[0]
    keys = k_refs[0].shape[0]
    q_t = q_ref[...].T * jnp.asarray(HD**-0.5, BF16)
    g_t = g_ref[...].T
    k_t = [k[...].T for k in k_refs]
    dqs, q_pads, g_pads = [], [], []
    for head in range(2 * GROUP):
        half = head // GROUP
        slot = head % 2
        here = slice(head * rows, (head + 1) * rows)
        q_pad = padded_rows(q_t[head * HD : (head + 1) * HD], half)
        g_pad = padded_rows(g_t[head * HD : (head + 1) * HD], half)
        q_pads.append(q_pad)
        g_pads.append(g_pad)
        lse = lse_ref[0, head : head + 1, :]
        delta = jnp.zeros((1, rows), F32)
        for c in range(chunks):
            part = slice(c * keys, (c + 1) * keys)
            prob = jnp.exp(mm(k_refs[c][...], q_pad) + bias_ref[part, :] - lse)
            grad_prob = mm(v_refs[c][...], g_pad)
            delta = delta + jnp.sum(prob * grad_prob, axis=0, keepdims=True)
            p_scr[slot, part, :] = prob
            gp_scr[slot, part, :] = grad_prob
            ps_scr[part, here] = prob.astype(BF16)
        dq = jnp.zeros((HD, rows), F32)
        for c in range(chunks):
            part = slice(c * keys, (c + 1) * keys)
            ds = (p_scr[slot, part, :] * (gp_scr[slot, part, :] - delta)).astype(BF16)
            ds_scr[part, here] = ds
            dq = dq + mm(k_t[c][half * HD : (half + 1) * HD], ds)
        dqs.append(dq * HD**-0.5)
    dq_ref[...] = jnp.concatenate(dqs, axis=0).T.astype(BF16)
    q_all = jnp.concatenate(q_pads, axis=1)
    g_all = jnp.concatenate(g_pads, axis=1)
    for c in range(chunks):
        part = slice(c * keys, (c + 1) * keys)
        out_refs[c][0] = mm_nt(ds_scr[part, :], q_all).astype(BF16)
        out_refs[c][1] = mm_nt(ps_scr[part, :], g_all).astype(BF16)


def attend_back(queries, grad_mixed, kv_chunks, bias, lse):
    rows, width = queries.shape
    chunks, keys = len(kv_chunks), kv_chunks[0].shape[0]
    work = 10 * H * rows * chunks * keys * HD
    q_spec = pl.BlockSpec((rows, PAIR_Q), lambda j: (0, j))
    return pl.pallas_call(
        functools.partial(attend_back_kernel, chunks),
        grid=(PAIRS,),
        in_specs=[q_spec, q_spec]
        + kv_specs(chunks, keys)
        + [
            pl.BlockSpec((chunks * keys, rows), lambda j: (0, 0)),
            pl.BlockSpec((1, 8, rows), lambda j: (j, 0, 0)),
        ],
        out_specs=[q_spec] + [pl.BlockSpec((2, keys, PAIR_K), lambda j: (0, 0, j))] * chunks,
        out_shape=[jax.ShapeDtypeStruct(queries.shape, BF16)]
        + [jax.ShapeDtypeStruct((2, keys, KV * HD), BF16)] * chunks,
        scratch_shapes=[
            pltpu.VMEM((2, chunks * keys, rows), F32),
            pltpu.VMEM((2, chunks * keys, rows), F32),
            pltpu.VMEM((chunks * keys, 2 * GROUP * rows), BF16),
            pltpu.VMEM((chunks * keys, 2 * GROUP * rows), BF16),
        ],
        compiler_params=pltpu.CompilerParams(vmem_limit_bytes=60 * 1024 * 1024),
        cost_estimate=pl.CostEstimate(
            flops=work // 64, bytes_accessed=1024 * 1024, transcendentals=0
        ),
        name="path_attention_back",
    )(queries, grad_mixed, *kv_chunks, *kv_chunks, bias, lse)


def ancestry(parents_in):
    count = parents_in.shape[-1]
    labels = jnp.arange(count, dtype=jnp.int32)
    reach = (parents_in[..., :, None] == labels) | (labels[:, None] == labels)
    steps = 1
    while steps < count:
        reach = jnp.any(reach[..., :, :, None] & reach[..., None, :, :], axis=-2)
        steps *= 2
    return reach


def mask_bias(parents, valid, dp_index, n_dp, rows):
    micro = parents.shape[0]
    per = rows // BLOCK
    reach = lax.dynamic_slice_in_dim(ancestry(parents), dp_index * per, per, 1)
    early = (n_dp - 1) * per
    reach = jnp.pad(reach, ((0, 0), (0, 0), (early, 0)))
    reach = lax.dynamic_slice_in_dim(reach, dp_index * per, n_dp * per, 2)
    ok = jnp.pad(valid > 0, ((0, 0), (early * BLOCK, 0)))
    ok = lax.dynamic_slice_in_dim(ok, dp_index * rows, n_dp * rows, 1)
    by_key = jnp.repeat(jnp.swapaxes(reach, 1, 2), BLOCK, axis=1)
    shape = (micro, n_dp * rows, rows)
    key = lax.broadcasted_iota(jnp.int32, shape, 1) - (n_dp - 1) * rows
    query = lax.broadcasted_iota(jnp.int32, shape, 2)
    onpath = jnp.zeros(shape, bool)
    for i in range(per):
        onpath = onpath | ((query // BLOCK == i) & by_key[:, :, i : i + 1])
    allowed = onpath & (key <= query) & (ok[:, :, None] | (key == query))
    return jnp.where(allowed, 0.0, NEGATIVE).astype(F32)


def expert_kernel(block, chips, shards, has_prev, has_acc, last, *refs):
    refs = list(refs)

    def take(n):
        out = refs[:n]
        del refs[:n]
        return out

    h_refs, c_refs = take(2 * chips), take(2)
    order_ref, gate_ref, w_ref = take(3)
    prev = take(4) if has_prev else None
    acc_in = take(2) if has_acc else None
    y_sib, y_own, gh_sib, gh_own = take(4)
    grad_refs = take(2)
    hb, cb, yb, gb, acc_gu, acc_d, wg_ref, wu_ref, wd_ref, sem_in, sem_out, sem_acc, sem_w = take(13)
    if has_prev:
        yp, gp, sem_prev = take(3)
    lead = h_refs[0].shape[0]
    per = block // lead
    half = chips // per
    steps = 2 * half

    def fetch(i, slot):
        for j in range(steps):

            @pl.when(i == j)
            def _():
                for r in range(per):
                    at = j * per + r
                    rows = pl.ds(r * lead, lead)
                    pltpu.make_async_copy(
                        h_refs[at], hb.at[slot, rows], sem_in.at[0, slot]
                    ).start()
                    pltpu.make_async_copy(
                        c_refs[at // chips].at[order_ref[at % chips]],
                        cb.at[slot, rows],
                        sem_in.at[1, slot],
                    ).start()
                if has_prev:
                    rows = pl.ds((j % half) * block, block)
                    for n, buffer in enumerate((yp, gp)):
                        pltpu.make_async_copy(
                            prev[2 * n + j // half].at[rows], buffer.at[slot], sem_prev.at[n, slot]
                        ).start()

    def fetched(slot):
        for n, buffer in enumerate((hb, cb)):
            pltpu.make_async_copy(buffer.at[slot], buffer.at[slot], sem_in.at[n, slot]).wait()
        if has_prev:
            for n, buffer in enumerate((yp, gp)):
                pltpu.make_async_copy(
                    buffer.at[slot], buffer.at[slot], sem_prev.at[n, slot]
                ).wait()

    def copies_out(y_ref, g_ref, at, slot):
        rows = pl.ds(pl.multiple_of(at * block, block), block)
        return (
            pltpu.make_async_copy(yb.at[slot], y_ref.at[rows], sem_out.at[0, slot]),
            pltpu.make_async_copy(gb.at[slot], g_ref.at[rows], sem_out.at[1, slot]),
        )

    def stored(slot):
        for copy in copies_out(y_own, gh_own, 0, slot):
            copy.wait()

    hidden, width = acc_d.shape
    tiles = width // hidden
    band = hidden // shards
    weight_copies = [
        pltpu.make_async_copy(w_ref.at[:, pl.ds(0, hidden)], wg_ref, sem_w.at[0]),
        pltpu.make_async_copy(w_ref.at[:, pl.ds(hidden, hidden)], wu_ref, sem_w.at[1]),
    ]
    for z in range(shards):
        for j in range(tiles):
            copy = pltpu.make_async_copy(
                w_ref.at[pl.ds((z * tiles + j) * band, band), pl.ds(2 * hidden, hidden)],
                wd_ref.at[pl.ds(z * band, band), pl.ds(j * hidden, hidden)],
                sem_w.at[2 + z * tiles + j],
            )
            weight_copies.append(copy)
    for copy in weight_copies:
        copy.start()
    fetch(0, 0)
    if has_acc:
        acc_copies = [
            pltpu.make_async_copy(acc_in[0], acc_gu, sem_acc.at[0]),
            pltpu.make_async_copy(acc_in[1], acc_d, sem_acc.at[1]),
        ]
        for copy in acc_copies:
            copy.start()
    else:
        acc_gu[...] = jnp.zeros_like(acc_gu)
        acc_d[...] = jnp.zeros_like(acc_d)

    for copy in weight_copies:
        copy.wait()

    def step(i, carry):
        slot = lax.rem(i, 2)

        @pl.when(i + 1 < steps)
        def _():
            fetch(i + 1, 1 - slot)

        fetched(slot)

        @pl.when(i >= 2)
        def _():
            stored(slot)

        tokens = hb[slot]
        grads = cb[slot]
        scale = jnp.broadcast_to(gate_ref[i], (8, block)).T[:, :1]
        gate = mm(tokens, wg_ref[...])
        up = mm(tokens, wu_ref[...])
        grad_act = mm_nt(grads, wd_ref[...]) * scale
        sig = jax.nn.sigmoid(gate)
        silu = gate * sig
        act = (silu * up * scale).astype(BF16)
        grad_gate = (grad_act * up * (sig + silu * (1.0 - sig))).astype(BF16)
        grad_up = (grad_act * silu).astype(BF16)
        y = mm(act, wd_ref[...])
        gh = mm_nt(grad_gate, wg_ref[...]) + mm_nt(grad_up, wu_ref[...])
        if has_prev:
            y = y + yp[slot].astype(F32)
            gh = gh + gp[slot].astype(F32)
        yb[slot] = y.astype(BF16)
        gb[slot] = gh.astype(BF16)

        @pl.when(i < half)
        def _():
            for copy in copies_out(y_sib, gh_sib, i, slot):
                copy.start()

        @pl.when(i >= half)
        def _():
            for copy in copies_out(y_own, gh_own, i - half, slot):
                copy.start()

        if has_acc:

            @pl.when(i == 0)
            def _():
                for copy in acc_copies:
                    copy.wait()

        acc_d[...] += mm_tn(act, grads)
        acc_gu[:, :FFE] += mm_tn(tokens, grad_gate)
        acc_gu[:, FFE:] += mm_tn(tokens, grad_up)
        return carry

    lax.fori_loop(0, steps, step, 0)
    stored(steps % 2)
    stored((steps - 1) % 2)
    if last:
        cut = grad_refs[0].shape[1]
        grad_refs[0][...] = acc_gu[:, :cut].astype(BF16)
        grad_refs[1][:, : 2 * hidden - cut] = acc_gu[:, cut:].astype(BF16)
        for z in range(shards):
            for j in range(tiles):
                rows = slice((z * tiles + j) * band, (z * tiles + j + 1) * band)
                piece = acc_d[z * band : (z + 1) * band, j * hidden : (j + 1) * hidden]
                grad_refs[1][rows, 2 * hidden - cut :] = piece.astype(BF16)
    else:
        out = [
            pltpu.make_async_copy(acc_gu, grad_refs[0], sem_acc.at[0]),
            pltpu.make_async_copy(acc_d, grad_refs[1], sem_acc.at[1]),
        ]
        for copy in out:
            copy.start()
        for copy in out:
            copy.wait()


def expert_pass(h_all, c_all, order, gates, weight, shards, previous, totals, last, block=512):
    chips = len(h_all) // 2
    lead, width = h_all[0].shape
    rows = chips * lead
    hidden = weight.shape[1] // 3
    far = pl.BlockSpec(memory_space=pl.ANY)
    near = pl.BlockSpec(memory_space=pltpu.VMEM)
    scalars = pl.BlockSpec(memory_space=pltpu.SMEM)
    token_out = jax.ShapeDtypeStruct((rows, width), BF16)
    token_buffer = pltpu.VMEM((2, block, width), BF16)
    if last:
        first = 3 * hidden // 2
        grads = [((width, first), BF16), ((width, 3 * hidden - first), BF16)]
    else:
        grads = [((width, 2 * hidden), F32), ((hidden, width), F32)]
    scratch = [token_buffer] * 4 + [
        pltpu.VMEM((width, 2 * hidden), F32),
        pltpu.VMEM((hidden, width), F32),
        pltpu.VMEM((width, hidden), BF16),
        pltpu.VMEM((width, hidden), BF16),
        pltpu.VMEM((hidden, width), BF16),
        pltpu.SemaphoreType.DMA((2, 2)),
        pltpu.SemaphoreType.DMA((2, 2)),
        pltpu.SemaphoreType.DMA((2,)),
        pltpu.SemaphoreType.DMA((2 + shards * (width // hidden),)),
    ]
    extra, aliases = [], {}
    if previous is not None:
        scratch += [token_buffer] * 2 + [pltpu.SemaphoreType.DMA((2, 2))]
        aliases = {2 * chips + 5 + n: n for n in range(4)}
        extra += list(previous)
    if totals is not None:
        extra += list(totals)
    return pl.pallas_call(
        functools.partial(
            expert_kernel, block, chips, shards, previous is not None, totals is not None, last
        ),
        in_specs=[far] * (2 * chips + 2) + [scalars, near, far] + [far] * len(extra),
        out_specs=[far] * 4 + [near if last else far] * len(grads),
        out_shape=[token_out] * 4 + [jax.ShapeDtypeStruct(*g) for g in grads],
        scratch_shapes=scratch,
        input_output_aliases=aliases,
        compiler_params=pltpu.CompilerParams(vmem_limit_bytes=60 * 1024 * 1024),
        cost_estimate=pl.CostEstimate(
            flops=rows * width, bytes_accessed=rows * width, transcendentals=0
        ),
        name="expert_pass",
    )(*h_all, *c_all, order, gates, weight, *extra)


SMALL = pl.CostEstimate(flops=1024, bytes_accessed=1024, transcendentals=0)
FAR = pl.BlockSpec(memory_space=pl.ANY)
NEAR = pl.BlockSpec(memory_space=pltpu.VMEM)
SCALARS = pl.BlockSpec(memory_space=pltpu.SMEM)


def small_call(kernel, name, inputs, outs, in_specs=None, scratch=()):
    return pl.pallas_call(
        kernel,
        in_specs=in_specs or [NEAR] * len(inputs),
        out_specs=[NEAR] * len(outs),
        out_shape=[jax.ShapeDtypeStruct(shape, dtype) for shape, dtype in outs],
        scratch_shapes=list(scratch),
        compiler_params=pltpu.CompilerParams(vmem_limit_bytes=48 * 1024 * 1024),
        cost_estimate=SMALL,
        name=name,
    )(*inputs)


def repeat_kernel(x_ref, out_ref):
    out_ref[...] = jnp.broadcast_to(x_ref[...][None], out_ref.shape)


def repeat(x, count):
    return small_call(repeat_kernel, "repeat", [x], [((count,) + x.shape, x.dtype)])[0]


def assemble_kernel(counts, chunk, place_ref, *refs):
    out_ref, sem = refs[len(counts) :]
    copies, n = [], 0
    for ref, count in zip(refs, counts):
        for at in range(count):
            rows = pl.ds(pl.multiple_of(place_ref[n] * chunk, chunk), chunk)
            copies.append(pltpu.make_async_copy(ref.at[at], out_ref.at[rows], sem))
            n += 1
    for copy in copies:
        copy.start()
    for copy in copies:
        copy.wait()


def assemble(blocks, places):
    chunk, width = blocks[0].shape[1:]
    counts = [x.shape[0] for x in blocks]
    rows = sum(counts) * chunk
    if chunk % 16:
        bands = jnp.concatenate(blocks, axis=0)
        whole = jnp.zeros_like(bands).at[places].set(bands)
        return whole.reshape(rows, width)
    return pl.pallas_call(
        functools.partial(assemble_kernel, counts, chunk),
        in_specs=[SCALARS] + [FAR] * len(blocks),
        out_specs=NEAR,
        out_shape=jax.ShapeDtypeStruct((rows, width), BF16),
        scratch_shapes=[pltpu.SemaphoreType.DMA],
        compiler_params=pltpu.CompilerParams(vmem_limit_bytes=32 * 1024 * 1024),
        cost_estimate=SMALL,
        name="assemble",
    )(places, *blocks)


def project_kernel(micro, counts, chunk, place_ref, *refs):
    refs = list(refs)

    def take(n):
        out = refs[:n]
        del refs[:n]
        return out

    x_refs, blocks = take(micro), take(len(counts))
    h_refs, kv_refs = take(micro), take(micro)
    gains_ref, whole_ref, w_ref, sem_in, sem_out = refs
    copies, n = [], 0
    for ref, count in zip(blocks, counts):
        for at in range(count):
            rows = pl.ds(pl.multiple_of(place_ref[n] * chunk, chunk), chunk)
            copies.append(pltpu.make_async_copy(ref.at[at], w_ref.at[rows], sem_in))
            n += 1
    for copy in copies:
        copy.start()
    for copy in copies:
        copy.wait()
    out = pltpu.make_async_copy(w_ref, whole_ref, sem_out)
    out.start()
    kv_from = w_ref.shape[1] - 128 - kv_refs[0].shape[1]
    gains = w_ref[:, -128:].astype(F32).T
    gains_ref[...] = gains[:8]
    for x_ref, h_ref, kv_ref in zip(x_refs, h_refs, kv_refs):
        h = rms_norm(x_ref[...].astype(F32), gains[:1]).astype(BF16)
        h_ref[...] = h
        kv_ref[...] = mm(h, w_ref[:, kv_from:-128]).astype(BF16)
    out.wait()


def project(xs, blocks, places, kv_width):
    micro, (rows, width) = len(xs), xs[0].shape
    if blocks[0].shape[1] % 16:
        blocks, places = [assemble(blocks, places)[None]], jnp.zeros((1,), jnp.int32)
    chunk, columns = blocks[0].shape[1:]
    counts = [x.shape[0] for x in blocks]
    weight = (sum(counts) * chunk, columns)
    outs = (
        [((rows, width), BF16)] * micro
        + [((rows, kv_width), BF16)] * micro
        + [((8, width), F32), (weight, BF16)]
    )
    got = pl.pallas_call(
        functools.partial(project_kernel, micro, counts, chunk),
        in_specs=[SCALARS] + [NEAR] * micro + [FAR] * len(blocks),
        out_specs=[NEAR] * (2 * micro + 1) + [FAR],
        out_shape=[jax.ShapeDtypeStruct(shape, dtype) for shape, dtype in outs],
        scratch_shapes=[
            pltpu.VMEM(weight, BF16),
            pltpu.SemaphoreType.DMA,
            pltpu.SemaphoreType.DMA,
        ],
        compiler_params=pltpu.CompilerParams(vmem_limit_bytes=48 * 1024 * 1024),
        cost_estimate=SMALL,
        name="project",
    )(places, *xs, *blocks)
    return list(got[:micro]), list(got[micro : 2 * micro]), got[-2], got[-1]


def middle_kernel(attn_ref, x_ref, gains_ref, w_ref, mid_ref, h_ref):
    mid = x_ref[...].astype(F32) + mm_nt(attn_ref[...], w_ref[...])
    mid_ref[...] = mid
    h_ref[...] = rms_norm(mid, gains_ref[1:2]).astype(BF16)


def middle(attn, x, gains, w_out_t):
    return small_call(
        middle_kernel,
        "middle",
        [attn, x, gains, w_out_t],
        [(x.shape, F32), (x.shape, BF16)],
    )


def middle_back_kernel(got_ref, mid_ref, c_ref, gains_ref, w_ref, gx_ref, branch_ref, gain_ref, mixed_ref):
    grad = got_ref[0].astype(F32)
    for k in range(1, got_ref.shape[0]):
        grad = grad + got_ref[k].astype(F32)
    part, gain_part = rms_back(mid_ref[...], gains_ref[1:2], grad)
    grad_x = c_ref[...].astype(F32) + part
    branch = grad_x.astype(BF16)
    gx_ref[...] = grad_x
    branch_ref[...] = branch
    gain_ref[...] = jnp.broadcast_to(gain_part[None], gain_ref.shape)
    mixed_ref[...] = mm(branch, w_ref[...]).astype(BF16)


def middle_back(got, mid, c, gains, w_out_t):
    return small_call(
        middle_back_kernel,
        "middle_back",
        [got, mid, c, gains, w_out_t],
        [(c.shape, F32), (c.shape, BF16), ((8, c.shape[1]), F32), (c.shape, BF16)],
    )


def input_back_kernel(q_ref, kv_ref, x_ref, mid_ref, gains_ref, w_ref, grad_ref):
    query_width = q_ref.shape[1]
    cut = w_ref.shape[1] - 128
    grad_h = mm_nt(q_ref[...], w_ref[:, :query_width])
    grad_h = grad_h + mm_nt(kv_ref[:, : cut - query_width], w_ref[:, query_width:cut])
    part, _ = rms_back(x_ref[...].astype(F32), gains_ref[:1], grad_h)
    grad_ref[...] = (mid_ref[...] + part).astype(BF16)


def input_back(grad_q, grad_kv, x, grad_x_mid, gains, weight):
    return small_call(
        input_back_kernel,
        "input_back",
        [grad_q, grad_kv, x, grad_x_mid, gains, weight],
        [(x.shape, BF16)],
    )[0]


def unpack_kernel(*refs):
    up_ref, down_ref = refs[-2:]
    for e in range(up_ref.shape[0]):
        first, second = refs[2 * e][...], refs[2 * e + 1][...]
        cut = up_ref.shape[2] - first.shape[1]
        up_ref[e] = jnp.concatenate([first, second[:, :cut]], axis=1).astype(F32)
        pieces = second[:, cut:].astype(F32)
        rows, wide = down_ref.shape[1], pieces.shape[1]
        for j in range(down_ref.shape[2] // wide):
            down_ref[e, :, j * wide : (j + 1) * wide] = pieces[j * rows : (j + 1) * rows]


def unpack(totals, up_shape, down_shape):
    flat = [t for pair in totals for t in pair]
    return small_call(unpack_kernel, "unpack", flat, [(up_shape, F32), (down_shape, F32)])


def band_totals_kernel(counts, dp_ref, *refs):
    refs = list(refs)
    groups = []
    for count in counts:
        groups.append(refs[:count])
        del refs[:count]
    own_ref, piece_refs = refs[0], refs[1:]

    def total(ref):
        held = ref[0].astype(F32)
        for k in range(1, ref.shape[0]):
            held = held + ref[k].astype(F32)
        return held

    columns = []
    for group in groups:
        if len(group) == 1 and len(group[0].shape) == 4:
            columns.append(total(group[0]))
        else:
            columns.append(functools.reduce(jnp.add, [ref[...].astype(F32) for ref in group]))
    whole = jnp.concatenate(columns, axis=-1)
    dp_index = dp_ref[0]
    for z in range(whole.shape[0]):

        @pl.when(dp_index == z)
        def _():
            own_ref[...] = whole[z]

        for k, ref in enumerate(piece_refs):

            @pl.when((dp_index ^ (k + 1)) == z)
            def _():
                ref[...] = whole[z].astype(BF16)


def band_totals(groups, dp_index):
    n_dp, chunk = groups[0][0].shape[-3:-1]
    width = sum(group[0].shape[-1] for group in groups)
    inputs = [dp_index.reshape(1)] + [x for group in groups for x in group]
    own, *pieces = small_call(
        functools.partial(band_totals_kernel, [len(group) for group in groups]),
        "band_totals",
        inputs,
        [((chunk, width), F32)] + [((chunk, width), BF16)] * (n_dp - 1),
        in_specs=[SCALARS] + [NEAR] * (len(inputs) - 1),
    )
    return own, pieces


def sums_kernel(order_ref, own_ref, other_ref, out_ref):
    out_ref[...] = (own_ref[...].astype(F32) + other_ref[...].astype(F32)).astype(BF16)


def sums(own, other, order):
    blank = (0,) * (own.ndim - 1)
    block = (1,) + own.shape[1:]
    spec = pl.BlockSpec(block, lambda i, order: (i,) + blank)
    return pl.pallas_call(
        sums_kernel,
        grid_spec=pltpu.PrefetchScalarGridSpec(
            num_scalar_prefetch=1,
            grid=(own.shape[0],),
            in_specs=[spec, spec],
            out_specs=pl.BlockSpec(block, lambda i, order: (order[i],) + blank),
        ),
        out_shape=jax.ShapeDtypeStruct(own.shape, BF16),
        compiler_params=pltpu.CompilerParams(vmem_limit_bytes=32 * 1024 * 1024),
        cost_estimate=SMALL,
        name="sums",
    )(order, own, other)


def weight_grad_kernel(parts, chunk, n_dp, has_extra, core_ref, *refs):
    left, right = refs[:parts], refs[parts : 2 * parts]
    own_ref, other_ref = refs[-2:]
    total = mm_tn(left[0][...], right[0][...])
    for a, b in zip(left[1:], right[1:]):
        total = total + mm_tn(a[...], b[...])
    if has_extra:
        total = total + refs[2 * parts][...].astype(F32)
    total = total.astype(BF16)
    chips = total.shape[0] // (2 * chunk * n_dp)
    pairs = total.reshape(n_dp, chips, 2, chunk, total.shape[1])
    first = core_ref[0] == 0
    for z in range(n_dp):
        for j in range(chips):
            own_ref[j, z] = jnp.where(first, pairs[z, j, 0], pairs[z, j, 1])
            other_ref[j, z] = jnp.where(first, pairs[z, j, 1], pairs[z, j, 0])


def weight_grad(left, right, n_dp, chips, core, extra=None):
    width, columns = left[0].shape[1], right[0].shape[1]
    chunk = width // (2 * n_dp * chips)
    if chunk % 16:
        total = sum(mm_tn(a, b) for a, b in zip(left, right))
        if extra is not None:
            total = total + extra.astype(F32)
        total = total.astype(BF16)
        pairs = total.reshape(n_dp, chips, 2, chunk, columns)
        return [
            jnp.swapaxes(lax.dynamic_index_in_dim(pairs, c, 2, keepdims=False), 0, 1)
            for c in (core, 1 - core)
        ]
    parts, tokens = len(left), left[0].shape[0]
    block = 512 if columns % 512 == 0 else 384
    shape = (chips, n_dp, chunk)
    extras = [] if extra is None else [extra]
    band = jax.ShapeDtypeStruct(shape + (columns,), BF16)
    band_spec = pl.BlockSpec(shape + (block,), lambda j: (0, 0, 0, j))
    return pl.pallas_call(
        functools.partial(weight_grad_kernel, parts, chunk, n_dp, bool(extras)),
        grid=(columns // block,),
        in_specs=[SCALARS]
        + [pl.BlockSpec((tokens, width), lambda j: (0, 0))] * parts
        + [pl.BlockSpec((tokens, block), lambda j: (0, j))] * parts
        + [pl.BlockSpec((width, block), lambda j: (0, j))] * len(extras),
        out_specs=[band_spec, band_spec],
        out_shape=[band, band],
        compiler_params=pltpu.CompilerParams(vmem_limit_bytes=32 * 1024 * 1024),
        cost_estimate=SMALL,
        name="weight_grad",
    )(core.reshape(1).astype(jnp.int32), *left, *right, *extras)


def join(*items):
    return lax.optimization_barrier(items)


class Plane:
    def __init__(self, count):
        self.count = count
        self.chips = count // 2

    def swap(self, x):
        return lax.ppermute(x, "expert", [(i, i ^ 1) for i in range(self.count)])

    def cross(self, x, k):
        return lax.ppermute(x, "expert", [(i, i ^ (2 * k)) for i in range(self.count)])

    def exchange(self, x):
        groups = [[chip * 2 + c for chip in range(self.chips)] for c in range(2)]
        return lax.all_to_all(
            x, "expert", split_axis=0, concat_axis=0, axis_index_groups=groups, tiled=True
        )

    def spread(self, x):
        return self.exchange(jnp.broadcast_to(x[None], (self.chips,) + x.shape))

    def doubled(self, held, n):
        bits = [1 << i for i in range(self.chips.bit_length() - 1)]
        return [
            {**blocks, **{k ^ bit: self.cross(x, bit) for k, x in blocks.items()}}
            for blocks, bit in zip(held, (bits[n], bits[-1 - n]))
        ]

    def crosses(self, x, ks):
        return [self.cross(x, k) for k in ks]


def added(first, others):
    for x in others:
        first = first + x.astype(F32)
    return first


def dp_cross(x, k, n_dp):
    return lax.ppermute(x, "dp", [(i, i ^ k) for i in range(n_dp)])


def dp_along(x, by, n_dp):
    pairs = [(i, i + by) for i in range(n_dp) if 0 <= i + by < n_dp]
    return lax.ppermute(x, "dp", pairs)


def dp_others(x, n_dp):
    return [dp_cross(x, k, n_dp) for k in range(1, n_dp)]


def body(
    n_dp,
    n_expert,
    tokens,
    cotangent,
    parents,
    valid_mask,
    routes,
    route_gates,
    norm_gains,
    w_qkv,
    w_out,
    w_gate_up,
    w_down,
):
    both = ("dp", "expert")
    micro, _, rows, width = tokens.shape
    micros = range(micro)
    count = micro * rows
    top = routes.shape[-1]
    query_width = H * HD
    kv_width = KV * HD
    local_experts = w_gate_up.shape[0]
    experts = local_experts * n_expert
    plane = Plane(n_expert)
    dp_index = lax.axis_index("dp")

    x_in = [tokens[m, 0] for m in micros]
    grad_out = [cotangent[m, 0] for m in micros]
    expert_index = lax.axis_index("expert")
    core, chip = expert_index % 2, expert_index // 2
    every, lags = range(1, plane.chips), range(1, n_dp)
    near, far = every[:-1], every[-1:]

    def over_dp(x):
        return lax.all_gather(x, "dp", axis=0, tiled=True)

    chosen = routes.reshape(count, top)[:, :, None] == jnp.arange(experts, dtype=jnp.int32)
    table = jnp.sum(jnp.where(chosen, route_gates.reshape(count, top)[:, :, None], 0.0), axis=1)
    table = table.T.reshape(n_expert, local_experts, micro, rows)
    table = lax.all_to_all(table, "expert", split_axis=0, concat_axis=0, tiled=True)
    sides = [2 * k + 1 for k in range(plane.chips)] + [2 * k for k in range(plane.chips)]
    table = jnp.take(table, expert_index ^ jnp.array(sides, jnp.int32), axis=0)
    gates = [[table[:, e, m].reshape(-1, 1, 512) for m in micros] for e in range(local_experts)]
    bias = mask_bias(
        parents.reshape(micro, -1), valid_mask.reshape(micro, -1), dp_index, n_dp, rows
    )
    bias = [bias[m] for m in micros]
    same = jnp.arange(plane.chips, dtype=jnp.int32)
    order = chip ^ same

    half = n_dp // 2

    def bands(line, chip_at, core_at):
        return [((dp_index ^ z) * plane.chips + chip_at) * 2 + core_at for z in line]

    def wide(x):
        return jnp.broadcast_to(x[None], (plane.chips,) + x.shape)

    packed = [
        jnp.concatenate(
            [w_gate_up[e], w_down[e].reshape(-1, width // FFE, FFE).swapaxes(0, 1).reshape(-1, FFE)],
            axis=1,
        )
        for e in range(local_experts)
    ]
    gains_t = jnp.pad(norm_gains.T, ((0, 0), (0, 126)))
    own_rows = jnp.concatenate([w_qkv, gains_t], axis=1)
    qkv_line, out_rows, gates, bias, order, w_first = join(
        [own_rows] + dp_others(own_rows, n_dp),
        jnp.broadcast_to(w_out.T[None], (n_dp,) + w_out.shape[::-1]),
        gates,
        bias,
        order,
        packed[0],
    )
    expert_w = [over_dp(w_first)]
    line = jnp.stack(qkv_line)
    held = plane.doubled([{0: line[:half]}, {0: line[half:]}], 0)
    out_line = lax.all_to_all(out_rows, "dp", split_axis=0, concat_axis=0, tiled=True)
    held, line_swap = join(held, plane.swap(line))
    for n in range(1, plane.chips.bit_length() - 1):
        held = plane.doubled(held, n)
    held, out_line, c_wide, w_last = join(
        held, out_line, [repeat(c, plane.chips) for c in grad_out], packed[1]
    )
    moved = [(h, k, held[h][k]) for k in every for h in range(2)]
    out_spread = plane.exchange(wide(out_line))
    swapped = list(join(*[plane.swap(x) for _, _, x in moved]))
    lines = [range(half), range(half, n_dp)]
    places = bands(range(n_dp), chip, core) + bands(range(n_dp), chip, 1 - core)
    for c in (core, 1 - core):
        for h, k, _ in moved:
            places += bands(lines[h], chip ^ k, c)
    blocks = [line, line_swap] + [x for _, _, x in moved] + swapped
    places = jnp.stack(places)

    (h_in, kv, gains, weight), out_spread = join(
        project(x_in, blocks, places, 2 * kv_width), out_spread
    )
    w_q = weight[:, :query_width]
    queries = [mm(h, w_q).astype(BF16) for h in h_in]

    c_0 = plane.exchange(c_wide[0])
    out_swap = plane.swap(out_spread)
    places = []
    for c in (core, 1 - core):
        for j in range(plane.chips):
            places += [(z * plane.chips + j) * 2 + c for z in range(n_dp)]
    w_out_t = assemble(
        [x.reshape((-1,) + x.shape[2:]) for x in (out_spread, out_swap)], jnp.stack(places)
    )
    chunks_0, kv[1], queries, w_out_t, c_0, expert_w[0] = join(
        [dp_along(kv[0], d, n_dp) for d in reversed(lags)],
        kv[1],
        queries,
        w_out_t,
        c_0,
        expert_w[0],
    )
    kv_chunks = [list(chunks_0) + [kv[0]]]
    ends = [lags[0], lags[-1]]
    between = [d for d in lags if d not in ends]
    (mixed, total), held, c_swap = join(
        attend(queries[0], kv_chunks[0], bias[0]),
        [dp_along(kv[1], d, n_dp) for d in between],
        plane.swap(c_0),
    )
    held_1 = dict(zip(between, held))
    c_1 = plane.exchange(c_wide[1])
    c_all = [[c_swap, c_0]]
    attn, lse = [mixed], [total]
    x, h = middle(attn[0], x_in[0], gains, w_out_t)
    x_mid, h_mid = [x], [h]
    held, h_others, w_last, c_1 = join(
        [dp_along(kv[1], d, n_dp) for d in ends], plane.crosses(h, every), w_last, c_1
    )
    held_1.update(zip(ends, held))
    kv_chunks.append([held_1[d] for d in reversed(lags)] + [kv[1]])
    (mixed, total), h_swap = join(
        attend(queries[1], kv_chunks[1], bias[1]),
        [plane.swap(x) for x in [h] + list(h_others)],
    )
    attn.append(mixed)
    lse.append(total)
    h_all = [[*h_swap, h, *h_others], None]
    (x, h), c_swap = join(middle(attn[1], x_in[1], gains, w_out_t), plane.swap(c_1))
    c_all.append([c_swap, c_1])
    x_mid.append(x)
    h_mid.append(h)

    def run(e, m, gate):
        out = expert_pass(
            h_all[m],
            c_all[m],
            order,
            gate,
            expert_w[e],
            n_dp,
            carried[m],
            totals[e],
            m + 1 == micro,
        )
        return out[:4], out[4:]

    def split(x):
        return x.reshape((plane.chips, -1) + x.shape[1:])

    totals, carried = [None] * local_experts, [None] * micro
    (carried[0], totals[0]), h_cross, h_swap = join(
        run(0, 0, gates[0][0]), plane.crosses(h_mid[1], every), plane.swap(h_mid[1])
    )
    h_all[1] = [h_swap] + [plane.swap(x) for x in h_cross] + [h_mid[1]] + h_cross
    (carried[1], totals[0]), w_whole, gate = join(
        run(0, 1, gates[0][1]), over_dp(w_last), gates[1][0]
    )
    expert_w.append(w_whole)

    def summed(x):
        return lax.psum_scatter(x, "dp", scatter_dimension=0, tiled=True)

    totals_s = [[summed(t) for t in totals[0]]]
    carried[0], totals[1] = run(1, 0, gate)
    y_sib_0, y_own_0, gh_sib_0, gh_own_0 = carried[0]
    gh_chips = sums(split(gh_own_0), split(plane.swap(gh_sib_0)), order)
    gate, gh_chips, y_sib_0 = join(gates[1][1], gh_chips, y_sib_0)
    (carried[1], totals[1]), gh_got, y_swap_0 = join(
        run(1, 1, gate), plane.exchange(gh_chips), plane.swap(y_sib_0)
    )
    y_sib_1, y_own_1, gh_sib_1, gh_own_1 = carried[1]

    def back_of(m, got):
        return middle_back(got, x_mid[m], grad_out[m], gains, w_out_t)

    def attention_back(m, grad_mixed):
        dq, *dkv = attend_back(queries[m], grad_mixed, kv_chunks[m], bias[m], lse[m])
        return dq, dkv

    def returned(dkv, ds):
        return [dp_along(dkv[n_dp - 1 - d], -d, n_dp) for d in ds]

    def weights_of(left, right, extra=None):
        return weight_grad(left, right, n_dp, plane.chips, core, extra)

    back_0, gh_swap, y_sib_1 = join(back_of(0, gh_got), plane.swap(gh_sib_1), y_sib_1)
    gh_chips = sums(split(gh_own_1), split(gh_swap), order)
    grad_mixed, gh_chips, y_swap_0 = join(back_0[3], gh_chips, y_swap_0)
    gh_got = plane.exchange(gh_chips)
    totals_s.append([summed(totals[1][0])])
    grad_q_0, dkv_0 = attention_back(0, grad_mixed)
    y_swap_0, grad_q_0 = join(y_swap_0, grad_q_0)
    grad_q_0, dkv_0, gh_got, y_chips_0, y_swap_1, totals_s[0], totals_s[1][0] = join(
        grad_q_0,
        dkv_0,
        gh_got,
        sums(split(y_own_0), split(y_swap_0), order),
        plane.swap(y_sib_1),
        totals_s[0],
        totals_s[1][0],
    )
    back_1 = back_of(1, gh_got)
    grad_x_mid, grad_branch, gain_parts, _ = zip(back_0, back_1)
    gain_mid = sum(g[0] for g in gain_parts)
    gain_high = gain_mid.astype(BF16)
    gain_mid = jnp.stack([gain_high, (gain_mid - gain_high.astype(F32)).astype(BF16)], axis=1)
    gain_mid = jnp.pad(gain_mid, ((0, 0), (2 * kv_width, 126)))
    soon, late = lags[:1], lags[-1:]
    grad_mixed, out_bands, held = join(
        back_1[3], weights_of(grad_branch, attn), returned(dkv_0, soon)
    )
    held_0 = dict(zip(soon, held))
    (grad_q_1, dkv_1), held, y_got_0, y_swap_1, gain_mid, out_swap = join(
        attention_back(1, grad_mixed),
        returned(dkv_0, between),
        plane.exchange(y_chips_0),
        y_swap_1,
        gain_mid,
        plane.swap(out_bands[1]),
    )
    held_0.update(zip(between, held))
    grad_q = [grad_q_0, grad_q_1]

    held, q_bands, y_chips_1, gain_mid, out_chips = join(
        returned(dkv_1, ends),
        weights_of(h_in, grad_q),
        sums(split(y_own_1), split(y_swap_1), order),
        gain_mid,
        sums(out_bands[0], out_swap, same),
    )
    held_1 = dict(zip(ends, held))
    out_got = plane.exchange(out_chips)
    held, held_late, q_chips, out_got, last_half = join(
        returned(dkv_1, between),
        returned(dkv_0, late),
        sums(q_bands[0], plane.swap(q_bands[1]), same),
        out_got,
        totals[1][1],
    )
    held_1.update(zip(between, held))
    held_0.update(zip(late, held_late))
    totals_s[1].append(summed(last_half))
    total_0 = added(dkv_0[-1].astype(F32), [held_0[d] for d in lags])
    total_1 = added(dkv_1[-1].astype(F32), [held_1[d] for d in lags])
    blank = jnp.zeros((rows, 128), F32)
    grad_kv = [
        jnp.concatenate([t[0], t[1], blank], axis=1).astype(BF16) for t in (total_0, total_1)
    ]
    kv_bands = weights_of(h_in, grad_kv, gain_mid)
    q_got = plane.exchange(q_chips)
    kv_swap, out_got = join(plane.swap(kv_bands[1]), out_got)
    kv_chips = sums(kv_bands[0], kv_swap, order)
    kv_own = [kv_chips[k] for k in range(plane.chips)]
    out_total, out_pieces = band_totals([[out_got]], dp_index)

    def over_dp_links(pieces):
        return [dp_cross(x, z, n_dp) for z, x in zip(lags, pieces)]

    kv_sent, q_got, grad_kv, totals_s, y_chips_1, out_sent = join(
        [plane.cross(kv_own[k], k) for k in every],
        q_got,
        grad_kv,
        totals_s,
        y_chips_1,
        over_dp_links(out_pieces),
    )
    grad_x = [
        input_back(grad_q[m], grad_kv[m], x_in[m], grad_x_mid[m], gains, weight) for m in micros
    ]
    y_got_1 = plane.exchange(y_chips_1)
    grad_gu_s, grad_down_s = unpack(totals_s, w_gate_up.shape, w_down.shape)
    total, pieces = band_totals([[q_got], [kv_own[0], *kv_sent]], dp_index)
    sent, y_got_1, grad_gu_s, grad_down_s, grad_x = join(
        over_dp_links(pieces), y_got_1, grad_gu_s, grad_down_s, grad_x
    )
    out_total, total = added(out_total, out_sent), added(total, sent)

    qkv_width = w_qkv.shape[1]
    grad_wqkv = total[:, :qkv_width]
    gain_in = jnp.sum(w_qkv.astype(F32) * grad_wqkv, axis=1) / norm_gains[0].astype(F32)
    x_out = [
        x_mid[m] + jnp.sum(y.astype(F32), axis=0) for m, y in enumerate((y_got_0, y_got_1))
    ]
    return (
        jnp.stack([x.astype(BF16) for x in x_out])[:, None],
        jnp.stack(grad_x)[:, None],
        jnp.stack([gain_in, total[:, qkv_width] + total[:, qkv_width + 1]]),
        grad_wqkv,
        out_total.T,
        grad_gu_s,
        grad_down_s,
    )


def solution(mesh):
    tokens_spec = P(None, "expert", "dp", None)
    experts_spec = P("expert", "dp", None)
    rows_spec = P(("dp", "expert"), None)
    columns_spec = P(None, ("dp", "expert"))
    return jax.shard_map(
        functools.partial(body, mesh.shape["dp"], mesh.shape["expert"]),
        mesh=mesh,
        in_specs=(
            tokens_spec,
            tokens_spec,
            P(None, "expert", None),
            P(None, "expert", None),
            tokens_spec,
            tokens_spec,
            columns_spec,
            rows_spec,
            columns_spec,
            experts_spec,
            experts_spec,
        ),
        out_specs=(
            tokens_spec,
            tokens_spec,
            columns_spec,
            rows_spec,
            columns_spec,
            experts_spec,
            experts_spec,
        ),
        check_vma=False,
    )
```

```python
import functools

import jax
import jax.numpy as jnp
from jax import lax
from jax.experimental import pallas as pl
from jax.experimental.pallas import tpu as pltpu
from jax.sharding import PartitionSpec as P

H = 24
KV = 8
HD = 64
FFE = 512
BLOCK = 128
PAIRS = KV // 2
GROUP = H // KV
PAIR_Q = 2 * GROUP * HD
PAIR_K = 2 * HD

EPSILON = 1e-06
NEGATIVE = -1e30
F32 = jnp.float32
BF16 = jnp.bfloat16


def mm(a, b):
    return jnp.dot(a, b, preferred_element_type=F32)


def mm_nt(a, b):
    return lax.dot_general(a, b, (((1,), (1,)), ((), ())), preferred_element_type=F32)


def mm_tn(a, b):
    return lax.dot_general(a, b, (((0,), (0,)), ((), ())), preferred_element_type=F32)


def rms_norm(values_in, gain):
    return (
        values_in
        * lax.rsqrt(jnp.mean(values_in * values_in, axis=-1, keepdims=True) + EPSILON)
        * gain
    )


def rms_back(values, gain, grad):
    inv = lax.rsqrt(jnp.mean(values * values, axis=-1, keepdims=True) + EPSILON)
    unit = values * inv
    scaled = grad * gain
    grad_values = inv * (scaled - unit * jnp.mean(scaled * unit, axis=-1, keepdims=True))
    return grad_values, jnp.sum(grad * unit, axis=0)


def padded_rows(rows, half):
    blank = jnp.zeros_like(rows)
    return jnp.concatenate([rows, blank] if half == 0 else [blank, rows], axis=0)


def attend_kernel(chunks, q_ref, *refs):
    k_refs, v_refs = refs[:chunks], refs[chunks : 2 * chunks]
    bias_ref, o_ref, lse_ref, s_scr, p_scr = refs[2 * chunks :]
    rows = q_ref.shape[0]
    keys = k_refs[0].shape[0]
    q_t = q_ref[...].T * jnp.asarray(HD**-0.5, BF16)
    v_t = [v[...].T for v in v_refs]
    outs, totals = [], []
    for head in range(2 * GROUP):
        half = head // GROUP
        slot = head % 2
        q_pad = padded_rows(q_t[head * HD : (head + 1) * HD], half)
        peak = None
        for c in range(chunks):
            part = slice(c * keys, (c + 1) * keys)
            scores = mm(k_refs[c][...], q_pad) + bias_ref[part, :]
            s_scr[slot, part, :] = scores
            top = jnp.max(scores, axis=0, keepdims=True)
            peak = top if peak is None else jnp.maximum(peak, top)
        total = jnp.zeros((1, rows), F32)
        mixed = jnp.zeros((HD, rows), F32)
        for c in range(chunks):
            part = slice(c * keys, (c + 1) * keys)
            prob = jnp.exp(s_scr[slot, part, :] - peak)
            total = total + jnp.sum(prob, axis=0, keepdims=True)
            p_scr[slot, part, :] = prob.astype(BF16)
        for c in range(chunks):
            part = slice(c * keys, (c + 1) * keys)
            mixed = mixed + mm(v_t[c][half * HD : (half + 1) * HD], p_scr[slot, part, :])
        outs.append(mixed / total)
        totals.append(peak + jnp.log(total))
    o_ref[...] = jnp.concatenate(outs, axis=0).T.astype(BF16)
    blank = jnp.zeros((8 - 2 * GROUP, rows), F32)
    lse_ref[0] = jnp.concatenate(totals + [blank], axis=0)


def kv_specs(chunks, keys):
    k_spec = pl.BlockSpec((keys, PAIR_K), lambda j: (0, j))
    v_spec = pl.BlockSpec((keys, PAIR_K), lambda j: (0, PAIRS + j))
    return [k_spec] * chunks + [v_spec] * chunks


def attend(queries, kv_chunks, bias):
    rows, width = queries.shape
    chunks, keys = len(kv_chunks), kv_chunks[0].shape[0]
    work = 4 * H * rows * chunks * keys * HD
    q_spec = pl.BlockSpec((rows, PAIR_Q), lambda j: (0, j))
    return pl.pallas_call(
        functools.partial(attend_kernel, chunks),
        grid=(PAIRS,),
        in_specs=[q_spec]
        + kv_specs(chunks, keys)
        + [pl.BlockSpec((chunks * keys, rows), lambda j: (0, 0))],
        out_specs=[q_spec, pl.BlockSpec((1, 8, rows), lambda j: (j, 0, 0))],
        out_shape=[
            jax.ShapeDtypeStruct(queries.shape, BF16),
            jax.ShapeDtypeStruct((PAIRS, 8, rows), F32),
        ],
        scratch_shapes=[
            pltpu.VMEM((2, chunks * keys, rows), F32),
            pltpu.VMEM((2, chunks * keys, rows), BF16),
        ],
        compiler_params=pltpu.CompilerParams(vmem_limit_bytes=60 * 1024 * 1024),
        cost_estimate=pl.CostEstimate(
            flops=work // 64, bytes_accessed=1024 * 1024, transcendentals=0
        ),
        name="path_attention",
    )(queries, *kv_chunks, *kv_chunks, bias)


def attend_back_kernel(chunks, q_ref, g_ref, *refs):
    k_refs, v_refs = refs[:chunks], refs[chunks : 2 * chunks]
    bias_ref, lse_ref, dq_ref = refs[2 * chunks : 2 * chunks + 3]
    out_refs = refs[2 * chunks + 3 : 3 * chunks + 3]
    p_scr, gp_scr, ps_scr, ds_scr = refs[3 * chunks + 3 :]
    rows = q_ref.shape[0]
    keys = k_refs[0].shape[0]
    q_t = q_ref[...].T * jnp.asarray(HD**-0.5, BF16)
    g_t = g_ref[...].T
    k_t = [k[...].T for k in k_refs]
    dqs, q_pads, g_pads = [], [], []
    for head in range(2 * GROUP):
        half = head // GROUP
        slot = head % 2
        here = slice(head * rows, (head + 1) * rows)
        q_pad = padded_rows(q_t[head * HD : (head + 1) * HD], half)
        g_pad = padded_rows(g_t[head * HD : (head + 1) * HD], half)
        q_pads.append(q_pad)
        g_pads.append(g_pad)
        lse = lse_ref[0, head : head + 1, :]
        delta = jnp.zeros((1, rows), F32)
        for c in range(chunks):
            part = slice(c * keys, (c + 1) * keys)
            prob = jnp.exp(mm(k_refs[c][...], q_pad) + bias_ref[part, :] - lse)
            grad_prob = mm(v_refs[c][...], g_pad)
            delta = delta + jnp.sum(prob * grad_prob, axis=0, keepdims=True)
            p_scr[slot, part, :] = prob
            gp_scr[slot, part, :] = grad_prob
            ps_scr[part, here] = prob.astype(BF16)
        dq = jnp.zeros((HD, rows), F32)
        for c in range(chunks):
            part = slice(c * keys, (c + 1) * keys)
            ds = (p_scr[slot, part, :] * (gp_scr[slot, part, :] - delta)).astype(BF16)
            ds_scr[part, here] = ds
            dq = dq + mm(k_t[c][half * HD : (half + 1) * HD], ds)
        dqs.append(dq * HD**-0.5)
    dq_ref[...] = jnp.concatenate(dqs, axis=0).T.astype(BF16)
    q_all = jnp.concatenate(q_pads, axis=1)
    g_all = jnp.concatenate(g_pads, axis=1)
    for c in range(chunks):
        part = slice(c * keys, (c + 1) * keys)
        out_refs[c][0] = mm_nt(ds_scr[part, :], q_all).astype(BF16)
        out_refs[c][1] = mm_nt(ps_scr[part, :], g_all).astype(BF16)


def attend_back(queries, grad_mixed, kv_chunks, bias, lse):
    rows, width = queries.shape
    chunks, keys = len(kv_chunks), kv_chunks[0].shape[0]
    work = 10 * H * rows * chunks * keys * HD
    q_spec = pl.BlockSpec((rows, PAIR_Q), lambda j: (0, j))
    return pl.pallas_call(
        functools.partial(attend_back_kernel, chunks),
        grid=(PAIRS,),
        in_specs=[q_spec, q_spec]
        + kv_specs(chunks, keys)
        + [
            pl.BlockSpec((chunks * keys, rows), lambda j: (0, 0)),
            pl.BlockSpec((1, 8, rows), lambda j: (j, 0, 0)),
        ],
        out_specs=[q_spec] + [pl.BlockSpec((2, keys, PAIR_K), lambda j: (0, 0, j))] * chunks,
        out_shape=[jax.ShapeDtypeStruct(queries.shape, BF16)]
        + [jax.ShapeDtypeStruct((2, keys, KV * HD), BF16)] * chunks,
        scratch_shapes=[
            pltpu.VMEM((2, chunks * keys, rows), F32),
            pltpu.VMEM((2, chunks * keys, rows), F32),
            pltpu.VMEM((chunks * keys, 2 * GROUP * rows), BF16),
            pltpu.VMEM((chunks * keys, 2 * GROUP * rows), BF16),
        ],
        compiler_params=pltpu.CompilerParams(vmem_limit_bytes=60 * 1024 * 1024),
        cost_estimate=pl.CostEstimate(
            flops=work // 64, bytes_accessed=1024 * 1024, transcendentals=0
        ),
        name="path_attention_back",
    )(queries, grad_mixed, *kv_chunks, *kv_chunks, bias, lse)


def ancestry(parents_in):
    count = parents_in.shape[-1]
    labels = jnp.arange(count, dtype=jnp.int32)
    reach = (parents_in[..., :, None] == labels) | (labels[:, None] == labels)
    steps = 1
    while steps < count:
        reach = jnp.any(reach[..., :, :, None] & reach[..., None, :, :], axis=-2)
        steps *= 2
    return reach


def mask_bias(parents, valid, dp_index, n_dp, rows):
    micro = parents.shape[0]
    per = rows // BLOCK
    reach = lax.dynamic_slice_in_dim(ancestry(parents), dp_index * per, per, 1)
    early = (n_dp - 1) * per
    reach = jnp.pad(reach, ((0, 0), (0, 0), (early, 0)))
    reach = lax.dynamic_slice_in_dim(reach, dp_index * per, n_dp * per, 2)
    ok = jnp.pad(valid > 0, ((0, 0), (early * BLOCK, 0)))
    ok = lax.dynamic_slice_in_dim(ok, dp_index * rows, n_dp * rows, 1)
    by_key = jnp.repeat(jnp.swapaxes(reach, 1, 2), BLOCK, axis=1)
    shape = (micro, n_dp * rows, rows)
    key = lax.broadcasted_iota(jnp.int32, shape, 1) - (n_dp - 1) * rows
    query = lax.broadcasted_iota(jnp.int32, shape, 2)
    onpath = jnp.zeros(shape, bool)
    for i in range(per):
        onpath = onpath | ((query // BLOCK == i) & by_key[:, :, i : i + 1])
    allowed = onpath & (key <= query) & (ok[:, :, None] | (key == query))
    return jnp.where(allowed, 0.0, NEGATIVE).astype(F32)


def expert_kernel(block, chips, shards, has_prev, has_acc, last, *refs):
    refs = list(refs)

    def take(n):
        out = refs[:n]
        del refs[:n]
        return out

    h_refs, c_refs = take(2 * chips), take(2)
    order_ref, gate_ref, w_ref = take(3)
    prev = take(4) if has_prev else None
    acc_in = take(2) if has_acc else None
    y_sib, y_own, gh_sib, gh_own = take(4)
    grad_refs = take(2)
    hb, cb, yb, gb, acc_gu, acc_d, wg_ref, wu_ref, wd_ref, sem_in, sem_out, sem_acc, sem_w = take(13)
    if has_prev:
        yp, gp, sem_prev = take(3)
    lead = h_refs[0].shape[0]
    per = block // lead
    half = chips // per
    steps = 2 * half

    def fetch(i, slot):
        for j in range(steps):

            @pl.when(i == j)
            def _():
                for r in range(per):
                    at = j * per + r
                    rows = pl.ds(r * lead, lead)
                    pltpu.make_async_copy(
                        h_refs[at], hb.at[slot, rows], sem_in.at[0, slot]
                    ).start()
                    pltpu.make_async_copy(
                        c_refs[at // chips].at[order_ref[at % chips]],
                        cb.at[slot, rows],
                        sem_in.at[1, slot],
                    ).start()
                if has_prev:
                    rows = pl.ds((j % half) * block, block)
                    for n, buffer in enumerate((yp, gp)):
                        pltpu.make_async_copy(
                            prev[2 * n + j // half].at[rows], buffer.at[slot], sem_prev.at[n, slot]
                        ).start()

    def fetched(slot):
        for n, buffer in enumerate((hb, cb)):
            pltpu.make_async_copy(buffer.at[slot], buffer.at[slot], sem_in.at[n, slot]).wait()
        if has_prev:
            for n, buffer in enumerate((yp, gp)):
                pltpu.make_async_copy(
                    buffer.at[slot], buffer.at[slot], sem_prev.at[n, slot]
                ).wait()

    def copies_out(y_ref, g_ref, at, slot):
        rows = pl.ds(pl.multiple_of(at * block, block), block)
        return (
            pltpu.make_async_copy(yb.at[slot], y_ref.at[rows], sem_out.at[0, slot]),
            pltpu.make_async_copy(gb.at[slot], g_ref.at[rows], sem_out.at[1, slot]),
        )

    def stored(slot):
        for copy in copies_out(y_own, gh_own, 0, slot):
            copy.wait()

    hidden, width = acc_d.shape
    tiles = width // hidden
    band = hidden // shards
    weight_copies = [
        pltpu.make_async_copy(w_ref.at[:, pl.ds(0, hidden)], wg_ref, sem_w.at[0]),
        pltpu.make_async_copy(w_ref.at[:, pl.ds(hidden, hidden)], wu_ref, sem_w.at[1]),
    ]
    for z in range(shards):
        for j in range(tiles):
            copy = pltpu.make_async_copy(
                w_ref.at[pl.ds((z * tiles + j) * band, band), pl.ds(2 * hidden, hidden)],
                wd_ref.at[pl.ds(z * band, band), pl.ds(j * hidden, hidden)],
                sem_w.at[2 + z * tiles + j],
            )
            weight_copies.append(copy)
    for copy in weight_copies:
        copy.start()
    fetch(0, 0)
    if has_acc:
        acc_copies = [
            pltpu.make_async_copy(acc_in[0], acc_gu, sem_acc.at[0]),
            pltpu.make_async_copy(acc_in[1], acc_d, sem_acc.at[1]),
        ]
        for copy in acc_copies:
            copy.start()
    else:
        acc_gu[...] = jnp.zeros_like(acc_gu)
        acc_d[...] = jnp.zeros_like(acc_d)

    for copy in weight_copies:
        copy.wait()

    def step(i, carry):
        slot = lax.rem(i, 2)

        @pl.when(i + 1 < steps)
        def _():
            fetch(i + 1, 1 - slot)

        fetched(slot)

        @pl.when(i >= 2)
        def _():
            stored(slot)

        tokens = hb[slot]
        grads = cb[slot]
        scale = jnp.broadcast_to(gate_ref[i], (8, block)).T[:, :1]
        gate = mm(tokens, wg_ref[...])
        up = mm(tokens, wu_ref[...])
        grad_act = mm_nt(grads, wd_ref[...]) * scale
        sig = jax.nn.sigmoid(gate)
        silu = gate * sig
        act = (silu * up * scale).astype(BF16)
        grad_gate = (grad_act * up * (sig + silu * (1.0 - sig))).astype(BF16)
        grad_up = (grad_act * silu).astype(BF16)
        y = mm(act, wd_ref[...])
        gh = mm_nt(grad_gate, wg_ref[...]) + mm_nt(grad_up, wu_ref[...])
        if has_prev:
            y = y + yp[slot].astype(F32)
            gh = gh + gp[slot].astype(F32)
        yb[slot] = y.astype(BF16)
        gb[slot] = gh.astype(BF16)

        @pl.when(i < half)
        def _():
            for copy in copies_out(y_sib, gh_sib, i, slot):
                copy.start()

        @pl.when(i >= half)
        def _():
            for copy in copies_out(y_own, gh_own, i - half, slot):
                copy.start()

        if has_acc:

            @pl.when(i == 0)
            def _():
                for copy in acc_copies:
                    copy.wait()

        acc_d[...] += mm_tn(act, grads)
        acc_gu[:, :FFE] += mm_tn(tokens, grad_gate)
        acc_gu[:, FFE:] += mm_tn(tokens, grad_up)
        return carry

    lax.fori_loop(0, steps, step, 0)
    stored(steps % 2)
    stored((steps - 1) % 2)
    if last:
        cut = grad_refs[0].shape[1]
        grad_refs[0][...] = acc_gu[:, :cut].astype(BF16)
        grad_refs[1][:, : 2 * hidden - cut] = acc_gu[:, cut:].astype(BF16)
        for z in range(shards):
            for j in range(tiles):
                rows = slice((z * tiles + j) * band, (z * tiles + j + 1) * band)
                piece = acc_d[z * band : (z + 1) * band, j * hidden : (j + 1) * hidden]
                grad_refs[1][rows, 2 * hidden - cut :] = piece.astype(BF16)
    else:
        out = [
            pltpu.make_async_copy(acc_gu, grad_refs[0], sem_acc.at[0]),
            pltpu.make_async_copy(acc_d, grad_refs[1], sem_acc.at[1]),
        ]
        for copy in out:
            copy.start()
        for copy in out:
            copy.wait()


def expert_pass(h_all, c_all, order, gates, weight, shards, previous, totals, last, block=512):
    chips = len(h_all) // 2
    lead, width = h_all[0].shape
    rows = chips * lead
    hidden = weight.shape[1] // 3
    far = pl.BlockSpec(memory_space=pl.ANY)
    near = pl.BlockSpec(memory_space=pltpu.VMEM)
    scalars = pl.BlockSpec(memory_space=pltpu.SMEM)
    token_out = jax.ShapeDtypeStruct((rows, width), BF16)
    token_buffer = pltpu.VMEM((2, block, width), BF16)
    if last:
        first = 3 * hidden // 2
        grads = [((width, first), BF16), ((width, 3 * hidden - first), BF16)]
    else:
        grads = [((width, 2 * hidden), F32), ((hidden, width), F32)]
    scratch = [token_buffer] * 4 + [
        pltpu.VMEM((width, 2 * hidden), F32),
        pltpu.VMEM((hidden, width), F32),
        pltpu.VMEM((width, hidden), BF16),
        pltpu.VMEM((width, hidden), BF16),
        pltpu.VMEM((hidden, width), BF16),
        pltpu.SemaphoreType.DMA((2, 2)),
        pltpu.SemaphoreType.DMA((2, 2)),
        pltpu.SemaphoreType.DMA((2,)),
        pltpu.SemaphoreType.DMA((2 + shards * (width // hidden),)),
    ]
    extra, aliases = [], {}
    if previous is not None:
        scratch += [token_buffer] * 2 + [pltpu.SemaphoreType.DMA((2, 2))]
        aliases = {2 * chips + 5 + n: n for n in range(4)}
        extra += list(previous)
    if totals is not None:
        extra += list(totals)
    return pl.pallas_call(
        functools.partial(
            expert_kernel, block, chips, shards, previous is not None, totals is not None, last
        ),
        in_specs=[far] * (2 * chips + 2) + [scalars, near, far] + [far] * len(extra),
        out_specs=[far] * 4 + [near if last else far] * len(grads),
        out_shape=[token_out] * 4 + [jax.ShapeDtypeStruct(*g) for g in grads],
        scratch_shapes=scratch,
        input_output_aliases=aliases,
        compiler_params=pltpu.CompilerParams(vmem_limit_bytes=60 * 1024 * 1024),
        cost_estimate=pl.CostEstimate(
            flops=rows * width, bytes_accessed=rows * width, transcendentals=0
        ),
        name="expert_pass",
    )(*h_all, *c_all, order, gates, weight, *extra)


SMALL = pl.CostEstimate(flops=1024, bytes_accessed=1024, transcendentals=0)
FAR = pl.BlockSpec(memory_space=pl.ANY)
NEAR = pl.BlockSpec(memory_space=pltpu.VMEM)
SCALARS = pl.BlockSpec(memory_space=pltpu.SMEM)


def small_call(kernel, name, inputs, outs, in_specs=None, scratch=()):
    return pl.pallas_call(
        kernel,
        in_specs=in_specs or [NEAR] * len(inputs),
        out_specs=[NEAR] * len(outs),
        out_shape=[jax.ShapeDtypeStruct(shape, dtype) for shape, dtype in outs],
        scratch_shapes=list(scratch),
        compiler_params=pltpu.CompilerParams(vmem_limit_bytes=48 * 1024 * 1024),
        cost_estimate=SMALL,
        name=name,
    )(*inputs)


def repeat_kernel(x_ref, out_ref):
    out_ref[...] = jnp.broadcast_to(x_ref[...][None], out_ref.shape)


def repeat(x, count):
    return small_call(repeat_kernel, "repeat", [x], [((count,) + x.shape, x.dtype)])[0]


def assemble_kernel(counts, chunk, place_ref, *refs):
    out_ref, sem = refs[len(counts) :]
    copies, n = [], 0
    for ref, count in zip(refs, counts):
        for at in range(count):
            rows = pl.ds(pl.multiple_of(place_ref[n] * chunk, chunk), chunk)
            copies.append(pltpu.make_async_copy(ref.at[at], out_ref.at[rows], sem))
            n += 1
    for copy in copies:
        copy.start()
    for copy in copies:
        copy.wait()


def assemble(blocks, places):
    chunk, width = blocks[0].shape[1:]
    counts = [x.shape[0] for x in blocks]
    rows = sum(counts) * chunk
    if chunk % 16:
        bands = jnp.concatenate(blocks, axis=0)
        whole = jnp.zeros_like(bands).at[places].set(bands)
        return whole.reshape(rows, width)
    return pl.pallas_call(
        functools.partial(assemble_kernel, counts, chunk),
        in_specs=[SCALARS] + [FAR] * len(blocks),
        out_specs=NEAR,
        out_shape=jax.ShapeDtypeStruct((rows, width), BF16),
        scratch_shapes=[pltpu.SemaphoreType.DMA],
        compiler_params=pltpu.CompilerParams(vmem_limit_bytes=32 * 1024 * 1024),
        cost_estimate=SMALL,
        name="assemble",
    )(places, *blocks)


def project_kernel(micro, counts, chunk, place_ref, *refs):
    refs = list(refs)

    def take(n):
        out = refs[:n]
        del refs[:n]
        return out

    x_refs, blocks = take(micro), take(len(counts))
    h_refs, kv_refs = take(micro), take(micro)
    gains_ref, whole_ref, w_ref, sem_in, sem_out = refs
    copies, n = [], 0
    for ref, count in zip(blocks, counts):
        for at in range(count):
            rows = pl.ds(pl.multiple_of(place_ref[n] * chunk, chunk), chunk)
            copies.append(pltpu.make_async_copy(ref.at[at], w_ref.at[rows], sem_in))
            n += 1
    for copy in copies:
        copy.start()
    for copy in copies:
        copy.wait()
    out = pltpu.make_async_copy(w_ref, whole_ref, sem_out)
    out.start()
    kv_from = w_ref.shape[1] - 128 - kv_refs[0].shape[1]
    gains = w_ref[:, -128:].astype(F32).T
    gains_ref[...] = gains[:8]
    for x_ref, h_ref, kv_ref in zip(x_refs, h_refs, kv_refs):
        h = rms_norm(x_ref[...].astype(F32), gains[:1]).astype(BF16)
        h_ref[...] = h
        kv_ref[...] = mm(h, w_ref[:, kv_from:-128]).astype(BF16)
    out.wait()


def project(xs, blocks, places, kv_width):
    micro, (rows, width) = len(xs), xs[0].shape
    if blocks[0].shape[1] % 16:
        blocks, places = [assemble(blocks, places)[None]], jnp.zeros((1,), jnp.int32)
    chunk, columns = blocks[0].shape[1:]
    counts = [x.shape[0] for x in blocks]
    weight = (sum(counts) * chunk, columns)
    outs = (
        [((rows, width), BF16)] * micro
        + [((rows, kv_width), BF16)] * micro
        + [((8, width), F32), (weight, BF16)]
    )
    got = pl.pallas_call(
        functools.partial(project_kernel, micro, counts, chunk),
        in_specs=[SCALARS] + [NEAR] * micro + [FAR] * len(blocks),
        out_specs=[NEAR] * (2 * micro + 1) + [FAR],
        out_shape=[jax.ShapeDtypeStruct(shape, dtype) for shape, dtype in outs],
        scratch_shapes=[
            pltpu.VMEM(weight, BF16),
            pltpu.SemaphoreType.DMA,
            pltpu.SemaphoreType.DMA,
        ],
        compiler_params=pltpu.CompilerParams(vmem_limit_bytes=48 * 1024 * 1024),
        cost_estimate=SMALL,
        name="project",
    )(places, *xs, *blocks)
    return list(got[:micro]), list(got[micro : 2 * micro]), got[-2], got[-1]


def middle_kernel(attn_ref, x_ref, gains_ref, w_ref, mid_ref, h_ref):
    mid = x_ref[...].astype(F32) + mm_nt(attn_ref[...], w_ref[...])
    mid_ref[...] = mid
    h_ref[...] = rms_norm(mid, gains_ref[1:2]).astype(BF16)


def middle(attn, x, gains, w_out_t):
    return small_call(
        middle_kernel,
        "middle",
        [attn, x, gains, w_out_t],
        [(x.shape, F32), (x.shape, BF16)],
    )


def middle_back_kernel(got_ref, mid_ref, c_ref, gains_ref, w_ref, gx_ref, branch_ref, gain_ref, mixed_ref):
    grad = got_ref[0].astype(F32)
    for k in range(1, got_ref.shape[0]):
        grad = grad + got_ref[k].astype(F32)
    part, gain_part = rms_back(mid_ref[...], gains_ref[1:2], grad)
    grad_x = c_ref[...].astype(F32) + part
    branch = grad_x.astype(BF16)
    gx_ref[...] = grad_x
    branch_ref[...] = branch
    gain_ref[...] = jnp.broadcast_to(gain_part[None], gain_ref.shape)
    mixed_ref[...] = mm(branch, w_ref[...]).astype(BF16)


def middle_back(got, mid, c, gains, w_out_t):
    return small_call(
        middle_back_kernel,
        "middle_back",
        [got, mid, c, gains, w_out_t],
        [(c.shape, F32), (c.shape, BF16), ((8, c.shape[1]), F32), (c.shape, BF16)],
    )


def input_back_kernel(q_ref, kv_ref, x_ref, mid_ref, gains_ref, w_ref, grad_ref):
    query_width = q_ref.shape[1]
    cut = w_ref.shape[1] - 128
    grad_h = mm_nt(q_ref[...], w_ref[:, :query_width])
    grad_h = grad_h + mm_nt(kv_ref[:, : cut - query_width], w_ref[:, query_width:cut])
    part, _ = rms_back(x_ref[...].astype(F32), gains_ref[:1], grad_h)
    grad_ref[...] = (mid_ref[...] + part).astype(BF16)


def input_back(grad_q, grad_kv, x, grad_x_mid, gains, weight):
    return small_call(
        input_back_kernel,
        "input_back",
        [grad_q, grad_kv, x, grad_x_mid, gains, weight],
        [(x.shape, BF16)],
    )[0]


def unpack_kernel(*refs):
    up_ref, down_ref = refs[-2:]
    for e in range(up_ref.shape[0]):
        first, second = refs[2 * e][...], refs[2 * e + 1][...]
        cut = up_ref.shape[2] - first.shape[1]
        up_ref[e] = jnp.concatenate([first, second[:, :cut]], axis=1).astype(F32)
        pieces = second[:, cut:].astype(F32)
        rows, wide = down_ref.shape[1], pieces.shape[1]
        for j in range(down_ref.shape[2] // wide):
            down_ref[e, :, j * wide : (j + 1) * wide] = pieces[j * rows : (j + 1) * rows]


def unpack(totals, up_shape, down_shape):
    flat = [t for pair in totals for t in pair]
    return small_call(unpack_kernel, "unpack", flat, [(up_shape, F32), (down_shape, F32)])


def band_totals_kernel(counts, dp_ref, *refs):
    refs = list(refs)
    groups = []
    for count in counts:
        groups.append(refs[:count])
        del refs[:count]
    own_ref, piece_refs = refs[0], refs[1:]

    def total(ref):
        held = ref[0].astype(F32)
        for k in range(1, ref.shape[0]):
            held = held + ref[k].astype(F32)
        return held

    columns = []
    for group in groups:
        if len(group) == 1 and len(group[0].shape) == 4:
            columns.append(total(group[0]))
        else:
            columns.append(functools.reduce(jnp.add, [ref[...].astype(F32) for ref in group]))
    whole = jnp.concatenate(columns, axis=-1)
    dp_index = dp_ref[0]
    for z in range(whole.shape[0]):

        @pl.when(dp_index == z)
        def _():
            own_ref[...] = whole[z]

        for k, ref in enumerate(piece_refs):

            @pl.when((dp_index ^ (k + 1)) == z)
            def _():
                ref[...] = whole[z].astype(BF16)


def band_totals(groups, dp_index):
    n_dp, chunk = groups[0][0].shape[-3:-1]
    width = sum(group[0].shape[-1] for group in groups)
    inputs = [dp_index.reshape(1)] + [x for group in groups for x in group]
    own, *pieces = small_call(
        functools.partial(band_totals_kernel, [len(group) for group in groups]),
        "band_totals",
        inputs,
        [((chunk, width), F32)] + [((chunk, width), BF16)] * (n_dp - 1),
        in_specs=[SCALARS] + [NEAR] * (len(inputs) - 1),
    )
    return own, pieces


def sums_kernel(order_ref, own_ref, other_ref, out_ref):
    out_ref[...] = (own_ref[...].astype(F32) + other_ref[...].astype(F32)).astype(BF16)


def sums(own, other, order):
    blank = (0,) * (own.ndim - 1)
    block = (1,) + own.shape[1:]
    spec = pl.BlockSpec(block, lambda i, order: (i,) + blank)
    return pl.pallas_call(
        sums_kernel,
        grid_spec=pltpu.PrefetchScalarGridSpec(
            num_scalar_prefetch=1,
            grid=(own.shape[0],),
            in_specs=[spec, spec],
            out_specs=pl.BlockSpec(block, lambda i, order: (order[i],) + blank),
        ),
        out_shape=jax.ShapeDtypeStruct(own.shape, BF16),
        compiler_params=pltpu.CompilerParams(vmem_limit_bytes=32 * 1024 * 1024),
        cost_estimate=SMALL,
        name="sums",
    )(order, own, other)


def weight_grad_kernel(parts, chunk, n_dp, has_extra, core_ref, *refs):
    left, right = refs[:parts], refs[parts : 2 * parts]
    own_ref, other_ref = refs[-2:]
    total = mm_tn(left[0][...], right[0][...])
    for a, b in zip(left[1:], right[1:]):
        total = total + mm_tn(a[...], b[...])
    if has_extra:
        total = total + refs[2 * parts][...].astype(F32)
    total = total.astype(BF16)
    chips = total.shape[0] // (2 * chunk * n_dp)
    pairs = total.reshape(n_dp, chips, 2, chunk, total.shape[1])
    first = core_ref[0] == 0
    for z in range(n_dp):
        for j in range(chips):
            own_ref[j, z] = jnp.where(first, pairs[z, j, 0], pairs[z, j, 1])
            other_ref[j, z] = jnp.where(first, pairs[z, j, 1], pairs[z, j, 0])


def weight_grad(left, right, n_dp, chips, core, extra=None):
    width, columns = left[0].shape[1], right[0].shape[1]
    chunk = width // (2 * n_dp * chips)
    if chunk % 16:
        total = sum(mm_tn(a, b) for a, b in zip(left, right))
        if extra is not None:
            total = total + extra.astype(F32)
        total = total.astype(BF16)
        pairs = total.reshape(n_dp, chips, 2, chunk, columns)
        return [
            jnp.swapaxes(lax.dynamic_index_in_dim(pairs, c, 2, keepdims=False), 0, 1)
            for c in (core, 1 - core)
        ]
    parts, tokens = len(left), left[0].shape[0]
    block = 512 if columns % 512 == 0 else 384
    shape = (chips, n_dp, chunk)
    extras = [] if extra is None else [extra]
    band = jax.ShapeDtypeStruct(shape + (columns,), BF16)
    band_spec = pl.BlockSpec(shape + (block,), lambda j: (0, 0, 0, j))
    return pl.pallas_call(
        functools.partial(weight_grad_kernel, parts, chunk, n_dp, bool(extras)),
        grid=(columns // block,),
        in_specs=[SCALARS]
        + [pl.BlockSpec((tokens, width), lambda j: (0, 0))] * parts
        + [pl.BlockSpec((tokens, block), lambda j: (0, j))] * parts
        + [pl.BlockSpec((width, block), lambda j: (0, j))] * len(extras),
        out_specs=[band_spec, band_spec],
        out_shape=[band, band],
        compiler_params=pltpu.CompilerParams(vmem_limit_bytes=32 * 1024 * 1024),
        cost_estimate=SMALL,
        name="weight_grad",
    )(core.reshape(1).astype(jnp.int32), *left, *right, *extras)


def join(*items):
    return lax.optimization_barrier(items)


class Plane:
    def __init__(self, count):
        self.count = count
        self.chips = count // 2

    def swap(self, x):
        return lax.ppermute(x, "expert", [(i, i ^ 1) for i in range(self.count)])

    def cross(self, x, k):
        return lax.ppermute(x, "expert", [(i, i ^ (2 * k)) for i in range(self.count)])

    def exchange(self, x):
        groups = [[chip * 2 + c for chip in range(self.chips)] for c in range(2)]
        return lax.all_to_all(
            x, "expert", split_axis=0, concat_axis=0, axis_index_groups=groups, tiled=True
        )

    def spread(self, x):
        return self.exchange(jnp.broadcast_to(x[None], (self.chips,) + x.shape))

    def doubled(self, held, n):
        bits = [1 << i for i in range(self.chips.bit_length() - 1)]
        return [
            {**blocks, **{k ^ bit: self.cross(x, bit) for k, x in blocks.items()}}
            for blocks, bit in zip(held, (bits[n], bits[-1 - n]))
        ]

    def crosses(self, x, ks):
        return [self.cross(x, k) for k in ks]


def added(first, others):
    for x in others:
        first = first + x.astype(F32)
    return first


def dp_cross(x, k, n_dp):
    return lax.ppermute(x, "dp", [(i, i ^ k) for i in range(n_dp)])


def dp_along(x, by, n_dp):
    pairs = [(i, i + by) for i in range(n_dp) if 0 <= i + by < n_dp]
    return lax.ppermute(x, "dp", pairs)


def dp_others(x, n_dp):
    return [dp_cross(x, k, n_dp) for k in range(1, n_dp)]


def body(
    n_dp,
    n_expert,
    tokens,
    cotangent,
    parents,
    valid_mask,
    routes,
    route_gates,
    norm_gains,
    w_qkv,
    w_out,
    w_gate_up,
    w_down,
):
    both = ("dp", "expert")
    micro, _, rows, width = tokens.shape
    micros = range(micro)
    count = micro * rows
    top = routes.shape[-1]
    query_width = H * HD
    kv_width = KV * HD
    local_experts = w_gate_up.shape[0]
    experts = local_experts * n_expert
    plane = Plane(n_expert)
    dp_index = lax.axis_index("dp")

    x_in = [tokens[m, 0] for m in micros]
    grad_out = [cotangent[m, 0] for m in micros]
    expert_index = lax.axis_index("expert")
    core, chip = expert_index % 2, expert_index // 2
    every, lags = range(1, plane.chips), range(1, n_dp)
    near, far = every[:-1], every[-1:]

    def over_dp(x):
        return lax.all_gather(x, "dp", axis=0, tiled=True)

    chosen = routes.reshape(count, top)[:, :, None] == jnp.arange(experts, dtype=jnp.int32)
    table = jnp.sum(jnp.where(chosen, route_gates.reshape(count, top)[:, :, None], 0.0), axis=1)
    table = table.T.reshape(n_expert, local_experts, micro, rows)
    table = lax.all_to_all(table, "expert", split_axis=0, concat_axis=0, tiled=True)
    sides = [2 * k + 1 for k in range(plane.chips)] + [2 * k for k in range(plane.chips)]
    table = jnp.take(table, expert_index ^ jnp.array(sides, jnp.int32), axis=0)
    gates = [[table[:, e, m].reshape(-1, 1, 512) for m in micros] for e in range(local_experts)]
    bias = mask_bias(
        parents.reshape(micro, -1), valid_mask.reshape(micro, -1), dp_index, n_dp, rows
    )
    bias = [bias[m] for m in micros]
    same = jnp.arange(plane.chips, dtype=jnp.int32)
    order = chip ^ same

    half = n_dp // 2

    def bands(line, chip_at, core_at):
        return [((dp_index ^ z) * plane.chips + chip_at) * 2 + core_at for z in line]

    def wide(x):
        return jnp.broadcast_to(x[None], (plane.chips,) + x.shape)

    packed = [
        jnp.concatenate(
            [w_gate_up[e], w_down[e].reshape(-1, width // FFE, FFE).swapaxes(0, 1).reshape(-1, FFE)],
            axis=1,
        )
        for e in range(local_experts)
    ]
    gains_t = jnp.pad(norm_gains.T, ((0, 0), (0, 126)))
    own_rows = jnp.concatenate([w_qkv, gains_t], axis=1)
    qkv_line, out_rows, gates, bias, order, w_first = join(
        [own_rows] + dp_others(own_rows, n_dp),
        jnp.broadcast_to(w_out.T[None], (n_dp,) + w_out.shape[::-1]),
        gates,
        bias,
        order,
        packed[0],
    )
    expert_w = [over_dp(w_first)]
    line = jnp.stack(qkv_line)
    held = plane.doubled([{0: line[:half]}, {0: line[half:]}], 0)
    out_line = lax.all_to_all(out_rows, "dp", split_axis=0, concat_axis=0, tiled=True)
    held, line_swap = join(held, plane.swap(line))
    for n in range(1, plane.chips.bit_length() - 1):
        held = plane.doubled(held, n)
    held, out_line, c_wide, w_last = join(
        held, out_line, [repeat(c, plane.chips) for c in grad_out], packed[1]
    )
    moved = [(h, k, held[h][k]) for k in every for h in range(2)]
    out_spread = plane.exchange(wide(out_line))
    swapped = list(join(*[plane.swap(x) for _, _, x in moved]))
    lines = [range(half), range(half, n_dp)]
    places = bands(range(n_dp), chip, core) + bands(range(n_dp), chip, 1 - core)
    for c in (core, 1 - core):
        for h, k, _ in moved:
            places += bands(lines[h], chip ^ k, c)
    blocks = [line, line_swap] + [x for _, _, x in moved] + swapped
    places = jnp.stack(places)

    h_in, kv, gains, weight = project(x_in, blocks, places, 2 * kv_width)
    w_q = weight[:, :query_width]
    queries = [mm(h, w_q).astype(BF16) for h in h_in]

    c_0 = plane.exchange(c_wide[0])
    out_swap = plane.swap(out_spread)
    places = []
    for c in (core, 1 - core):
        for j in range(plane.chips):
            places += [(z * plane.chips + j) * 2 + c for z in range(n_dp)]
    w_out_t = assemble(
        [x.reshape((-1,) + x.shape[2:]) for x in (out_spread, out_swap)], jnp.stack(places)
    )
    chunks_0, kv[1], queries, w_out_t, c_0, expert_w[0] = join(
        [dp_along(kv[0], d, n_dp) for d in reversed(lags)],
        kv[1],
        queries,
        w_out_t,
        c_0,
        expert_w[0],
    )
    kv_chunks = [list(chunks_0) + [kv[0]]]
    ends = [lags[0], lags[-1]]
    between = [d for d in lags if d not in ends]
    (mixed, total), held, c_swap = join(
        attend(queries[0], kv_chunks[0], bias[0]),
        [dp_along(kv[1], d, n_dp) for d in between],
        plane.swap(c_0),
    )
    held_1 = dict(zip(between, held))
    c_1 = plane.exchange(c_wide[1])
    c_all = [[c_swap, c_0]]
    attn, lse = [mixed], [total]
    x, h = middle(attn[0], x_in[0], gains, w_out_t)
    x_mid, h_mid = [x], [h]
    held, h_others, w_last, c_1 = join(
        [dp_along(kv[1], d, n_dp) for d in ends], plane.crosses(h, every), w_last, c_1
    )
    held_1.update(zip(ends, held))
    kv_chunks.append([held_1[d] for d in reversed(lags)] + [kv[1]])
    (mixed, total), h_swap = join(
        attend(queries[1], kv_chunks[1], bias[1]),
        [plane.swap(x) for x in [h] + list(h_others)],
    )
    attn.append(mixed)
    lse.append(total)
    h_all = [[*h_swap, h, *h_others], None]
    (x, h), c_swap = join(middle(attn[1], x_in[1], gains, w_out_t), plane.swap(c_1))
    c_all.append([c_swap, c_1])
    x_mid.append(x)
    h_mid.append(h)

    def run(e, m, gate):
        out = expert_pass(
            h_all[m],
            c_all[m],
            order,
            gate,
            expert_w[e],
            n_dp,
            carried[m],
            totals[e],
            m + 1 == micro,
        )
        return out[:4], out[4:]

    def split(x):
        return x.reshape((plane.chips, -1) + x.shape[1:])

    totals, carried = [None] * local_experts, [None] * micro
    (carried[0], totals[0]), h_cross, h_swap = join(
        run(0, 0, gates[0][0]), plane.crosses(h_mid[1], every), plane.swap(h_mid[1])
    )
    h_all[1] = [h_swap] + [plane.swap(x) for x in h_cross] + [h_mid[1]] + h_cross
    (carried[1], totals[0]), w_whole, gate = join(
        run(0, 1, gates[0][1]), over_dp(w_last), gates[1][0]
    )
    expert_w.append(w_whole)

    def summed(x):
        return lax.psum_scatter(x, "dp", scatter_dimension=0, tiled=True)

    totals_s = [[summed(t) for t in totals[0]]]
    carried[0], totals[1] = run(1, 0, gate)
    y_sib_0, y_own_0, gh_sib_0, gh_own_0 = carried[0]
    gh_chips = sums(split(gh_own_0), split(plane.swap(gh_sib_0)), order)
    gate, gh_chips, y_sib_0 = join(gates[1][1], gh_chips, y_sib_0)
    (carried[1], totals[1]), gh_got, y_swap_0 = join(
        run(1, 1, gate), plane.exchange(gh_chips), plane.swap(y_sib_0)
    )
    y_sib_1, y_own_1, gh_sib_1, gh_own_1 = carried[1]

    def back_of(m, got):
        return middle_back(got, x_mid[m], grad_out[m], gains, w_out_t)

    def attention_back(m, grad_mixed):
        dq, *dkv = attend_back(queries[m], grad_mixed, kv_chunks[m], bias[m], lse[m])
        return dq, dkv

    def returned(dkv, ds):
        return [dp_along(dkv[n_dp - 1 - d], -d, n_dp) for d in ds]

    def weights_of(left, right, extra=None):
        return weight_grad(left, right, n_dp, plane.chips, core, extra)

    back_0, gh_swap, y_sib_1 = join(back_of(0, gh_got), plane.swap(gh_sib_1), y_sib_1)
    gh_chips = sums(split(gh_own_1), split(gh_swap), order)
    grad_mixed, gh_chips, y_swap_0 = join(back_0[3], gh_chips, y_swap_0)
    gh_got = plane.exchange(gh_chips)
    totals_s.append([summed(totals[1][0])])
    grad_q_0, dkv_0 = attention_back(0, grad_mixed)
    y_swap_0, grad_q_0 = join(y_swap_0, grad_q_0)
    grad_q_0, dkv_0, gh_got, y_chips_0, y_swap_1, totals_s[0], totals_s[1][0] = join(
        grad_q_0,
        dkv_0,
        gh_got,
        sums(split(y_own_0), split(y_swap_0), order),
        plane.swap(y_sib_1),
        totals_s[0],
        totals_s[1][0],
    )
    back_1 = back_of(1, gh_got)
    grad_x_mid, grad_branch, gain_parts, _ = zip(back_0, back_1)
    gain_mid = sum(g[0] for g in gain_parts)
    gain_high = gain_mid.astype(BF16)
    gain_mid = jnp.stack([gain_high, (gain_mid - gain_high.astype(F32)).astype(BF16)], axis=1)
    gain_mid = jnp.pad(gain_mid, ((0, 0), (2 * kv_width, 126)))
    soon, late = lags[:1], lags[-1:]
    grad_mixed, out_bands, held = join(
        back_1[3], weights_of(grad_branch, attn), returned(dkv_0, soon)
    )
    held_0 = dict(zip(soon, held))
    (grad_q_1, dkv_1), held, y_got_0, y_swap_1, gain_mid, out_swap = join(
        attention_back(1, grad_mixed),
        returned(dkv_0, between),
        plane.exchange(y_chips_0),
        y_swap_1,
        gain_mid,
        plane.swap(out_bands[1]),
    )
    held_0.update(zip(between, held))
    grad_q = [grad_q_0, grad_q_1]

    held, q_bands, y_chips_1, gain_mid, out_chips = join(
        returned(dkv_1, ends),
        weights_of(h_in, grad_q),
        sums(split(y_own_1), split(y_swap_1), order),
        gain_mid,
        sums(out_bands[0], out_swap, same),
    )
    held_1 = dict(zip(ends, held))
    out_got = plane.exchange(out_chips)
    held, held_late, q_chips, out_got, last_half = join(
        returned(dkv_1, between),
        returned(dkv_0, late),
        sums(q_bands[0], plane.swap(q_bands[1]), same),
        out_got,
        totals[1][1],
    )
    held_1.update(zip(between, held))
    held_0.update(zip(late, held_late))
    totals_s[1].append(summed(last_half))
    total_0 = added(dkv_0[-1].astype(F32), [held_0[d] for d in lags])
    total_1 = added(dkv_1[-1].astype(F32), [held_1[d] for d in lags])
    blank = jnp.zeros((rows, 128), F32)
    grad_kv = [
        jnp.concatenate([t[0], t[1], blank], axis=1).astype(BF16) for t in (total_0, total_1)
    ]
    kv_bands = weights_of(h_in, grad_kv, gain_mid)
    q_got = plane.exchange(q_chips)
    kv_swap, out_got = join(plane.swap(kv_bands[1]), out_got)
    kv_chips = sums(kv_bands[0], kv_swap, order)
    kv_own = [kv_chips[k] for k in range(plane.chips)]
    out_total, out_pieces = band_totals([[out_got]], dp_index)

    def over_dp_links(pieces):
        return [dp_cross(x, z, n_dp) for z, x in zip(lags, pieces)]

    kv_sent, q_got, grad_kv, totals_s, y_chips_1, out_sent = join(
        [plane.cross(kv_own[k], k) for k in every],
        q_got,
        grad_kv,
        totals_s,
        y_chips_1,
        over_dp_links(out_pieces),
    )
    grad_x = [
        input_back(grad_q[m], grad_kv[m], x_in[m], grad_x_mid[m], gains, weight) for m in micros
    ]
    y_got_1 = plane.exchange(y_chips_1)
    grad_gu_s, grad_down_s = unpack(totals_s, w_gate_up.shape, w_down.shape)
    total, pieces = band_totals([[q_got], [kv_own[0], *kv_sent]], dp_index)
    sent, y_got_1, grad_gu_s, grad_down_s, grad_x = join(
        over_dp_links(pieces), y_got_1, grad_gu_s, grad_down_s, grad_x
    )
    out_total, total = added(out_total, out_sent), added(total, sent)

    qkv_width = w_qkv.shape[1]
    grad_wqkv = total[:, :qkv_width]
    gain_in = jnp.sum(w_qkv.astype(F32) * grad_wqkv, axis=1) / norm_gains[0].astype(F32)
    x_out = [
        x_mid[m] + jnp.sum(y.astype(F32), axis=0) for m, y in enumerate((y_got_0, y_got_1))
    ]
    return (
        jnp.stack([x.astype(BF16) for x in x_out])[:, None],
        jnp.stack(grad_x)[:, None],
        jnp.stack([gain_in, total[:, qkv_width] + total[:, qkv_width + 1]]),
        grad_wqkv,
        out_total.T,
        grad_gu_s,
        grad_down_s,
    )


def solution(mesh):
    tokens_spec = P(None, "expert", "dp", None)
    experts_spec = P("expert", "dp", None)
    rows_spec = P(("dp", "expert"), None)
    columns_spec = P(None, ("dp", "expert"))
    return jax.shard_map(
        functools.partial(body, mesh.shape["dp"], mesh.shape["expert"]),
        mesh=mesh,
        in_specs=(
            tokens_spec,
            tokens_spec,
            P(None, "expert", None),
            P(None, "expert", None),
            tokens_spec,
            tokens_spec,
            columns_spec,
            rows_spec,
            columns_spec,
            experts_spec,
            experts_spec,
        ),
        out_specs=(
            tokens_spec,
            tokens_spec,
            columns_spec,
            rows_spec,
            columns_spec,
            experts_spec,
            experts_spec,
        ),
        check_vma=False,
    )
```
